128 devices in a mesh: seq: 32 (over x, y, core), exp: 4 (over z).
Axes of the slice: x: 4, y: 4, z: 4, core: 2. Of those that a mesh axis runs over, the one named last changes fastest.
Arguments:
- ssd_input: bfloat16 [16384, 8192], P('seq', 'exp'), may hold values from -26 to 26
- dt_raw: float32 [16384, 128], P('seq', 'exp'), may hold values from -4 to 4
- dt_bias: float32 [128], P('exp'), may hold values from -1 to 1
- log_decay: float32 [16384, 128], P('seq', 'exp'), may hold values from -2 to 0, as said below
- input_map: bfloat16 [16384, 8, 128], P('seq', 'exp'), may hold values from -5 to 5
- output_map: bfloat16 [16384, 8, 128], P('seq', 'exp'), may hold values from -0.5 to 0.5
- head_group: int32 [128], P('exp'), may hold values from 0 to 7
- d_skip: float32 [128], P('exp'), may hold values from 0.5 to 2
- norm_gain: float32 [8192], P('exp'), may hold values from 0.5 to 1.5
- w_out: bfloat16 [8192, 2048], P('exp'), may hold values from -0.0625 to 0.0625
- residual: bfloat16 [16384, 2048], P(('seq', 'exp')), may hold values from -26 to 26
- moe_gain: float32 [2048], replicated, may hold values from 0.5 to 1.5
- w_router: bfloat16 [2048, 64], replicated, may hold values from -0.125 to 0.125
- expert_ids: int32 [16384, 4], P(('seq', 'exp')), may hold values from 0 to 63, as said below
- w_gate: bfloat16 [128, 2048, 1024], P(('seq', 'exp')), may hold values from -0.125 to 0.125
- w_up: bfloat16 [128, 2048, 1024], P(('seq', 'exp')), may hold values from -0.125 to 0.125
- w_down: bfloat16 [128, 1024, 2048], P(('seq', 'exp')), may hold values from -0.125 to 0.125
Outputs:
- mixed: bfloat16 [16384, 2048], P(('seq', 'exp'))
The draws below stay inside these ranges and needn't reach their ends.
Inputs may be any that keep to these rules, and one draw needn't show every extreme that they name: `log_decay`: every entry is negative. `expert_ids`: each row names 4 different experts. In each aligned block of 128 rows (the rows of one device) no expert is named by more than 14 rows, and one expert, the same in every block, is named by exactly 14 rows of every block.
All inputs are finite; a program needn't handle non-finite values.
Results may differ from the reference program's by a relative error of at most 0.009.
Values may be sent and summed in bfloat16 or wider, within the bound.
No kernel may reach another device: no remote copies, remote signals or barrier semaphores. Data moves between devices by JAX's collectives and lax.ppermute only.
A program may use at most 192 MiB of HBM per device.

```python
import math
import jax
import jax.numpy as jnp
from jax import lax

D = 2048
SCAN_HEADS = 128
P_SIZE = 64
NST = 128
G = 8
FF = 2048
TOPK = 4
BLOCK = 256
TOK_DEV = 512
SEQUENCE_LENGTH = 16384
ROWS = 128
PER_GROUP = 16
EXPERTS = 64
MEAN = 8
CAP = 14
N_EXP = 4


def draw_ssd_input(key, part):
    key = jax.random.fold_in(key, 7)
    first, second, third = jax.random.split(key, 3)
    columns = SCAN_HEADS * P_SIZE
    row_scale = jnp.exp(jax.random.uniform(second, (SEQUENCE_LENGTH, 1), jnp.float32, -0.69, 0.69))
    column_scale = jnp.exp(jax.random.uniform(first, (1, columns), jnp.float32, -1.15, 1.15))
    noise = jax.random.truncated_normal(third, -4.0, 4.0, (SEQUENCE_LENGTH, columns), jnp.float32)
    return (noise * column_scale * row_scale).astype(jnp.bfloat16)


def draw_residual(key, part):
    key = jax.random.fold_in(key, 9)
    first, second, third = jax.random.split(key, 3)
    row_scale = jnp.exp(jax.random.uniform(second, (SEQUENCE_LENGTH, 1), jnp.float32, -0.69, 0.69))
    column_scale = jnp.exp(jax.random.uniform(first, (1, D), jnp.float32, -1.15, 1.15))
    noise = jax.random.truncated_normal(third, -4.0, 4.0, (SEQUENCE_LENGTH, D), jnp.float32)
    return (noise * column_scale * row_scale).astype(jnp.bfloat16)


def draw_log_decay(key, part):
    key = jax.random.fold_in(key, 5)
    first, second, third, fourth, fifth_entry, sixth_entry, seventh = jax.random.split(key, 7)
    slow_share = 0.5
    jaggedness = jax.random.uniform(seventh, (SEQUENCE_LENGTH, SCAN_HEADS), jnp.float32, 0.5, 1.5)
    slow_heads = jax.random.bernoulli(first, slow_share, (SCAN_HEADS,))
    slow_rates = jnp.exp(jax.random.uniform(second, (SCAN_HEADS,), jnp.float32, math.log(0.05), math.log(0.25))) / SEQUENCE_LENGTH
    fast_rates = jnp.exp(jax.random.uniform(third, (SCAN_HEADS,), jnp.float32, math.log(5.0), math.log(8.0))) / BLOCK
    decay_rates = jnp.where(slow_heads, slow_rates, fast_rates)
    segments = SEQUENCE_LENGTH // TOK_DEV
    segment_factor = jnp.exp(jax.random.uniform(fourth, (segments, 1, SCAN_HEADS), jnp.float32, -0.69, 0.69))
    segment_factor = jnp.broadcast_to(segment_factor, (segments, TOK_DEV, SCAN_HEADS)).reshape(SEQUENCE_LENGTH, SCAN_HEADS)
    spike_position = jax.random.randint(fifth_entry, (3,), 0, SEQUENCE_LENGTH)
    token_positions = jnp.arange(SEQUENCE_LENGTH)
    hit_flags = jnp.any(token_positions[:, None] == spike_position[None, :], axis=1)
    spike_penalty = jax.random.uniform(sixth_entry, (SEQUENCE_LENGTH, SCAN_HEADS), jnp.float32, 0.2, 0.35)
    return -decay_rates[None, :] * jaggedness * segment_factor + jnp.where(hit_flags[:, None], jnp.log1p(-spike_penalty), 0.0)


def draw_expert_ids(key, part):
    key = jax.random.fold_in(key, 11)
    first, second = jax.random.split(key, 2)
    block_count = SEQUENCE_LENGTH // ROWS
    pair_count = ROWS * TOPK
    hot_expert = jax.random.randint(first, (), 0, EXPERTS)

    def one_block(block_key):
        key_one, key_two, key_three, key_four = jax.random.split(block_key, 4)
        others = jax.random.permutation(key_one, EXPERTS - 1)
        others = others + (others >= hot_expert).astype(jnp.int32)
        partner = others[0]
        remaining = others[1:]
        firsts = remaining[0::2]
        seconds = remaining[1::2]
        amounts = jax.random.randint(key_two, ((EXPERTS - 2) // 2,), 0, CAP - MEAN + 1)
        counts = jnp.zeros((EXPERTS,), jnp.int32)
        counts = counts.at[hot_expert].set(CAP).at[partner].set(2 * MEAN - CAP)
        counts = counts.at[firsts].set(MEAN + amounts).at[seconds].set(MEAN - amounts)
        order = jax.random.permutation(key_three, EXPERTS)
        ends = jnp.cumsum(counts[order])
        pairs = jnp.arange(pair_count)
        which = jnp.sum((ends[None, :] <= pairs[:, None]).astype(jnp.int32), axis=1)
        listed = order[which]
        grid_rows = listed.reshape(TOPK, ROWS).T
        shuffle = jax.random.permutation(key_four, ROWS)
        return grid_rows[shuffle]
    drawn = jax.lax.map(one_block, jax.random.split(second, block_count))
    return drawn.reshape(SEQUENCE_LENGTH, TOPK).astype(jnp.int32)


def set_ends(values, key, least, top_value):
    longest = values.shape.index(max(values.shape))
    spots = []
    for shift in (0, 1):
        where = [jax.random.randint(jax.random.fold_in(key, axis), (), 0, length) for axis, length in enumerate(values.shape)]
        where[longest] = (where[longest] + shift) % values.shape[longest]
        spots.append(tuple(where))
    return values.at[spots[0]].set(least).at[spots[1]].set(top_value)


def steps_of(own_key, dims, cuts, smallest, high):
    def one(axis_at, parts):
        steps = jax.random.uniform(jax.random.fold_in(jax.random.fold_in(own_key, 6), axis_at), (parts,), jnp.float32, smallest / len(cuts), high / len(cuts))
        return jnp.repeat(jnp.exp(steps), dims[axis_at] // parts).reshape((-1,) + (1,) * (len(dims) - axis_at - 1))

    loudness = one(*cuts[0])
    for cut in cuts[1:]:
        loudness = loudness * one(*cut)
    return loudness


def gaussian(own_key, shape, scale, reach, pieces=(), held_as=jnp.bfloat16):
    values = jax.random.normal(own_key, shape, jnp.float32) * scale
    if len(pieces) > 0:
        values = steps_of(own_key, shape, pieces, -0.22, 0.18) * values
    return jnp.clip(values, min=-reach, max=reach).astype(held_as)


def setup_inputs(seed: int = 0) -> dict:
    splits = jax.random.split(jax.random.key(seed), 18)
    return {
        "ssd_input": draw_ssd_input(jax.random.fold_in(splits[17], 71), 0),
        "dt_raw": gaussian(splits[1], (SEQUENCE_LENGTH, SCAN_HEADS), 1.0, 4.0, ((0, 32), (1, 4)), jnp.float32),
        "dt_bias": jnp.clip(jax.random.uniform(splits[2], (SCAN_HEADS,), jnp.float32, -1.0, 1.0) * steps_of(splits[2], (SCAN_HEADS,), ((0, 4),), -0.4, 0.0), -1.0, 1.0),
        "log_decay": draw_log_decay(jax.random.fold_in(splits[17], 71), 0),
        "input_map": gaussian(splits[4], (SEQUENCE_LENGTH, G, NST), 1.0, 5.0, ((0, 32), (1, 4))),
        "output_map": gaussian(splits[5], (SEQUENCE_LENGTH, G, NST), NST ** -0.5, 0.5, ((0, 32), (1, 4))),
        "head_group": set_ends(jax.random.randint(splits[6], (SCAN_HEADS,), 0, G), jax.random.fold_in(splits[6], 1), 0, G - 1).astype(jnp.int32),
        "d_skip": jnp.clip(jnp.exp(math.log(2.0) - 1.3862944 * jax.random.uniform(splits[7], (SCAN_HEADS,), jnp.float32) ** steps_of(splits[7], (SCAN_HEADS,), ((0, 4),), -0.2, 0.2)), 0.5, 2.0),
        "norm_gain": jnp.clip(1.0 + 0.1 * jax.random.normal(splits[8], (SCAN_HEADS * P_SIZE,), jnp.float32), 0.5, 1.5),
        "w_out": gaussian(splits[9], (SCAN_HEADS * P_SIZE, D), (SCAN_HEADS * P_SIZE) ** -0.5, 0.0625, ((0, 4),)),
        "residual": draw_residual(jax.random.fold_in(splits[17], 71), 0),
        "moe_gain": jnp.clip(1.0 + 0.1 * jax.random.normal(splits[11], (D,), jnp.float32), 0.5, 1.5),
        "w_router": gaussian(splits[12], (D, EXPERTS), D ** -0.5, 0.125),
        "expert_ids": draw_expert_ids(jax.random.fold_in(splits[17], 71), 0),
        "w_gate": gaussian(splits[14], (2 * EXPERTS, D, FF // 2), D ** -0.5, 0.125, ((0, 128),)),
        "w_up": gaussian(splits[15], (2 * EXPERTS, D, FF // 2), D ** -0.5, 0.125, ((0, 128),)),
        "w_down": gaussian(splits[16], (2 * EXPERTS, FF // 2, D), FF ** -0.5, 0.125, ((0, 128),)),
    }


EPS = 1e-06

def reference(ssd_input, dt_raw, dt_bias, log_decay, input_map, output_map, head_group, d_skip, norm_gain, w_out, residual, moe_gain, w_router, expert_ids, w_gate, w_up, w_down):
    select = (head_group[:, None] == jnp.arange(G, dtype=jnp.int32)[None, :]).astype(jnp.float32)
    causal = jnp.tril(jnp.ones((BLOCK, BLOCK), dtype=bool))
    head_gains = norm_gain.reshape(SCAN_HEADS, P_SIZE)

    def one_block(carry_state, block_index):
        first_row = (block_index * BLOCK).astype(jnp.int32)
        values = lax.dynamic_slice_in_dim(ssd_input, first_row, BLOCK, 0).reshape(BLOCK, SCAN_HEADS, P_SIZE).astype(jnp.float32)
        input_rows = lax.dynamic_slice_in_dim(input_map, first_row, BLOCK, 0).astype(jnp.float32)
        output_rows = lax.dynamic_slice_in_dim(output_map, first_row, BLOCK, 0).astype(jnp.float32)
        input_heads = jnp.einsum('tgn,hg->thn', input_rows, select)
        output_heads = jnp.einsum('tgn,hg->thn', output_rows, select)
        step_size = jax.nn.softplus(lax.dynamic_slice_in_dim(dt_raw, first_row, BLOCK, 0) + dt_bias[None, :])
        running = jnp.cumsum(lax.dynamic_slice_in_dim(log_decay, first_row, BLOCK, 0), axis=0)
        running_heads = running.T
        spread = jnp.where(causal[None], running_heads[:, :, None] - running_heads[:, None, :], 0.0)
        scores = jnp.einsum('thn,shn->hts', output_heads, input_heads)
        mixing = jnp.where(causal[None], scores * jnp.exp(spread) * step_size.T[:, None, :], 0.0)
        mixing = lax.optimization_barrier(mixing.astype(jnp.bfloat16)).astype(jnp.float32)
        within = jnp.einsum('hts,shp->thp', mixing, values)
        carried = jnp.einsum('thn,hpn->thp', output_heads, carry_state, precision=lax.Precision.HIGHEST) * jnp.exp(running)[:, :, None]
        ssd_out = within + carried + d_skip[None, :, None] * values
        scaled = (jnp.exp(running[-1:] - running) * step_size)[:, :, None] * values
        scaled = lax.optimization_barrier(scaled.astype(jnp.bfloat16)).astype(jnp.float32)
        fresh_state = jnp.einsum('thp,thn->hpn', scaled, input_heads)
        next_state = jnp.exp(running[-1])[:, None, None] * carry_state + fresh_state
        square = lax.optimization_barrier(jnp.mean(ssd_out * ssd_out, axis=-1, keepdims=True))
        normed = (ssd_out * lax.rsqrt(square + EPS) * head_gains[None]).astype(jnp.bfloat16)
        return (next_state, normed.reshape(BLOCK, SCAN_HEADS * P_SIZE))
    start_state = jnp.zeros((SCAN_HEADS, P_SIZE, NST), jnp.float32)
    _, normed = lax.scan(one_block, start_state, jnp.arange(SEQUENCE_LENGTH // BLOCK, dtype=jnp.int32))
    normed = normed.reshape(SEQUENCE_LENGTH, SCAN_HEADS * P_SIZE)
    projected = jnp.dot(normed, w_out, preferred_element_type=jnp.float32)
    stream = residual.astype(jnp.float32) + projected
    square = lax.optimization_barrier(jnp.mean(stream * stream, axis=-1, keepdims=True))
    tokens = (stream * lax.rsqrt(square + EPS) * moe_gain[None, :]).astype(jnp.bfloat16)
    logits = jnp.dot(tokens, w_router, preferred_element_type=jnp.float32)
    route_weight = jax.nn.sigmoid(jnp.take_along_axis(logits, expert_ids, axis=1))
    block_count = SEQUENCE_LENGTH // ROWS
    grouped_ids = expert_ids.reshape(block_count, ROWS * TOPK)
    onehot = (grouped_ids[:, :, None] == jnp.arange(EXPERTS, dtype=jnp.int32)[None, None, :]).astype(jnp.int32)
    slot_index = lax.optimization_barrier(jnp.sum((jnp.cumsum(onehot, axis=1) - onehot) * onehot, axis=2)).astype(jnp.int32)
    block_ids = jnp.broadcast_to(jnp.arange(block_count, dtype=jnp.int32)[:, None], grouped_ids.shape)
    pair_rows = jnp.broadcast_to(jnp.arange(ROWS * TOPK, dtype=jnp.int32)[None, :] // TOPK, grouped_ids.shape)
    source_row = block_ids * ROWS + pair_rows
    row_table = jnp.full((EXPERTS, block_count, CAP), SEQUENCE_LENGTH, jnp.int32).at[grouped_ids, block_ids, slot_index].set(source_row)
    weight_table = jnp.zeros((EXPERTS, block_count, CAP), jnp.float32).at[grouped_ids, block_ids, slot_index].set(route_weight.reshape(block_count, ROWS * TOPK))
    padded = jnp.concatenate([tokens, jnp.zeros((1, D), jnp.bfloat16)], axis=0)
    half_width = FF // 2

    def one_expert(total, expert):
        group_index = expert // PER_GROUP
        member = expert % PER_GROUP
        low_index = (2 * member * N_EXP + group_index).astype(jnp.int32)
        high_index = (low_index + N_EXP).astype(jnp.int32)
        gate_full = jnp.concatenate([w_gate[low_index], w_gate[high_index]], axis=1)
        up_full = jnp.concatenate([w_up[low_index], w_up[high_index]], axis=1)
        rows_here = row_table[expert].reshape(-1)
        chosen = padded[rows_here]
        gate_part = jnp.dot(chosen, gate_full, preferred_element_type=jnp.float32)
        up_part = jnp.dot(chosen, up_full, preferred_element_type=jnp.float32)
        hidden = (jax.nn.silu(gate_part) * up_part).astype(jnp.bfloat16)
        low_part = jnp.dot(hidden[:, :half_width], w_down[low_index], preferred_element_type=jnp.float32).astype(jnp.bfloat16)
        high_part = jnp.dot(hidden[:, half_width:], w_down[high_index], preferred_element_type=jnp.float32).astype(jnp.bfloat16)
        expert_out = low_part.astype(jnp.float32) + high_part.astype(jnp.float32)
        total = total.at[rows_here].add(weight_table[expert].reshape(-1)[:, None] * expert_out, mode='drop')
        return (total, None)
    expert_sum, _ = lax.scan(one_expert, jnp.zeros((SEQUENCE_LENGTH, D), jnp.float32), jnp.arange(EXPERTS, dtype=jnp.int32))
    return (stream + expert_sum).astype(jnp.bfloat16)
```

```python
import functools

import jax
import jax.numpy as jnp
from jax import lax
from jax.experimental import pallas as pl
from jax.experimental.pallas import tpu as pltpu
from jax.sharding import PartitionSpec as P

P_SIZE = 64
NST = 128
G = 8
BLOCK = 256
PAIR = 2 * P_SIZE
STEP_PAIRS = 4
SLOTS = 16

EPS = 1e-06
F32 = jnp.float32
BF16 = jnp.bfloat16
MIB = 1024 * 1024


def dot(a, b):
    return jnp.dot(a, b, preferred_element_type=F32)


def lanes_of_first(shape):
    return lax.broadcasted_iota(jnp.int32, shape, 1) < P_SIZE


def columns_of(first_row, second_row):
    length = first_row.shape[1]
    rows = jnp.concatenate(
        [
            jnp.broadcast_to(first_row, (P_SIZE, length)),
            jnp.broadcast_to(second_row, (P_SIZE, length)),
        ],
        axis=0,
    )
    return rows.T


def lane_pair(first, second):
    return jnp.concatenate(
        [jnp.broadcast_to(first, (1, P_SIZE)), jnp.broadcast_to(second, (1, P_SIZE))], axis=1
    )


def split_pair(values):
    first = lanes_of_first(values.shape)
    zero = jnp.zeros_like(values)
    return jnp.concatenate([jnp.where(first, values, zero), jnp.where(first, zero, values)], axis=0)


def states_kernel(slot_ref, x_ref, prep_ref, m0, m1, m2a, m2b, m3, fresh_ref, send_ref, maps):
    step = pl.program_id(0)

    @pl.when(step == 0)
    def _():
        maps[0:2] = m0[...]
        maps[2:4] = m1[...]
        maps[4] = m2a[...]
        maps[5] = m2b[...]
        maps[6:8] = m3[...]

    for p in range(STEP_PAIRS):
        slots = [slot_ref[step * 2 * STEP_PAIRS + 2 * p + i] for i in range(2)]
        x = x_ref[:, p * PAIR : (p + 1) * PAIR].astype(F32)
        weight = columns_of(prep_ref[2 * p, 2:3, :], prep_ref[2 * p + 1, 2:3, :])
        scaled = (x * weight).astype(BF16)
        fresh = []
        for b in range(2):
            rows = slice(b * BLOCK, (b + 1) * BLOCK)
            both = split_pair(scaled[rows])
            left = jnp.concatenate([maps[slots[0], :, rows], maps[slots[1], :, rows]], axis=1)
            fresh.append(dot(left, both))
        ends = [
            lane_pair(
                prep_ref[2 * p, 3:4, e - 1 : e],
                prep_ref[2 * p + 1, 3:4, e - 1 : e],
            )
            for e in (BLOCK, 2 * BLOCK)
        ]
        fresh_ref[p] = fresh[0]
        final = (ends[1] * fresh[0] + fresh[1]).astype(BF16)
        decay = ends[0] * ends[1]
        high = decay.astype(BF16).astype(F32)
        row = lax.broadcasted_iota(jnp.int32, (8, PAIR), 0)
        tail = jnp.where(row == 0, high, jnp.where(row == 1, decay - high, 0.0)).astype(BF16)
        for i in range(2):
            send_ref[2 * p + i, 0:64] = final[64 * i : 64 * (i + 1)]
            send_ref[2 * p + i, 64:72] = tail


def scan_kernel(in_ref, out_ref):
    state = jnp.zeros((64, PAIR), F32)
    for j in range(in_ref.shape[0]):
        out_ref[j] = state.astype(BF16)
        tail = in_ref[j, 64:72].astype(F32)
        decay = tail[0:1] + tail[1:2]
        state = decay * state + in_ref[j, 0:64].astype(F32)


def within_kernel(
    slot_ref, x_ref, prep_ref, skip_ref, i0, i1, i2a, i2b, i3, o0, o1, o2a, o2b, o3, out_ref, scores
):
    step = pl.program_id(0)

    @pl.when(step == 0)
    def _():
        inputs = [i0.at[0], i0.at[1], i1.at[0], i1.at[1], i2a, i2b, i3.at[0], i3.at[1]]
        outputs = [o0.at[0], o0.at[1], o1.at[0], o1.at[1], o2a, o2b, o3.at[0], o3.at[1]]
        for g in range(G):
            for b in range(2):
                rows = slice(b * BLOCK, (b + 1) * BLOCK)
                scores[g, b] = dot(outputs[g][rows, :], inputs[g][:, rows])

    half = BLOCK // 2
    causal = lax.broadcasted_iota(jnp.int32, (half, half), 0) >= lax.broadcasted_iota(
        jnp.int32, (half, half), 1
    )
    for p in range(STEP_PAIRS):
        columns = slice(p * PAIR, (p + 1) * PAIR)
        slots = [slot_ref[step * 2 * STEP_PAIRS + 2 * p + i] for i in range(2)]
        for b in range(2):
            rows = slice(b * BLOCK, (b + 1) * BLOCK)
            x = x_ref[rows, columns]
            early, late = [], []
            for i in range(2):
                running = prep_ref[2 * p + i, 0:1, rows]
                size = prep_ref[2 * p + i, 1:2, rows]
                down = jnp.broadcast_to(running, (half, BLOCK)).T

                def tile(t, s, masked):
                    ts, ss = slice(t * half, (t + 1) * half), slice(s * half, (s + 1) * half)
                    spread = down[ts] - running[:, ss]
                    score = scores[slots[i], b, ts, ss]
                    value = score * jnp.exp(spread) * size[:, ss]
                    return (jnp.where(causal, value, 0.0) if masked else value).astype(BF16)

                early.append(tile(0, 0, True))
                late.append(tile(1, 0, False))
                late.append(tile(1, 1, True))
            both = split_pair(x)
            first = jnp.concatenate([both[0:half], both[BLOCK : BLOCK + half]], axis=0)
            skipped = skip_ref[:, columns] * x.astype(F32)
            top = dot(jnp.concatenate(early, axis=1), first)
            bottom = dot(jnp.concatenate(late, axis=1), both)
            out_ref[b * BLOCK : b * BLOCK + half, columns] = top + skipped[0:half]
            out_ref[b * BLOCK + half : (b + 1) * BLOCK, columns] = bottom + skipped[half:]


def project_kernel(
    slot_ref,
    place_ref,
    within_ref,
    prep_ref,
    gain_ref,
    enter_ref,
    fresh_ref,
    o0,
    o1,
    o2a,
    o2b,
    o3,
    w_ref,
    own_ref,
    up_ref,
    far_ref,
    down_ref,
    maps,
    normed,
    total,
):
    step = pl.program_id(0)

    @pl.when(step == 0)
    def _():
        maps[0:2] = o0[...]
        maps[2:4] = o1[...]
        maps[4] = o2a[...]
        maps[5] = o2b[...]
        maps[6:8] = o3[...]
        total[...] = jnp.zeros_like(total)

    same = (
        lax.broadcasted_iota(jnp.int32, (2 * PAIR, PAIR), 0) % PAIR // P_SIZE
        == lax.broadcasted_iota(jnp.int32, (2 * PAIR, PAIR), 1) // P_SIZE
    )
    summing = jnp.where(same, 1.0, 0.0).astype(BF16)
    for p in range(STEP_PAIRS):
        columns = slice(p * PAIR, (p + 1) * PAIR)
        slots = [slot_ref[step * 2 * STEP_PAIRS + 2 * p + i] for i in range(2)]
        growth = columns_of(prep_ref[2 * p, 3:4, :], prep_ref[2 * p + 1, 3:4, :])
        first_end = lane_pair(
            prep_ref[2 * p, 3:4, BLOCK - 1 : BLOCK], prep_ref[2 * p + 1, 3:4, BLOCK - 1 : BLOCK]
        )
        arriving = enter_ref[p].astype(F32)
        entering = [arriving, first_end * arriving + fresh_ref[p]]
        for b in range(2):
            rows = slice(b * BLOCK, (b + 1) * BLOCK)
            left = jnp.concatenate([maps[slots[0], rows, :], maps[slots[1], rows, :]], axis=1)
            carried = dot(left, split_pair(entering[b].astype(BF16)))
            y = within_ref[rows, columns] + carried * growth[rows]
            square = y * y
            high = square.astype(BF16)
            low = (square - high.astype(F32)).astype(BF16)
            mean = dot(jnp.concatenate([high, low], axis=1), summing) * (1.0 / P_SIZE)
            normed[rows, columns] = (y * lax.rsqrt(mean + EPS) * gain_ref[:, columns]).astype(BF16)
    total[...] += dot(normed[...], w_ref[...])

    @pl.when(step == pl.num_programs(0) - 1)
    def _():
        share = own_ref.shape[0]

        def rows_for(offset):
            place = lax.rem(place_ref[0] + offset, 4)
            return total[pl.ds(pl.multiple_of(place * share, share), share), :]

        own_ref[...] = rows_for(0)
        up_ref[...] = rows_for(1)
        far_ref[...] = rows_for(2).astype(BF16)
        down_ref[...] = rows_for(3)


def whole(shape):
    return pl.BlockSpec(shape, lambda s, *_: (0,) * len(shape))


def params(mib=56):
    return pltpu.CompilerParams(
        dimension_semantics=("arbitrary",), vmem_limit_bytes=mib * MIB
    )


def ring_gather(own, nxt, prv):
    from_prev = lax.ppermute(own, "exp", nxt)
    from_next = lax.ppermute(own, "exp", prv)
    far_a = lax.ppermute(from_prev[0], "exp", nxt)
    far_b = lax.ppermute(from_next[1], "exp", prv)
    return own, from_next, far_a, far_b, from_prev


def body(
    ssd_input,
    dt_raw,
    dt_bias,
    log_decay,
    input_map,
    output_map,
    head_group,
    d_skip,
    norm_gain,
    w_out,
    residual,
    moe_gain,
    w_router,
    expert_ids,
    w_gate,
    w_up,
    w_down,
):
    length = ssd_input.shape[0]
    heads = dt_raw.shape[1]
    blocks = length // BLOCK
    width = w_out.shape[1]
    share = residual.shape[0]
    me = lax.axis_index("exp")
    ring = lax.axis_size("exp")
    seq_count = lax.axis_size("seq")
    nxt = [(i, (i + 1) % ring) for i in range(ring)]
    prv = [(i, (i - 1) % ring) for i in range(ring)]
    partner = [(i, i ^ 1) for i in range(seq_count)]
    steps = heads // (2 * STEP_PAIRS)
    columns = STEP_PAIRS * PAIR

    in_maps = ring_gather(input_map.transpose(1, 2, 0), nxt, prv)
    out_maps = ring_gather(output_map.transpose(1, 0, 2), nxt, prv)
    slot = (lax.rem(head_group // 2 - me + ring, ring) * 2 + head_group % 2).astype(jnp.int32)

    other_gate = lax.ppermute(w_gate[0], "seq", partner)
    other_up = lax.ppermute(w_up[0], "seq", partner)
    other_down = lax.ppermute(w_down[0], "seq", partner)

    step_size = jax.nn.softplus(dt_raw + dt_bias[None, :])
    running = jnp.cumsum(log_decay.reshape(blocks, BLOCK, heads), axis=1)
    to_end = jnp.exp(running[:, -1:, :] - running).reshape(length, heads) * step_size
    running = running.reshape(length, heads)
    prep = jnp.stack([running, step_size, to_end, jnp.exp(running)], axis=0).transpose(2, 0, 1)
    skip_lanes = jnp.repeat(d_skip, P_SIZE)[None, :]
    gain_lanes = norm_gain[None, :]

    x_spec = pl.BlockSpec((length, columns), lambda s, *_: (0, s))
    prep_spec = pl.BlockSpec((2 * STEP_PAIRS, 4, length), lambda s, *_: (s, 0, 0))
    lane_spec = pl.BlockSpec((1, columns), lambda s, *_: (0, s))
    state_spec = pl.BlockSpec((STEP_PAIRS, NST, PAIR), lambda s, *_: (s, 0, 0))
    in_specs = [whole((2, NST, length))] * 2 + [whole((NST, length))] * 2 + [whole((2, NST, length))]
    out_specs = [whole((2, length, NST))] * 2 + [whole((length, NST))] * 2 + [whole((2, length, NST))]

    fresh, sending = pl.pallas_call(
        states_kernel,
        grid_spec=pltpu.PrefetchScalarGridSpec(
            num_scalar_prefetch=1,
            grid=(steps,),
            in_specs=[x_spec, prep_spec] + in_specs,
            out_specs=[state_spec, pl.BlockSpec((2 * STEP_PAIRS, 72, PAIR), lambda s, *_: (s, 0, 0))],
            scratch_shapes=[pltpu.VMEM((G, NST, length), BF16)],
        ),
        out_shape=[
            jax.ShapeDtypeStruct((heads // 2, NST, PAIR), F32),
            jax.ShapeDtypeStruct((heads, 72, PAIR), BF16),
        ],
        compiler_params=params(),
        cost_estimate=pl.CostEstimate(
            flops=600_000_000, bytes_accessed=5_000_000, transcendentals=0
        ),
        name="states",
    )(slot, ssd_input, prep, *in_maps)

    arrived = lax.all_to_all(sending, "seq", split_axis=0, concat_axis=0, tiled=True)
    prefix = pl.pallas_call(
        scan_kernel,
        out_shape=jax.ShapeDtypeStruct((seq_count, 64, PAIR), BF16),
        compiler_params=pltpu.CompilerParams(vmem_limit_bytes=16 * MIB),
        name="scan",
    )(arrived)
    entering = lax.all_to_all(prefix, "seq", split_axis=0, concat_axis=0, tiled=True)
    entering = entering.reshape(heads // 2, NST, PAIR)

    within = pl.pallas_call(
        within_kernel,
        grid_spec=pltpu.PrefetchScalarGridSpec(
            num_scalar_prefetch=1,
            grid=(steps,),
            in_specs=[x_spec, prep_spec, lane_spec] + in_specs + out_specs,
            out_specs=x_spec,
            scratch_shapes=[pltpu.VMEM((G, 2, BLOCK, BLOCK), F32)],
        ),
        out_shape=jax.ShapeDtypeStruct(ssd_input.shape, F32),
        compiler_params=params(),
        cost_estimate=pl.CostEstimate(
            flops=12_000_000_000, bytes_accessed=8_000_000, transcendentals=4_000_000
        ),
        name="within",
    )(slot, ssd_input, prep, skip_lanes, *in_maps, *out_maps)

    share_spec = whole((share, width))
    own, up, far, down = pl.pallas_call(
        project_kernel,
        grid_spec=pltpu.PrefetchScalarGridSpec(
            num_scalar_prefetch=2,
            grid=(steps,),
            in_specs=[x_spec, prep_spec, lane_spec, state_spec, state_spec]
            + out_specs
            + [pl.BlockSpec((columns, width), lambda s, *_: (s, 0))],
            out_specs=[share_spec] * 4,
            scratch_shapes=[
                pltpu.VMEM((G, length, NST), BF16),
                pltpu.VMEM((length, columns), BF16),
                pltpu.VMEM((length, width), F32),
            ],
        ),
        out_shape=[
            jax.ShapeDtypeStruct((share, width), F32),
            jax.ShapeDtypeStruct((share, width), F32),
            jax.ShapeDtypeStruct((share, width), BF16),
            jax.ShapeDtypeStruct((share, width), F32),
        ],
        compiler_params=params(),
        cost_estimate=pl.CostEstimate(
            flops=6_000_000_000, bytes_accessed=18_000_000, transcendentals=0
        ),
        name="project",
    )(slot, me[None].astype(jnp.int32), within, prep, gain_lanes, entering, fresh, *out_maps, w_out)

    middle = width // 2
    far_left = lax.ppermute(far[:, :middle], "exp", nxt)
    far_right = lax.ppermute(far[:, middle:], "exp", prv)
    up = jnp.concatenate([up[:, :middle] + far_left.astype(F32), up[:, middle:]], axis=1).astype(BF16)
    down = jnp.concatenate(
        [down[:, :middle], down[:, middle:] + far_right.astype(F32)], axis=1
    ).astype(BF16)
    from_prev = lax.ppermute(up, "exp", nxt)
    from_next = lax.ppermute(down, "exp", prv)
    stream = (
        residual.astype(F32) + own + from_prev.astype(F32) + from_next.astype(F32)
    )

    square_rows = jnp.mean(stream * stream, axis=-1, keepdims=True)
    tokens = (stream * lax.rsqrt(square_rows + EPS) * moe_gain[None, :]).astype(BF16)

    experts = w_router.shape[1]
    per_group = experts // ring
    chips = experts
    hosted = jnp.arange(chips) % ring * per_group + jnp.arange(chips) // ring
    router = w_router.reshape(-1, ring, per_group).swapaxes(1, 2).reshape(-1, experts)
    logits = lax.dot_general(
        router, tokens, (((0,), (1,)), ((), ())), preferred_element_type=F32
    )
    weight = jax.nn.sigmoid(logits)
    routed = jnp.any(expert_ids.T[None, :, :] == hosted[:, None, None], axis=1)
    earlier = jnp.triu(jnp.ones((share, share), BF16), 1)
    rank = dot(routed.astype(BF16), earlier)
    slots = jnp.arange(SLOTS, dtype=jnp.int32).astype(F32)
    placed = routed[:, None, :] & (rank[:, None, :] == slots[None, :, None])
    dispatch = placed.astype(BF16).reshape(chips * SLOTS, share)
    outgoing = dot(dispatch, tokens).astype(BF16).reshape(chips, SLOTS, width)

    cores = [
        [(c // ring * 2 + h) * ring + c % ring for c in range(chips)] for h in range(2)
    ]
    swap = functools.partial(
        lax.all_to_all,
        axis_name=("seq", "exp"),
        split_axis=0,
        concat_axis=0,
        tiled=True,
        axis_index_groups=cores,
    )
    rows = swap(outgoing).reshape(chips * SLOTS, width)

    def half_expert(gate, up_weight, down_weight):
        hidden = (jax.nn.silu(dot(rows, gate)) * dot(rows, up_weight)).astype(BF16)
        return dot(hidden, down_weight)

    result = half_expert(w_gate[0], w_up[0], w_down[0]) + half_expert(
        other_gate, other_up, other_down
    )
    returned = swap(result.astype(BF16).reshape(chips, SLOTS, width))
    combine = jnp.where(placed, weight[:, None, :], 0.0).reshape(chips * SLOTS, share).T
    high = combine.astype(BF16)
    low = (combine - high.astype(F32)).astype(BF16)
    both = dot(
        jnp.concatenate([high, low], axis=0), returned.reshape(chips * SLOTS, width)
    )
    return (stream + both[:share] + both[share:]).astype(BF16)


def solution(mesh):
    return jax.shard_map(
        body,
        mesh=mesh,
        in_specs=(
            P("seq", "exp"),
            P("seq", "exp"),
            P("exp"),
            P("seq", "exp"),
            P("seq", "exp", None),
            P("seq", "exp", None),
            P("exp"),
            P("exp"),
            P("exp"),
            P("exp", None),
            P(("seq", "exp"), None),
            P(),
            P(),
            P(("seq", "exp"), None),
            P(("seq", "exp"), None, None),
            P(("seq", "exp"), None, None),
            P(("seq", "exp"), None, None),
        ),
        out_specs=P(("seq", "exp"), None),
        check_vma=False,
    )
```

```python
import functools

import jax
import jax.numpy as jnp
from jax import lax
from jax.experimental import pallas as pl
from jax.experimental.pallas import tpu as pltpu
from jax.sharding import PartitionSpec as P

P_SIZE = 64
NST = 128
G = 8
BLOCK = 256
PAIR = 2 * P_SIZE
STEP_PAIRS = 4
SLOTS = 14
CHUNKS = 2
ROW = 8
CELL = 256

EPS = 1e-06
F32 = jnp.float32
BF16 = jnp.bfloat16
MIB = 1024 * 1024


def dot(a, b):
    return jnp.dot(a, b, preferred_element_type=F32)


def lanes_of_first(shape):
    return lax.broadcasted_iota(jnp.int32, shape, 1) < P_SIZE


def columns_of(first_row, second_row):
    length = first_row.shape[1]
    rows = jnp.concatenate(
        [
            jnp.broadcast_to(first_row, (P_SIZE, length)),
            jnp.broadcast_to(second_row, (P_SIZE, length)),
        ],
        axis=0,
    )
    return rows.T


def lane_pair(first, second):
    return jnp.concatenate(
        [jnp.broadcast_to(first, (1, P_SIZE)), jnp.broadcast_to(second, (1, P_SIZE))], axis=1
    )


def split_pair(values):
    first = lanes_of_first(values.shape)
    zero = jnp.zeros_like(values)
    return jnp.concatenate([jnp.where(first, values, zero), jnp.where(first, zero, values)], axis=0)


def states_kernel(slot_ref, x_ref, prep_ref, m0, m1, m2a, m2b, m3, fresh_ref, send_ref, maps):
    step = pl.program_id(0)

    @pl.when(step == 0)
    def _():
        maps[0:2] = m0[...]
        maps[2:4] = m1[...]
        maps[4] = m2a[...]
        maps[5] = m2b[...]
        maps[6:8] = m3[...]

    for p in range(STEP_PAIRS):
        slots = [slot_ref[step * 2 * STEP_PAIRS + 2 * p + i] for i in range(2)]
        x = x_ref[:, p * PAIR : (p + 1) * PAIR].astype(F32)
        weight = columns_of(prep_ref[2 * p, 2:3, :], prep_ref[2 * p + 1, 2:3, :])
        scaled = (x * weight).astype(BF16)
        fresh = []
        for b in range(2):
            rows = slice(b * BLOCK, (b + 1) * BLOCK)
            both = split_pair(scaled[rows])
            left = jnp.concatenate([maps[slots[0], :, rows], maps[slots[1], :, rows]], axis=1)
            fresh.append(dot(left, both))
        ends = [
            lane_pair(
                prep_ref[2 * p, 3:4, e - 1 : e],
                prep_ref[2 * p + 1, 3:4, e - 1 : e],
            )
            for e in (BLOCK, 2 * BLOCK)
        ]
        fresh_ref[p] = fresh[0]
        final = (ends[1] * fresh[0] + fresh[1]).astype(BF16)
        decay = ends[0] * ends[1]
        high = decay.astype(BF16).astype(F32)
        row = lax.broadcasted_iota(jnp.int32, (8, PAIR), 0)
        tail = jnp.where(row == 0, high, jnp.where(row == 1, decay - high, 0.0)).astype(BF16)
        for i in range(2):
            send_ref[2 * p + i, 0:64] = final[64 * i : 64 * (i + 1)]
            send_ref[2 * p + i, 64:72] = tail


def scan_kernel(in_ref, out_ref):
    state = jnp.zeros((64, PAIR), F32)
    for j in range(in_ref.shape[0]):
        out_ref[j] = state.astype(BF16)
        tail = in_ref[j, 64:72].astype(F32)
        decay = tail[0:1] + tail[1:2]
        state = decay * state + in_ref[j, 0:64].astype(F32)


def within_kernel(
    slot_ref, x_ref, prep_ref, skip_ref, i0, i1, i2a, i2b, i3, o0, o1, o2a, o2b, o3, out_ref, scores
):
    step = pl.program_id(0)

    @pl.when(step == 0)
    def _():
        inputs = [i0.at[0], i0.at[1], i1.at[0], i1.at[1], i2a, i2b, i3.at[0], i3.at[1]]
        outputs = [o0.at[0], o0.at[1], o1.at[0], o1.at[1], o2a, o2b, o3.at[0], o3.at[1]]
        for g in range(G):
            for b in range(2):
                rows = slice(b * BLOCK, (b + 1) * BLOCK)
                scores[g, b] = dot(outputs[g][rows, :], inputs[g][:, rows])

    half = BLOCK // 2
    causal = lax.broadcasted_iota(jnp.int32, (half, half), 0) >= lax.broadcasted_iota(
        jnp.int32, (half, half), 1
    )
    for p in range(STEP_PAIRS):
        columns = slice(p * PAIR, (p + 1) * PAIR)
        slots = [slot_ref[step * 2 * STEP_PAIRS + 2 * p + i] for i in range(2)]
        for b in range(2):
            rows = slice(b * BLOCK, (b + 1) * BLOCK)
            x = x_ref[rows, columns]
            early, late = [], []
            for i in range(2):
                running = prep_ref[2 * p + i, 0:1, rows]
                size = prep_ref[2 * p + i, 1:2, rows]
                down = jnp.broadcast_to(running, (half, BLOCK)).T

                def tile(t, s, masked):
                    ts, ss = slice(t * half, (t + 1) * half), slice(s * half, (s + 1) * half)
                    spread = down[ts] - running[:, ss]
                    score = scores[slots[i], b, ts, ss]
                    value = score * jnp.exp(spread) * size[:, ss]
                    return (jnp.where(causal, value, 0.0) if masked else value).astype(BF16)

                early.append(tile(0, 0, True))
                late.append(tile(1, 0, False))
                late.append(tile(1, 1, True))
            both = split_pair(x)
            first = jnp.concatenate([both[0:half], both[BLOCK : BLOCK + half]], axis=0)
            skipped = skip_ref[:, columns] * x.astype(F32)
            top = dot(jnp.concatenate(early, axis=1), first)
            bottom = dot(jnp.concatenate(late, axis=1), both)
            out_ref[b * BLOCK : b * BLOCK + half, columns] = top + skipped[0:half]
            out_ref[b * BLOCK + half : (b + 1) * BLOCK, columns] = bottom + skipped[half:]


def project_kernel(
    slot_ref,
    place_ref,
    within_ref,
    prep_ref,
    gain_ref,
    enter_ref,
    fresh_ref,
    o0,
    o1,
    o2a,
    o2b,
    o3,
    w_ref,
    own_ref,
    up_ref,
    far_ref,
    down_ref,
    maps,
    normed,
    total,
):
    step = pl.program_id(0)

    @pl.when(step == 0)
    def _():
        maps[0:2] = o0[...]
        maps[2:4] = o1[...]
        maps[4] = o2a[...]
        maps[5] = o2b[...]
        maps[6:8] = o3[...]
        total[...] = jnp.zeros_like(total)

    same = (
        lax.broadcasted_iota(jnp.int32, (2 * PAIR, PAIR), 0) % PAIR // P_SIZE
        == lax.broadcasted_iota(jnp.int32, (2 * PAIR, PAIR), 1) // P_SIZE
    )
    summing = jnp.where(same, 1.0, 0.0).astype(BF16)
    for p in range(STEP_PAIRS):
        columns = slice(p * PAIR, (p + 1) * PAIR)
        slots = [slot_ref[step * 2 * STEP_PAIRS + 2 * p + i] for i in range(2)]
        growth = columns_of(prep_ref[2 * p, 3:4, :], prep_ref[2 * p + 1, 3:4, :])
        first_end = lane_pair(
            prep_ref[2 * p, 3:4, BLOCK - 1 : BLOCK], prep_ref[2 * p + 1, 3:4, BLOCK - 1 : BLOCK]
        )
        arriving = enter_ref[p].astype(F32)
        entering = [arriving, first_end * arriving + fresh_ref[p]]
        for b in range(2):
            rows = slice(b * BLOCK, (b + 1) * BLOCK)
            left = jnp.concatenate([maps[slots[0], rows, :], maps[slots[1], rows, :]], axis=1)
            carried = dot(left, split_pair(entering[b].astype(BF16)))
            y = within_ref[rows, columns] + carried * growth[rows]
            square = y * y
            high = square.astype(BF16)
            low = (square - high.astype(F32)).astype(BF16)
            mean = dot(jnp.concatenate([high, low], axis=1), summing) * (1.0 / P_SIZE)
            normed[rows, columns] = (y * lax.rsqrt(mean + EPS) * gain_ref[:, columns]).astype(BF16)
    total[...] += dot(normed[...], w_ref[...])

    @pl.when(step == pl.num_programs(0) - 1)
    def _():
        share = own_ref.shape[0]

        def rows_for(offset):
            place = lax.rem(place_ref[0] + offset, 4)
            return total[pl.ds(pl.multiple_of(place * share, share), share), :]

        own_ref[...] = rows_for(0)
        up_ref[...] = rows_for(1)
        far_ref[...] = rows_for(2).astype(BF16)
        down_ref[...] = rows_for(3)


def put_cells(stage, j, value):
    for h in range(2):
        stage[h, pl.ds(j, value.shape[0], stride=ROW), :] = value[:, h * 128 : (h + 1) * 128]


def take_cells(stage, j, count):
    return jnp.concatenate(
        [stage[h, pl.ds(j, count, stride=ROW), :] for h in range(2)], axis=1
    ).astype(BF16)


def fill_stage(stage, rows_ref):
    for h in range(2):
        stage[h] = rows_ref[:, h * 128 : (h + 1) * 128].astype(F32)


def drain_stage(stage, rows_ref):
    for h in range(2):
        rows_ref[:, h * 128 : (h + 1) * 128] = stage[h].astype(BF16)


def tokens_kernel(
    residual_ref,
    own_ref,
    prev_ref,
    next_ref,
    gain_ref,
    router_ref,
    ids_ref,
    stream_ref,
    weight_ref,
    *rest,
    ring,
):
    out_refs, (stage, tokens) = rest[:-2], rest[-2:]
    share, width = stream_ref.shape
    stream = (
        residual_ref[...].astype(F32)
        + own_ref[...]
        + prev_ref[...].astype(F32)
        + next_ref[...].astype(F32)
    )
    stream_ref[...] = stream
    square = jnp.mean(stream * stream, axis=-1, keepdims=True)
    tokens[...] = (stream * lax.rsqrt(square + EPS) * gain_ref[...]).astype(BF16)
    experts = router_ref.shape[1]
    place = lax.broadcasted_iota(jnp.int32, (share, experts), 1)
    hosted = place % ring * (experts // ring) + place // ring
    routed = jnp.zeros((share, experts), F32)
    for k in range(ids_ref.shape[1]):
        routed = routed + jnp.where(ids_ref[:, k : k + 1] == hosted, 1.0, 0.0)
    earlier = jnp.where(
        lax.broadcasted_iota(jnp.int32, (share, share), 0)
        > lax.broadcasted_iota(jnp.int32, (share, share), 1),
        1.0,
        0.0,
    ).astype(BF16)
    rank = dot(earlier, routed.astype(BF16))
    key = jnp.where(routed > 0.5, rank, -1.0).astype(BF16)
    logits = dot(tokens[...], router_ref[...])
    weight = 1.0 / (1.0 + jnp.exp(-logits))
    high = weight.astype(BF16)
    low = (weight - high.astype(F32)).astype(BF16)
    chunk = SLOTS // CHUNKS
    rows = experts * chunk
    spread = jnp.where(
        lax.broadcasted_iota(jnp.int32, (experts, rows), 0)
        == lax.broadcasted_iota(jnp.int32, (experts, rows), 1) // chunk,
        1.0,
        0.0,
    ).astype(BF16)
    wide = dot(jnp.concatenate([key, high, low], axis=0), spread)
    ranks, highs, lows = wide[:share], wide[share : 2 * share], wide[2 * share :]
    slot = (lax.broadcasted_iota(jnp.int32, (share, rows), 1) % chunk).astype(F32)
    for i in range(CHUNKS):
        placed = ranks == slot + float(i * chunk)
        weight_ref[i, :share] = jnp.where(placed, highs, 0.0).astype(BF16)
        weight_ref[i, share:] = jnp.where(placed, lows, 0.0).astype(BF16)
        pick = jnp.where(placed, 1.0, 0.0).T.astype(BF16)
        for j in range(ROW):
            put_cells(stage, j, dot(pick, tokens[:, j * CELL : (j + 1) * CELL]))
        drain_stage(stage, out_refs[i])


def experts_kernel(x_ref, g0, u0, d0, g1, u1, d1, out_ref, stage, rows, total, *, half_steps):
    step = pl.program_id(0)
    count, width = rows.shape
    last = 2 * half_steps - 1

    @pl.when(step == 0)
    def _():
        fill_stage(stage, x_ref)
        for j in range(ROW):
            rows[:, j * CELL : (j + 1) * CELL] = take_cells(stage, j, count)

    def work(gate, up, down):
        x = rows[...]
        gated = dot(x, gate[...])
        hidden = (gated / (1.0 + jnp.exp(-gated)) * dot(x, up[...])).astype(BF16)
        for c in range(0, width, 2 * CELL):
            part = dot(hidden, down[:, c : c + 2 * CELL])

            @pl.when(step == 0)
            def _():
                total[:, c : c + 2 * CELL] = part

            @pl.when(step > 0)
            def _():
                total[:, c : c + 2 * CELL] += part

    pl.when(step < half_steps)(lambda: work(g0, u0, d0))
    pl.when(step >= half_steps)(lambda: work(g1, u1, d1))

    @pl.when(step == last)
    def _():
        for j in range(ROW):
            put_cells(stage, j, total[:, j * CELL : (j + 1) * CELL])
        drain_stage(stage, out_ref)


def combine_kernel(base_ref, weight_ref, rows_ref, out_ref, stage):
    share = base_ref.shape[0]
    count = weight_ref.shape[1]
    fill_stage(stage, rows_ref)
    for j in range(ROW):
        columns = slice(j * CELL, (j + 1) * CELL)
        part = dot(weight_ref[...], take_cells(stage, j, count))
        out_ref[:, columns] = (base_ref[:, columns] + part[:share] + part[share:]).astype(
            out_ref.dtype
        )


def whole(shape):
    return pl.BlockSpec(shape, lambda s, *_: (0,) * len(shape))


def params(mib=56):
    return pltpu.CompilerParams(
        dimension_semantics=("arbitrary",), vmem_limit_bytes=mib * MIB
    )


def ring_gather(own, nxt, prv):
    from_prev = lax.ppermute(own, "exp", nxt)
    from_next = lax.ppermute(own, "exp", prv)
    far_a = lax.ppermute(from_prev[0], "exp", nxt)
    far_b = lax.ppermute(from_next[1], "exp", prv)
    return own, from_next, far_a, far_b, from_prev


def body(
    ssd_input,
    dt_raw,
    dt_bias,
    log_decay,
    input_map,
    output_map,
    head_group,
    d_skip,
    norm_gain,
    w_out,
    residual,
    moe_gain,
    w_router,
    expert_ids,
    w_gate,
    w_up,
    w_down,
):
    length = ssd_input.shape[0]
    heads = dt_raw.shape[1]
    blocks = length // BLOCK
    width = w_out.shape[1]
    share = residual.shape[0]
    me = lax.axis_index("exp")
    ring = lax.axis_size("exp")
    seq_count = lax.axis_size("seq")
    nxt = [(i, (i + 1) % ring) for i in range(ring)]
    prv = [(i, (i - 1) % ring) for i in range(ring)]
    partner = [(i, i ^ 1) for i in range(seq_count)]
    steps = heads // (2 * STEP_PAIRS)
    columns = STEP_PAIRS * PAIR

    in_maps = ring_gather(input_map.transpose(1, 2, 0), nxt, prv)
    output_first = output_map.transpose(1, 0, 2)
    output_first, *_ = lax.optimization_barrier((output_first, in_maps[2], in_maps[3]))
    out_maps = ring_gather(output_first, nxt, prv)
    slot = (lax.rem(head_group // 2 - me + ring, ring) * 2 + head_group % 2).astype(jnp.int32)

    other_gate = lax.ppermute(w_gate[0], "seq", partner)
    other_up = lax.ppermute(w_up[0], "seq", partner)
    other_down = lax.ppermute(w_down[0], "seq", partner)

    step_size = jax.nn.softplus(dt_raw + dt_bias[None, :])
    running = jnp.cumsum(log_decay.reshape(blocks, BLOCK, heads), axis=1)
    to_end = jnp.exp(running[:, -1:, :] - running).reshape(length, heads) * step_size
    running = running.reshape(length, heads)
    prep = jnp.stack([running, step_size, to_end, jnp.exp(running)], axis=0).transpose(2, 0, 1)
    skip_lanes = jnp.repeat(d_skip, P_SIZE)[None, :]
    gain_lanes = norm_gain[None, :]

    x_spec = pl.BlockSpec((length, columns), lambda s, *_: (0, s))
    prep_spec = pl.BlockSpec((2 * STEP_PAIRS, 4, length), lambda s, *_: (s, 0, 0))
    lane_spec = pl.BlockSpec((1, columns), lambda s, *_: (0, s))
    state_spec = pl.BlockSpec((STEP_PAIRS, NST, PAIR), lambda s, *_: (s, 0, 0))
    in_specs = [whole((2, NST, length))] * 2 + [whole((NST, length))] * 2 + [whole((2, NST, length))]
    out_specs = [whole((2, length, NST))] * 2 + [whole((length, NST))] * 2 + [whole((2, length, NST))]

    fresh, sending = pl.pallas_call(
        states_kernel,
        grid_spec=pltpu.PrefetchScalarGridSpec(
            num_scalar_prefetch=1,
            grid=(steps,),
            in_specs=[x_spec, prep_spec] + in_specs,
            out_specs=[state_spec, pl.BlockSpec((2 * STEP_PAIRS, 72, PAIR), lambda s, *_: (s, 0, 0))],
            scratch_shapes=[pltpu.VMEM((G, NST, length), BF16)],
        ),
        out_shape=[
            jax.ShapeDtypeStruct((heads // 2, NST, PAIR), F32),
            jax.ShapeDtypeStruct((heads, 72, PAIR), BF16),
        ],
        compiler_params=params(16),
        cost_estimate=pl.CostEstimate(
            flops=600_000_000, bytes_accessed=5_000_000, transcendentals=0
        ),
        name="states",
    )(slot, ssd_input, prep, *in_maps)

    arrived = lax.all_to_all(sending, "seq", split_axis=0, concat_axis=0, tiled=True)
    prefix = pl.pallas_call(
        scan_kernel,
        out_shape=jax.ShapeDtypeStruct((seq_count, 64, PAIR), BF16),
        compiler_params=pltpu.CompilerParams(vmem_limit_bytes=16 * MIB),
        name="scan",
    )(arrived)
    entering = lax.all_to_all(prefix, "seq", split_axis=0, concat_axis=0, tiled=True)
    entering = entering.reshape(heads // 2, NST, PAIR)

    within = pl.pallas_call(
        within_kernel,
        grid_spec=pltpu.PrefetchScalarGridSpec(
            num_scalar_prefetch=1,
            grid=(steps,),
            in_specs=[x_spec, prep_spec, lane_spec] + in_specs + out_specs,
            out_specs=x_spec,
            scratch_shapes=[pltpu.VMEM((G, 2, BLOCK, BLOCK), F32)],
        ),
        out_shape=jax.ShapeDtypeStruct(ssd_input.shape, F32),
        compiler_params=params(24),
        cost_estimate=pl.CostEstimate(
            flops=12_000_000_000, bytes_accessed=8_000_000, transcendentals=4_000_000
        ),
        name="within",
    )(slot, ssd_input, prep, skip_lanes, *in_maps, *out_maps)

    share_spec = whole((share, width))
    own, up, far, down = pl.pallas_call(
        project_kernel,
        grid_spec=pltpu.PrefetchScalarGridSpec(
            num_scalar_prefetch=2,
            grid=(steps,),
            in_specs=[x_spec, prep_spec, lane_spec, state_spec, state_spec]
            + out_specs
            + [pl.BlockSpec((columns, width), lambda s, *_: (s, 0))],
            out_specs=[share_spec] * 4,
            scratch_shapes=[
                pltpu.VMEM((G, length, NST), BF16),
                pltpu.VMEM((length, columns), BF16),
                pltpu.VMEM((length, width), F32),
            ],
        ),
        out_shape=[
            jax.ShapeDtypeStruct((share, width), F32),
            jax.ShapeDtypeStruct((share, width), F32),
            jax.ShapeDtypeStruct((share, width), BF16),
            jax.ShapeDtypeStruct((share, width), F32),
        ],
        compiler_params=params(36),
        cost_estimate=pl.CostEstimate(
            flops=6_000_000_000, bytes_accessed=18_000_000, transcendentals=0
        ),
        name="project",
    )(slot, me[None].astype(jnp.int32), within, prep, gain_lanes, entering, fresh, *out_maps, w_out)

    middle = width // 2
    far_left = lax.ppermute(far[:, :middle], "exp", nxt)
    far_right = lax.ppermute(far[:, middle:], "exp", prv)
    up = jnp.concatenate([up[:, :middle] + far_left.astype(F32), up[:, middle:]], axis=1).astype(BF16)
    down = jnp.concatenate(
        [down[:, :middle], down[:, middle:] + far_right.astype(F32)], axis=1
    ).astype(BF16)
    from_prev = lax.ppermute(up, "exp", nxt)
    from_next = lax.ppermute(down, "exp", prv)
    experts = w_router.shape[1]
    per_group = experts // ring
    router = w_router.reshape(-1, ring, per_group).swapaxes(1, 2).reshape(-1, experts)
    chunk = SLOTS // CHUNKS
    count = experts * chunk
    cells = (count * ROW, CELL)
    stage = (2, count * ROW, CELL // 2)
    stream, weights, *outgoing = pl.pallas_call(
        functools.partial(tokens_kernel, ring=ring),
        out_shape=[
            jax.ShapeDtypeStruct((share, width), F32),
            jax.ShapeDtypeStruct((CHUNKS, 2 * share, count), BF16),
        ]
        + [jax.ShapeDtypeStruct(cells, BF16)] * CHUNKS,
        scratch_shapes=[pltpu.VMEM(stage, F32), pltpu.VMEM((share, width), BF16)],
        compiler_params=pltpu.CompilerParams(vmem_limit_bytes=32 * MIB),
        cost_estimate=pl.CostEstimate(
            flops=1_000_000_000, bytes_accessed=8_000_000, transcendentals=0
        ),
        name="tokens",
    )(residual, own, from_prev, from_next, moe_gain[None, :], router, expert_ids)

    cores = [
        [(c // ring * 2 + h) * ring + c % ring for c in range(experts)] for h in range(2)
    ]

    def swap(rows):
        swapped = lax.all_to_all(
            rows.reshape(count, ROW, CELL),
            ("seq", "exp"),
            split_axis=0,
            concat_axis=0,
            tiled=True,
            axis_index_groups=cores,
        )
        return swapped.reshape(cells)

    half_steps = 4
    block = w_gate.shape[2] // half_steps

    def first_half(s):
        return jnp.minimum(s, half_steps - 1)

    def second_half(s):
        return jnp.maximum(s - half_steps, 0)

    def weight_specs(at):
        return [pl.BlockSpec((width, block), lambda s: (0, at(s)))] * 2 + [
            pl.BlockSpec((block, width), lambda s: (at(s), 0))
        ]

    run_experts = pl.pallas_call(
        functools.partial(experts_kernel, half_steps=half_steps),
        grid=(2 * half_steps,),
        in_specs=[pl.BlockSpec(cells, lambda s: (0, 0))]
        + weight_specs(first_half)
        + weight_specs(second_half),
        out_specs=pl.BlockSpec(cells, lambda s: (0, 0)),
        out_shape=jax.ShapeDtypeStruct(cells, BF16),
        scratch_shapes=[
            pltpu.VMEM(stage, F32),
            pltpu.VMEM((count, width), BF16),
            pltpu.VMEM((count, width), F32),
        ],
        compiler_params=params(48),
        cost_estimate=pl.CostEstimate(
            flops=12 * count * width * w_gate.shape[2],
            bytes_accessed=28_000_000,
            transcendentals=0,
        ),
        name="experts",
    )

    def combine(base, weight, rows, dtype):
        return pl.pallas_call(
            combine_kernel,
            out_shape=jax.ShapeDtypeStruct((share, width), dtype),
            scratch_shapes=[pltpu.VMEM(stage, F32)],
            compiler_params=pltpu.CompilerParams(vmem_limit_bytes=24 * MIB),
            cost_estimate=pl.CostEstimate(
                flops=500_000_000, bytes_accessed=4_000_000, transcendentals=0
            ),
            name="combine",
        )(base, weight, rows)

    arrivals = [swap(rows) for rows in outgoing]
    returned = [
        swap(
            run_experts(
                rows, w_gate[0], w_up[0], w_down[0], other_gate, other_up, other_down
            )
        )
        for rows in arrivals
    ]
    mixed = stream
    for i in range(CHUNKS):
        mixed = combine(mixed, weights[i], returned[i], BF16 if i == CHUNKS - 1 else F32)
    return mixed


def solution(mesh):
    return jax.shard_map(
        body,
        mesh=mesh,
        in_specs=(
            P("seq", "exp"),
            P("seq", "exp"),
            P("exp"),
            P("seq", "exp"),
            P("seq", "exp", None),
            P("seq", "exp", None),
            P("exp"),
            P("exp"),
            P("exp"),
            P("exp", None),
            P(("seq", "exp"), None),
            P(),
            P(),
            P(("seq", "exp"), None),
            P(("seq", "exp"), None, None),
            P(("seq", "exp"), None, None),
            P(("seq", "exp"), None, None),
        ),
        out_specs=P(("seq", "exp"), None),
        check_vma=False,
    )
```

```python
import functools

import jax
import jax.numpy as jnp
from jax import lax
from jax.experimental import pallas as pl
from jax.experimental.pallas import tpu as pltpu
from jax.sharding import PartitionSpec as P

P_SIZE = 64
NST = 128
G = 8
BLOCK = 256
PAIR = 2 * P_SIZE
STEP_PAIRS = 4
SLOTS = 14
CHUNKS = 2
ROW = 8
CELL = 256

EPS = 1e-06
F32 = jnp.float32
BF16 = jnp.bfloat16
MIB = 1024 * 1024


def dot(a, b):
    return jnp.dot(a, b, preferred_element_type=F32)


def lanes_of_first(shape):
    return lax.broadcasted_iota(jnp.int32, shape, 1) < P_SIZE


def columns_of(first_row, second_row):
    length = first_row.shape[1]
    rows = jnp.concatenate(
        [
            jnp.broadcast_to(first_row, (P_SIZE, length)),
            jnp.broadcast_to(second_row, (P_SIZE, length)),
        ],
        axis=0,
    )
    return rows.T


def lane_pair(first, second):
    return jnp.concatenate(
        [jnp.broadcast_to(first, (1, P_SIZE)), jnp.broadcast_to(second, (1, P_SIZE))], axis=1
    )


def split_pair(values):
    first = lanes_of_first(values.shape)
    zero = jnp.zeros_like(values)
    return jnp.concatenate([jnp.where(first, values, zero), jnp.where(first, zero, values)], axis=0)


def states_kernel(slot_ref, x_ref, prep_ref, m0, m1, m2a, m2b, m3, fresh_ref, send_ref, maps):
    step = pl.program_id(0)

    @pl.when(step == 0)
    def _():
        maps[0:2] = m0[...]
        maps[2:4] = m1[...]
        maps[4] = m2a[...]
        maps[5] = m2b[...]
        maps[6:8] = m3[...]

    for p in range(STEP_PAIRS):
        slots = [slot_ref[step * 2 * STEP_PAIRS + 2 * p + i] for i in range(2)]
        x = x_ref[:, p * PAIR : (p + 1) * PAIR].astype(F32)
        weight = columns_of(prep_ref[2 * p, 2:3, :], prep_ref[2 * p + 1, 2:3, :])
        scaled = (x * weight).astype(BF16)
        fresh = []
        for b in range(2):
            rows = slice(b * BLOCK, (b + 1) * BLOCK)
            both = split_pair(scaled[rows])
            left = jnp.concatenate([maps[slots[0], :, rows], maps[slots[1], :, rows]], axis=1)
            fresh.append(dot(left, both))
        ends = [
            lane_pair(
                prep_ref[2 * p, 3:4, e - 1 : e],
                prep_ref[2 * p + 1, 3:4, e - 1 : e],
            )
            for e in (BLOCK, 2 * BLOCK)
        ]
        fresh_ref[p] = fresh[0]
        final = (ends[1] * fresh[0] + fresh[1]).astype(BF16)
        decay = ends[0] * ends[1]
        high = decay.astype(BF16).astype(F32)
        row = lax.broadcasted_iota(jnp.int32, (8, PAIR), 0)
        tail = jnp.where(row == 0, high, jnp.where(row == 1, decay - high, 0.0)).astype(BF16)
        for i in range(2):
            send_ref[2 * p + i, 0:64] = final[64 * i : 64 * (i + 1)]
            send_ref[2 * p + i, 64:72] = tail


def scan_kernel(in_ref, out_ref):
    state = jnp.zeros((64, PAIR), F32)
    for j in range(in_ref.shape[0]):
        out_ref[j] = state.astype(BF16)
        tail = in_ref[j, 64:72].astype(F32)
        decay = tail[0:1] + tail[1:2]
        state = decay * state + in_ref[j, 0:64].astype(F32)


def within_kernel(
    slot_ref, x_ref, prep_ref, skip_ref, i0, i1, i2a, i2b, i3, o0, o1, o2a, o2b, o3, out_ref, scores
):
    step = pl.program_id(0)

    @pl.when(step == 0)
    def _():
        inputs = [i0.at[0], i0.at[1], i1.at[0], i1.at[1], i2a, i2b, i3.at[0], i3.at[1]]
        outputs = [o0.at[0], o0.at[1], o1.at[0], o1.at[1], o2a, o2b, o3.at[0], o3.at[1]]
        for g in range(G):
            for b in range(2):
                rows = slice(b * BLOCK, (b + 1) * BLOCK)
                scores[g, b] = dot(outputs[g][rows, :], inputs[g][:, rows])

    half = BLOCK // 2
    causal = lax.broadcasted_iota(jnp.int32, (half, half), 0) >= lax.broadcasted_iota(
        jnp.int32, (half, half), 1
    )
    for p in range(STEP_PAIRS):
        columns = slice(p * PAIR, (p + 1) * PAIR)
        slots = [slot_ref[step * 2 * STEP_PAIRS + 2 * p + i] for i in range(2)]
        for b in range(2):
            rows = slice(b * BLOCK, (b + 1) * BLOCK)
            x = x_ref[rows, columns]
            early, late = [], []
            for i in range(2):
                running = prep_ref[2 * p + i, 0:1, rows]
                size = prep_ref[2 * p + i, 1:2, rows]
                down = jnp.broadcast_to(running, (half, BLOCK)).T

                def tile(t, s, masked):
                    ts, ss = slice(t * half, (t + 1) * half), slice(s * half, (s + 1) * half)
                    spread = down[ts] - running[:, ss]
                    score = scores[slots[i], b, ts, ss]
                    value = score * jnp.exp(spread) * size[:, ss]
                    return (jnp.where(causal, value, 0.0) if masked else value).astype(BF16)

                early.append(tile(0, 0, True))
                late.append(tile(1, 0, False))
                late.append(tile(1, 1, True))
            both = split_pair(x)
            first = jnp.concatenate([both[0:half], both[BLOCK : BLOCK + half]], axis=0)
            skipped = skip_ref[:, columns] * x.astype(F32)
            top = dot(jnp.concatenate(early, axis=1), first)
            bottom = dot(jnp.concatenate(late, axis=1), both)
            out_ref[b * BLOCK : b * BLOCK + half, columns] = top + skipped[0:half]
            out_ref[b * BLOCK + half : (b + 1) * BLOCK, columns] = bottom + skipped[half:]


def project_kernel(
    offsets,
    slot_ref,
    place_ref,
    within_ref,
    prep_ref,
    gain_ref,
    enter_ref,
    fresh_ref,
    o0,
    o1,
    o2a,
    o2b,
    o3,
    w_ref,
    *rest,
):
    out_refs, (maps, states, normed, total) = rest[:-4], rest[-4:]
    step = pl.program_id(0)

    @pl.when(step == 0)
    def _():
        maps[0:2] = o0[...]
        maps[2:4] = o1[...]
        maps[4] = o2a[...]
        maps[5] = o2b[...]
        maps[6:8] = o3[...]
        total[...] = jnp.zeros_like(total)

    share = total.shape[0] // len(offsets)
    places = [lax.rem(place_ref[0] + offset, 4) for offset in offsets]
    same = (
        lax.broadcasted_iota(jnp.int32, (2 * PAIR, PAIR), 0) % PAIR // P_SIZE
        == lax.broadcasted_iota(jnp.int32, (2 * PAIR, PAIR), 1) // P_SIZE
    )
    summing = jnp.where(same, 1.0, 0.0).astype(BF16)
    for p in range(STEP_PAIRS):
        columns = slice(p * PAIR, (p + 1) * PAIR)
        slots = [slot_ref[step * 2 * STEP_PAIRS + 2 * p + i] for i in range(2)]
        first_end = lane_pair(
            prep_ref[2 * p, 3:4, BLOCK - 1 : BLOCK], prep_ref[2 * p + 1, 3:4, BLOCK - 1 : BLOCK]
        )
        arriving = enter_ref[p].astype(F32)
        states[p, 0] = split_pair(arriving.astype(BF16))
        states[p, 1] = split_pair((first_end * arriving + fresh_ref[p]).astype(BF16))
        for i, place in enumerate(places):
            rows = pl.ds(pl.multiple_of(place * share, share), share)
            growth = columns_of(prep_ref[2 * p, 3:4, rows], prep_ref[2 * p + 1, 3:4, rows])
            left = jnp.concatenate([maps[slots[0], rows, :], maps[slots[1], rows, :]], axis=1)
            carried = dot(left, states[p, place // (BLOCK // share)])
            y = within_ref[rows, columns] + carried * growth
            square = y * y
            high = square.astype(BF16)
            low = (square - high.astype(F32)).astype(BF16)
            mean = dot(jnp.concatenate([high, low], axis=1), summing) * (1.0 / P_SIZE)
            normed[i * share : (i + 1) * share, columns] = (
                y * lax.rsqrt(mean + EPS) * gain_ref[:, columns]
            ).astype(BF16)
    total[...] += dot(normed[...], w_ref[...])

    @pl.when(step == pl.num_programs(0) - 1)
    def _():
        if len(offsets) == 1:
            middle = total.shape[1] // 2
            out_refs[0][...] = total[:, :middle].astype(BF16)
            out_refs[1][...] = total[:, middle:].astype(BF16)
        else:
            for i, out_ref in enumerate(out_refs):
                out_ref[...] = total[i * share : (i + 1) * share, :]


def put_cells(stage, j, value):
    for h in range(2):
        stage[h, pl.ds(j, value.shape[0], stride=ROW), :] = value[:, h * 128 : (h + 1) * 128]


def take_cells(stage, j, count):
    return jnp.concatenate(
        [stage[h, pl.ds(j, count, stride=ROW), :] for h in range(2)], axis=1
    ).astype(BF16)


def fill_stage(stage, rows_ref):
    for h in range(2):
        stage[h] = rows_ref[:, h * 128 : (h + 1) * 128].astype(F32)


def drain_stage(stage, rows_ref):
    for h in range(2):
        rows_ref[:, h * 128 : (h + 1) * 128] = stage[h].astype(BF16)


def tokens_kernel(
    residual_ref,
    own_ref,
    prev_ref,
    next_ref,
    gain_ref,
    router_ref,
    ids_ref,
    stream_ref,
    weight_ref,
    *rest,
    ring,
):
    out_refs, (stage, tokens) = rest[:-2], rest[-2:]
    share, width = stream_ref.shape
    stream = (
        residual_ref[...].astype(F32)
        + own_ref[...]
        + prev_ref[...].astype(F32)
        + next_ref[...].astype(F32)
    )
    stream_ref[...] = stream
    square = jnp.mean(stream * stream, axis=-1, keepdims=True)
    tokens[...] = (stream * lax.rsqrt(square + EPS) * gain_ref[...]).astype(BF16)
    experts = router_ref.shape[1]
    place = lax.broadcasted_iota(jnp.int32, (share, experts), 1)
    hosted = place % ring * (experts // ring) + place // ring
    routed = jnp.zeros((share, experts), F32)
    for k in range(ids_ref.shape[1]):
        routed = routed + jnp.where(ids_ref[:, k : k + 1] == hosted, 1.0, 0.0)
    earlier = jnp.where(
        lax.broadcasted_iota(jnp.int32, (share, share), 0)
        > lax.broadcasted_iota(jnp.int32, (share, share), 1),
        1.0,
        0.0,
    ).astype(BF16)
    rank = dot(earlier, routed.astype(BF16))
    key = jnp.where(routed > 0.5, rank, -1.0).astype(BF16)
    logits = dot(tokens[...], router_ref[...])
    weight = 1.0 / (1.0 + jnp.exp(-logits))
    high = weight.astype(BF16)
    low = (weight - high.astype(F32)).astype(BF16)
    chunk = SLOTS // CHUNKS
    rows = experts * chunk
    spread = jnp.where(
        lax.broadcasted_iota(jnp.int32, (experts, rows), 0)
        == lax.broadcasted_iota(jnp.int32, (experts, rows), 1) // chunk,
        1.0,
        0.0,
    ).astype(BF16)
    wide = dot(jnp.concatenate([key, high, low], axis=0), spread)
    ranks, highs, lows = wide[:share], wide[share : 2 * share], wide[2 * share :]
    slot = (lax.broadcasted_iota(jnp.int32, (share, rows), 1) % chunk).astype(F32)
    for i in range(CHUNKS):
        placed = ranks == slot + float(i * chunk)
        weight_ref[i, :share] = jnp.where(placed, highs, 0.0).astype(BF16)
        weight_ref[i, share:] = jnp.where(placed, lows, 0.0).astype(BF16)
        pick = jnp.where(placed, 1.0, 0.0).T.astype(BF16)
        for j in range(ROW):
            put_cells(stage, j, dot(pick, tokens[:, j * CELL : (j + 1) * CELL]))
        drain_stage(stage, out_refs[i])


def experts_kernel(
    x_ref, g0, u0, d0, g1, u1, d1, out_ref, stage, rows, hidden, wide, deep, wide_sem, deep_sem
):
    count, width = rows.shape
    unit = g0.shape[1]
    n_wide, n_deep = wide.shape[0], deep.shape[0]
    wide_step, deep_step = 2 * unit // n_wide, width // n_deep
    halves = [(g0, u0, d0), (g1, u1, d1)]

    def copies(s):
        if s < n_wide:
            half = halves[s * wide_step // unit]
            columns = pl.ds(s * wide_step % unit, wide_step)
            return [
                pltpu.make_async_copy(half[i].at[:, columns], wide.at[s, i], wide_sem.at[s, i])
                for i in range(2)
            ]
        s -= n_wide
        columns = pl.ds(s * deep_step, deep_step)
        return [
            pltpu.make_async_copy(
                halves[i][2].at[:, columns], deep.at[s, pl.ds(i * unit, unit)], deep_sem.at[s, i]
            )
            for i in range(2)
        ]

    total_steps = n_wide + n_deep
    ahead = 3
    for s in range(ahead):
        for copy in copies(s):
            copy.start()
    fill_stage(stage, x_ref)
    for j in range(ROW):
        rows[:, j * CELL : (j + 1) * CELL] = take_cells(stage, j, count)
    for s in range(total_steps):
        if s + ahead < total_steps:
            for copy in copies(s + ahead):
                copy.start()
        for copy in copies(s):
            copy.wait()
        if s < n_wide:
            gated = dot(rows[...], wide[s, 0])
            raised = dot(rows[...], wide[s, 1])
            hidden[:, s * wide_step : (s + 1) * wide_step] = (
                gated / (1.0 + jnp.exp(-gated)) * raised
            ).astype(BF16)
        else:
            d = s - n_wide
            for c in range(deep_step // CELL):
                part = dot(hidden[...], deep[d, :, c * CELL : (c + 1) * CELL])
                put_cells(stage, d * (deep_step // CELL) + c, part)
    drain_stage(stage, out_ref)


def combine_kernel(base_ref, weight_ref, rows_ref, out_ref, stage):
    share = base_ref.shape[0]
    count = weight_ref.shape[1]
    fill_stage(stage, rows_ref)
    for j in range(ROW):
        columns = slice(j * CELL, (j + 1) * CELL)
        part = dot(weight_ref[...], take_cells(stage, j, count))
        out_ref[:, columns] = (base_ref[:, columns] + part[:share] + part[share:]).astype(
            out_ref.dtype
        )


def whole(shape):
    return pl.BlockSpec(shape, lambda s, *_: (0,) * len(shape))


def params(mib=60):
    return pltpu.CompilerParams(
        dimension_semantics=("arbitrary",), vmem_limit_bytes=mib * MIB
    )


def ring_gather(own, nxt, prv):
    from_prev = lax.ppermute(own, "exp", nxt)
    from_next = lax.ppermute(own, "exp", prv)
    far_a = lax.ppermute(from_prev[0], "exp", nxt)
    far_b = lax.ppermute(from_next[1], "exp", prv)
    return own, from_next, far_a, far_b, from_prev


def body(
    ssd_input,
    dt_raw,
    dt_bias,
    log_decay,
    input_map,
    output_map,
    head_group,
    d_skip,
    norm_gain,
    w_out,
    residual,
    moe_gain,
    w_router,
    expert_ids,
    w_gate,
    w_up,
    w_down,
):
    length = ssd_input.shape[0]
    heads = dt_raw.shape[1]
    blocks = length // BLOCK
    width = w_out.shape[1]
    share = residual.shape[0]
    me = lax.axis_index("exp")
    ring = lax.axis_size("exp")
    seq_count = lax.axis_size("seq")
    nxt = [(i, (i + 1) % ring) for i in range(ring)]
    prv = [(i, (i - 1) % ring) for i in range(ring)]
    partner = [(i, i ^ 1) for i in range(seq_count)]
    steps = heads // (2 * STEP_PAIRS)
    columns = STEP_PAIRS * PAIR

    in_maps = ring_gather(input_map.transpose(1, 2, 0), nxt, prv)
    slot = (lax.rem(head_group // 2 - me + ring, ring) * 2 + head_group % 2).astype(jnp.int32)

    other_gate = lax.ppermute(w_gate[0], "seq", partner)
    other_up = lax.ppermute(w_up[0], "seq", partner)
    other_down = lax.ppermute(w_down[0], "seq", partner)

    step_size = jax.nn.softplus(dt_raw + dt_bias[None, :])
    running = jnp.cumsum(log_decay.reshape(blocks, BLOCK, heads), axis=1)
    to_end = jnp.exp(running[:, -1:, :] - running).reshape(length, heads) * step_size
    running = running.reshape(length, heads)
    prep = jnp.stack([running, step_size, to_end, jnp.exp(running)], axis=0).transpose(2, 0, 1)
    skip_lanes = jnp.repeat(d_skip, P_SIZE)[None, :]
    gain_lanes = norm_gain[None, :]

    x_spec = pl.BlockSpec((length, columns), lambda s, *_: (0, s))
    prep_spec = pl.BlockSpec((2 * STEP_PAIRS, 4, length), lambda s, *_: (s, 0, 0))
    lane_spec = pl.BlockSpec((1, columns), lambda s, *_: (0, s))
    state_spec = pl.BlockSpec((STEP_PAIRS, NST, PAIR), lambda s, *_: (s, 0, 0))
    in_specs = [whole((2, NST, length))] * 2 + [whole((NST, length))] * 2 + [whole((2, NST, length))]
    out_specs = [whole((2, length, NST))] * 2 + [whole((length, NST))] * 2 + [whole((2, length, NST))]

    fresh, sending = pl.pallas_call(
        states_kernel,
        grid_spec=pltpu.PrefetchScalarGridSpec(
            num_scalar_prefetch=1,
            grid=(steps,),
            in_specs=[x_spec, prep_spec] + in_specs,
            out_specs=[state_spec, pl.BlockSpec((2 * STEP_PAIRS, 72, PAIR), lambda s, *_: (s, 0, 0))],
            scratch_shapes=[pltpu.VMEM((G, NST, length), BF16)],
        ),
        out_shape=[
            jax.ShapeDtypeStruct((heads // 2, NST, PAIR), F32),
            jax.ShapeDtypeStruct((heads, 72, PAIR), BF16),
        ],
        compiler_params=params(),
        cost_estimate=pl.CostEstimate(
            flops=600_000_000, bytes_accessed=5_000_000, transcendentals=0
        ),
        name="states",
    )(slot, ssd_input, prep, *in_maps)

    output_first, fresh, sending = lax.optimization_barrier(
        (output_map.transpose(1, 0, 2), fresh, sending)
    )
    out_maps = ring_gather(output_first, nxt, prv)

    arrived = lax.all_to_all(sending, "seq", split_axis=0, concat_axis=0, tiled=True)
    prefix = pl.pallas_call(
        scan_kernel,
        out_shape=jax.ShapeDtypeStruct((seq_count, 64, PAIR), BF16),
        compiler_params=pltpu.CompilerParams(vmem_limit_bytes=60 * MIB),
        name="scan",
    )(arrived)
    entering = lax.all_to_all(prefix, "seq", split_axis=0, concat_axis=0, tiled=True)
    entering = entering.reshape(heads // 2, NST, PAIR)

    within = pl.pallas_call(
        within_kernel,
        grid_spec=pltpu.PrefetchScalarGridSpec(
            num_scalar_prefetch=1,
            grid=(steps,),
            in_specs=[x_spec, prep_spec, lane_spec] + in_specs + out_specs,
            out_specs=x_spec,
            scratch_shapes=[pltpu.VMEM((G, 2, BLOCK, BLOCK), F32)],
        ),
        out_shape=jax.ShapeDtypeStruct(ssd_input.shape, F32),
        compiler_params=params(),
        cost_estimate=pl.CostEstimate(
            flops=12_000_000_000, bytes_accessed=8_000_000, transcendentals=4_000_000
        ),
        name="within",
    )(slot, ssd_input, prep, skip_lanes, *in_maps, *out_maps)

    middle = width // 2

    def project(offsets, outs, name):
        return pl.pallas_call(
            functools.partial(project_kernel, offsets),
            grid_spec=pltpu.PrefetchScalarGridSpec(
                num_scalar_prefetch=2,
                grid=(steps,),
                in_specs=[x_spec, prep_spec, lane_spec, state_spec, state_spec]
                + out_specs
                + [pl.BlockSpec((columns, width), lambda s, *_: (s, 0))],
                out_specs=[whole(out.shape) for out in outs],
                scratch_shapes=[
                    pltpu.VMEM((G, length, NST), BF16),
                    pltpu.VMEM((STEP_PAIRS, 2, 2 * PAIR, PAIR), BF16),
                    pltpu.VMEM((share * len(offsets), columns), BF16),
                    pltpu.VMEM((share * len(offsets), width), F32),
                ],
            ),
            out_shape=outs,
            compiler_params=params(),
            cost_estimate=pl.CostEstimate(
                flops=3_000_000_000 * len(offsets),
                bytes_accessed=18_000_000,
                transcendentals=0,
            ),
            name=name,
        )(
            slot,
            me[None].astype(jnp.int32),
            within,
            prep,
            gain_lanes,
            entering,
            fresh,
            *out_maps,
            w_out,
        )

    far = project((2,), [jax.ShapeDtypeStruct((share, middle), BF16)] * 2, "project_far")
    far_left = lax.ppermute(far[0], "exp", nxt)
    far_right = lax.ppermute(far[1], "exp", prv)
    own, up, down = project((0, 1, 3), [jax.ShapeDtypeStruct((share, width), F32)] * 3, "project_near")
    up = jnp.concatenate([up[:, :middle] + far_left.astype(F32), up[:, middle:]], axis=1).astype(BF16)
    down = jnp.concatenate(
        [down[:, :middle], down[:, middle:] + far_right.astype(F32)], axis=1
    ).astype(BF16)
    from_prev = lax.ppermute(up, "exp", nxt)
    from_next = lax.ppermute(down, "exp", prv)
    experts = w_router.shape[1]
    per_group = experts // ring
    router = w_router.reshape(-1, ring, per_group).swapaxes(1, 2).reshape(-1, experts)
    chunk = SLOTS // CHUNKS
    count = experts * chunk
    cells = (count * ROW, CELL)
    stage = (2, count * ROW, CELL // 2)
    stream, weights, *outgoing = pl.pallas_call(
        functools.partial(tokens_kernel, ring=ring),
        out_shape=[
            jax.ShapeDtypeStruct((share, width), F32),
            jax.ShapeDtypeStruct((CHUNKS, 2 * share, count), BF16),
        ]
        + [jax.ShapeDtypeStruct(cells, BF16)] * CHUNKS,
        scratch_shapes=[pltpu.VMEM(stage, F32), pltpu.VMEM((share, width), BF16)],
        compiler_params=pltpu.CompilerParams(vmem_limit_bytes=60 * MIB),
        cost_estimate=pl.CostEstimate(
            flops=1_000_000_000, bytes_accessed=8_000_000, transcendentals=0
        ),
        name="tokens",
    )(residual, own, from_prev, from_next, moe_gain[None, :], router, expert_ids)

    cores = [
        [(c // ring * 2 + h) * ring + c % ring for c in range(experts)] for h in range(2)
    ]

    def swap(rows):
        swapped = lax.all_to_all(
            rows.reshape(count, ROW, CELL),
            ("seq", "exp"),
            split_axis=0,
            concat_axis=0,
            tiled=True,
            axis_index_groups=cores,
        )
        return swapped.reshape(cells)

    unit = w_gate.shape[2]
    hbm = pl.BlockSpec(memory_space=pl.ANY)
    run_experts = pl.pallas_call(
        experts_kernel,
        in_specs=[pl.BlockSpec(memory_space=pltpu.VMEM)] + [hbm] * 6,
        out_specs=pl.BlockSpec(memory_space=pltpu.VMEM),
        out_shape=jax.ShapeDtypeStruct(cells, BF16),
        scratch_shapes=[
            pltpu.VMEM(stage, F32),
            pltpu.VMEM((count, width), BF16),
            pltpu.VMEM((count, 2 * unit), BF16),
            pltpu.VMEM((8, 2, width, unit // 4), BF16),
            pltpu.VMEM((4, 2 * unit, width // 4), BF16),
            pltpu.SemaphoreType.DMA((8, 2)),
            pltpu.SemaphoreType.DMA((4, 2)),
        ],
        compiler_params=pltpu.CompilerParams(vmem_limit_bytes=60 * MIB),
        cost_estimate=pl.CostEstimate(
            flops=12 * count * width * unit,
            bytes_accessed=28_000_000,
            transcendentals=0,
        ),
        name="experts",
    )

    def combine(base, weight, rows, dtype):
        return pl.pallas_call(
            combine_kernel,
            out_shape=jax.ShapeDtypeStruct((share, width), dtype),
            scratch_shapes=[pltpu.VMEM(stage, F32)],
            compiler_params=pltpu.CompilerParams(vmem_limit_bytes=60 * MIB),
            cost_estimate=pl.CostEstimate(
                flops=500_000_000, bytes_accessed=4_000_000, transcendentals=0
            ),
            name="combine",
        )(base, weight, rows)

    arrivals = [swap(rows) for rows in outgoing]
    returned = [
        swap(
            run_experts(
                rows, w_gate[0], w_up[0], w_down[0], other_gate, other_up, other_down
            )
        )
        for rows in arrivals
    ]
    mixed = stream
    for i in range(CHUNKS):
        mixed = combine(mixed, weights[i], returned[i], BF16 if i == CHUNKS - 1 else F32)
    return mixed


def solution(mesh):
    return jax.shard_map(
        body,
        mesh=mesh,
        in_specs=(
            P("seq", "exp"),
            P("seq", "exp"),
            P("exp"),
            P("seq", "exp"),
            P("seq", "exp", None),
            P("seq", "exp", None),
            P("exp"),
            P("exp"),
            P("exp"),
            P("exp", None),
            P(("seq", "exp"), None),
            P(),
            P(),
            P(("seq", "exp"), None),
            P(("seq", "exp"), None, None),
            P(("seq", "exp"), None, None),
            P(("seq", "exp"), None, None),
        ),
        out_specs=P(("seq", "exp"), None),
        check_vma=False,
    )
```

```python
import functools

import jax
import jax.numpy as jnp
from jax import lax
from jax.experimental import pallas as pl
from jax.experimental.pallas import tpu as pltpu
from jax.sharding import PartitionSpec as P

P_SIZE = 64
NST = 128
G = 8
BLOCK = 256
PAIR = 2 * P_SIZE
STEP_PAIRS = 4
SLOTS = 14
CHUNKS = 2
ROW = 8
CELL = 256

EPS = 1e-06
F32 = jnp.float32
BF16 = jnp.bfloat16
MIB = 1024 * 1024


def dot(a, b):
    return jnp.dot(a, b, preferred_element_type=F32)


def lanes_of_first(shape):
    return lax.broadcasted_iota(jnp.int32, shape, 1) < P_SIZE


def columns_of(first_row, second_row):
    length = first_row.shape[1]
    rows = jnp.concatenate(
        [
            jnp.broadcast_to(first_row, (P_SIZE, length)),
            jnp.broadcast_to(second_row, (P_SIZE, length)),
        ],
        axis=0,
    )
    return rows.T


def lane_pair(first, second):
    return jnp.concatenate(
        [jnp.broadcast_to(first, (1, P_SIZE)), jnp.broadcast_to(second, (1, P_SIZE))], axis=1
    )


def split_pair(values):
    first = lanes_of_first(values.shape)
    zero = jnp.zeros_like(values)
    return jnp.concatenate([jnp.where(first, values, zero), jnp.where(first, zero, values)], axis=0)


def states_kernel(slot_ref, x_ref, prep_ref, m0, m1, m2a, m2b, m3, fresh_ref, send_ref, maps):
    step = pl.program_id(0)

    @pl.when(step == 0)
    def _():
        maps[0:2] = m0[...]
        maps[2:4] = m1[...]
        maps[4] = m2a[...]
        maps[5] = m2b[...]
        maps[6:8] = m3[...]

    for p in range(STEP_PAIRS):
        slots = [slot_ref[step * 2 * STEP_PAIRS + 2 * p + i] for i in range(2)]
        x = x_ref[:, p * PAIR : (p + 1) * PAIR].astype(F32)
        weight = columns_of(prep_ref[2 * p, 2:3, :], prep_ref[2 * p + 1, 2:3, :])
        scaled = (x * weight).astype(BF16)
        fresh = []
        for b in range(2):
            rows = slice(b * BLOCK, (b + 1) * BLOCK)
            both = split_pair(scaled[rows])
            left = jnp.concatenate([maps[slots[0], :, rows], maps[slots[1], :, rows]], axis=1)
            fresh.append(dot(left, both))
        ends = [
            lane_pair(
                prep_ref[2 * p, 3:4, e - 1 : e],
                prep_ref[2 * p + 1, 3:4, e - 1 : e],
            )
            for e in (BLOCK, 2 * BLOCK)
        ]
        fresh_ref[p] = fresh[0]
        final = (ends[1] * fresh[0] + fresh[1]).astype(BF16)
        decay = ends[0] * ends[1]
        high = decay.astype(BF16).astype(F32)
        row = lax.broadcasted_iota(jnp.int32, (8, PAIR), 0)
        tail = jnp.where(row == 0, high, jnp.where(row == 1, decay - high, 0.0)).astype(BF16)
        for i in range(2):
            send_ref[2 * p + i, 0:64] = final[64 * i : 64 * (i + 1)]
            send_ref[2 * p + i, 64:72] = tail


def scan_kernel(in_ref, out_ref):
    state = jnp.zeros((64, PAIR), F32)
    for j in range(in_ref.shape[0]):
        out_ref[j] = state.astype(BF16)
        tail = in_ref[j, 64:72].astype(F32)
        decay = tail[0:1] + tail[1:2]
        state = decay * state + in_ref[j, 0:64].astype(F32)


def within_kernel(
    slot_ref, x_ref, prep_ref, skip_ref, i0, i1, i2a, i2b, i3, o0, o1, o2a, o2b, o3, out_ref, scores
):
    step = pl.program_id(0)

    @pl.when(step == 0)
    def _():
        inputs = [i0.at[0], i0.at[1], i1.at[0], i1.at[1], i2a, i2b, i3.at[0], i3.at[1]]
        outputs = [o0.at[0], o0.at[1], o1.at[0], o1.at[1], o2a, o2b, o3.at[0], o3.at[1]]
        for g in range(G):
            for b in range(2):
                rows = slice(b * BLOCK, (b + 1) * BLOCK)
                scores[g, b] = dot(outputs[g][rows, :], inputs[g][:, rows])

    half = BLOCK // 2
    causal = lax.broadcasted_iota(jnp.int32, (half, half), 0) >= lax.broadcasted_iota(
        jnp.int32, (half, half), 1
    )
    for p in range(STEP_PAIRS):
        columns = slice(p * PAIR, (p + 1) * PAIR)
        slots = [slot_ref[step * 2 * STEP_PAIRS + 2 * p + i] for i in range(2)]
        for b in range(2):
            rows = slice(b * BLOCK, (b + 1) * BLOCK)
            x = x_ref[rows, columns]
            early, late = [], []
            for i in range(2):
                running = prep_ref[2 * p + i, 0:1, rows]
                size = prep_ref[2 * p + i, 1:2, rows]
                down = jnp.broadcast_to(running, (half, BLOCK)).T

                def tile(t, s, masked):
                    ts, ss = slice(t * half, (t + 1) * half), slice(s * half, (s + 1) * half)
                    spread = down[ts] - running[:, ss]
                    score = scores[slots[i], b, ts, ss]
                    value = score * jnp.exp(spread) * size[:, ss]
                    return (jnp.where(causal, value, 0.0) if masked else value).astype(BF16)

                early.append(tile(0, 0, True))
                late.append(tile(1, 0, False))
                late.append(tile(1, 1, True))
            both = split_pair(x)
            first = jnp.concatenate([both[0:half], both[BLOCK : BLOCK + half]], axis=0)
            skipped = skip_ref[:, columns] * x.astype(F32)
            top = dot(jnp.concatenate(early, axis=1), first)
            bottom = dot(jnp.concatenate(late, axis=1), both)
            out_ref[b * BLOCK : b * BLOCK + half, columns] = top + skipped[0:half]
            out_ref[b * BLOCK + half : (b + 1) * BLOCK, columns] = bottom + skipped[half:]


def project_kernel(
    slot_ref,
    place_ref,
    prep_ref,
    gain_ref,
    enter_ref,
    fresh_ref,
    within_hbm,
    o0,
    o1,
    o2a,
    o2b,
    o3,
    w_hbm,
    own_ref,
    far_left,
    far_right,
    up_left,
    up_right,
    down_left,
    down_right,
    maps,
    within,
    normed,
    weights,
    total,
    map_sem,
    within_sem,
    weight_sem,
):
    parts, length, columns = within.shape
    share = own_ref.shape[0]
    map_copies = [
        pltpu.make_async_copy(o0, maps.at[pl.ds(0, 2)], map_sem.at[0]),
        pltpu.make_async_copy(o1, maps.at[pl.ds(2, 2)], map_sem.at[1]),
        pltpu.make_async_copy(o2a, maps.at[4], map_sem.at[2]),
        pltpu.make_async_copy(o2b, maps.at[5], map_sem.at[3]),
        pltpu.make_async_copy(o3, maps.at[pl.ds(6, 2)], map_sem.at[4]),
    ]
    within_copies = [
        pltpu.make_async_copy(
            within_hbm.at[:, pl.ds(i * columns, columns)], within.at[i], within_sem.at[i]
        )
        for i in range(parts)
    ]
    weight_copies = [
        pltpu.make_async_copy(
            w_hbm.at[:, pl.ds(i * columns, columns)], weights.at[i], weight_sem.at[i]
        )
        for i in range(parts)
    ]
    for copy in map_copies + within_copies + weight_copies:
        copy.start()
    for copy in map_copies:
        copy.wait()
    same = (
        lax.broadcasted_iota(jnp.int32, (2 * PAIR, PAIR), 0) % PAIR // P_SIZE
        == lax.broadcasted_iota(jnp.int32, (2 * PAIR, PAIR), 1) // P_SIZE
    )
    summing = jnp.where(same, 1.0, 0.0).astype(BF16)
    per_part = columns // PAIR
    for p in range(parts * per_part):
        if p % per_part == 0:
            within_copies[p // per_part].wait()
        here = slice(p % per_part * PAIR, (p % per_part + 1) * PAIR)
        there = slice(p * PAIR, (p + 1) * PAIR)
        slots = [slot_ref[2 * p + i] for i in range(2)]
        growth = columns_of(prep_ref[2 * p, 3:4, :], prep_ref[2 * p + 1, 3:4, :])
        first_end = lane_pair(
            prep_ref[2 * p, 3:4, BLOCK - 1 : BLOCK], prep_ref[2 * p + 1, 3:4, BLOCK - 1 : BLOCK]
        )
        arriving = enter_ref[p].astype(F32)
        entering = [arriving, first_end * arriving + fresh_ref[p]]
        for b in range(length // BLOCK):
            rows = slice(b * BLOCK, (b + 1) * BLOCK)
            left = jnp.concatenate([maps[slots[0], rows, :], maps[slots[1], rows, :]], axis=1)
            carried = dot(left, split_pair(entering[b].astype(BF16)))
            y = within[p // per_part, rows, here] + carried * growth[rows]
            square = y * y
            high = square.astype(BF16)
            low = (square - high.astype(F32)).astype(BF16)
            mean = dot(jnp.concatenate([high, low], axis=1), summing) * (1.0 / P_SIZE)
            normed[rows, there] = (y * lax.rsqrt(mean + EPS) * gain_ref[:, there]).astype(BF16)

    def rows_for(offset):
        place = lax.rem(place_ref[0] + offset, 4)
        return total[pl.ds(pl.multiple_of(place * share, share), share), :]

    for i in range(parts):
        weight_copies[i].wait()
        total[...] = dot(normed[...], weights[i])
        side = i * 2 // parts
        there = slice(i * columns, (i + 1) * columns)
        here = slice(i % (parts // 2) * columns, (i % (parts // 2) + 1) * columns)
        own_ref[:, there] = rows_for(0)
        up_ref, far_ref, down_ref = (
            (up_left, far_left, down_left) if side == 0 else (up_right, far_right, down_right)
        )
        up_ref[:, here] = rows_for(1).astype(up_ref.dtype)
        far_ref[:, here] = rows_for(2).astype(far_ref.dtype)
        down_ref[:, here] = rows_for(3).astype(down_ref.dtype)


def put_cells(stage, j, value):
    for h in range(2):
        stage[h, pl.ds(j, value.shape[0], stride=ROW), :] = value[:, h * 128 : (h + 1) * 128]


def take_cells(stage, j, count):
    return jnp.concatenate(
        [stage[h, pl.ds(j, count, stride=ROW), :] for h in range(2)], axis=1
    ).astype(BF16)


def fill_stage(stage, rows_ref):
    for h in range(2):
        stage[h] = rows_ref[:, h * 128 : (h + 1) * 128].astype(F32)


def drain_stage(stage, rows_ref):
    for h in range(2):
        rows_ref[:, h * 128 : (h + 1) * 128] = stage[h].astype(BF16)


def tokens_kernel(
    residual_ref,
    own_ref,
    prev_left,
    prev_right,
    next_left,
    next_right,
    gain_ref,
    router_ref,
    ids_ref,
    stream_ref,
    weight_ref,
    *rest,
    ring,
):
    out_refs, (stage, tokens) = rest[:-2], rest[-2:]
    share, width = stream_ref.shape
    received = jnp.concatenate(
        [
            prev_left[...].astype(F32) + next_left[...].astype(F32),
            prev_right[...].astype(F32) + next_right[...].astype(F32),
        ],
        axis=1,
    )
    stream = residual_ref[...].astype(F32) + own_ref[...] + received
    stream_ref[...] = stream
    square = jnp.mean(stream * stream, axis=-1, keepdims=True)
    tokens[...] = (stream * lax.rsqrt(square + EPS) * gain_ref[...]).astype(BF16)
    experts = router_ref.shape[1]
    place = lax.broadcasted_iota(jnp.int32, (share, experts), 1)
    hosted = place % ring * (experts // ring) + place // ring
    routed = jnp.zeros((share, experts), F32)
    for k in range(ids_ref.shape[1]):
        routed = routed + jnp.where(ids_ref[:, k : k + 1] == hosted, 1.0, 0.0)
    earlier = jnp.where(
        lax.broadcasted_iota(jnp.int32, (share, share), 0)
        > lax.broadcasted_iota(jnp.int32, (share, share), 1),
        1.0,
        0.0,
    ).astype(BF16)
    rank = dot(earlier, routed.astype(BF16))
    key = jnp.where(routed > 0.5, rank, -1.0).astype(BF16)
    logits = dot(tokens[...], router_ref[...])
    weight = 1.0 / (1.0 + jnp.exp(-logits))
    high = weight.astype(BF16)
    low = (weight - high.astype(F32)).astype(BF16)
    chunk = SLOTS // CHUNKS
    rows = experts * chunk
    spread = jnp.where(
        lax.broadcasted_iota(jnp.int32, (experts, rows), 0)
        == lax.broadcasted_iota(jnp.int32, (experts, rows), 1) // chunk,
        1.0,
        0.0,
    ).astype(BF16)
    wide = dot(jnp.concatenate([key, high, low], axis=0), spread)
    ranks, highs, lows = wide[:share], wide[share : 2 * share], wide[2 * share :]
    slot = (lax.broadcasted_iota(jnp.int32, (share, rows), 1) % chunk).astype(F32)
    for i in range(CHUNKS):
        placed = ranks == slot + float(i * chunk)
        weight_ref[i, :share] = jnp.where(placed, highs, 0.0).astype(BF16)
        weight_ref[i, share:] = jnp.where(placed, lows, 0.0).astype(BF16)
        pick = jnp.where(placed, 1.0, 0.0).T.astype(BF16)
        for j in range(ROW):
            put_cells(stage, j, dot(pick, tokens[:, j * CELL : (j + 1) * CELL]))
        drain_stage(stage, out_refs[i])


def experts_kernel(
    x_ref, g0, u0, d0, g1, u1, d1, out_ref, stage, rows, hidden, wide, deep, wide_sem, deep_sem
):
    count, width = rows.shape
    unit = g0.shape[1]
    n_wide, n_deep = wide.shape[0], deep.shape[0]
    wide_step, deep_step = 2 * unit // n_wide, width // n_deep
    halves = [(g0, u0, d0), (g1, u1, d1)]

    def copies(s):
        if s < n_wide:
            half = halves[s * wide_step // unit]
            columns = pl.ds(s * wide_step % unit, wide_step)
            return [
                pltpu.make_async_copy(half[i].at[:, columns], wide.at[s, i], wide_sem.at[s, i])
                for i in range(2)
            ]
        s -= n_wide
        columns = pl.ds(s * deep_step, deep_step)
        return [
            pltpu.make_async_copy(
                halves[i][2].at[:, columns], deep.at[s, pl.ds(i * unit, unit)], deep_sem.at[s, i]
            )
            for i in range(2)
        ]

    total_steps = n_wide + n_deep
    ahead = 3
    for s in range(ahead):
        for copy in copies(s):
            copy.start()
    fill_stage(stage, x_ref)
    for j in range(ROW):
        rows[:, j * CELL : (j + 1) * CELL] = take_cells(stage, j, count)
    for s in range(total_steps):
        if s + ahead < total_steps:
            for copy in copies(s + ahead):
                copy.start()
        for copy in copies(s):
            copy.wait()
        if s < n_wide:
            gated = dot(rows[...], wide[s, 0])
            raised = dot(rows[...], wide[s, 1])
            hidden[:, s * wide_step : (s + 1) * wide_step] = (
                gated / (1.0 + jnp.exp(-gated)) * raised
            ).astype(BF16)
        else:
            d = s - n_wide
            for c in range(deep_step // CELL):
                part = dot(hidden[...], deep[d, :, c * CELL : (c + 1) * CELL])
                put_cells(stage, d * (deep_step // CELL) + c, part)
    drain_stage(stage, out_ref)


def combine_kernel(base_ref, weight_ref, rows_ref, out_ref, stage):
    share = base_ref.shape[0]
    count = weight_ref.shape[1]
    fill_stage(stage, rows_ref)
    for j in range(ROW):
        columns = slice(j * CELL, (j + 1) * CELL)
        part = dot(weight_ref[...], take_cells(stage, j, count))
        out_ref[:, columns] = (base_ref[:, columns] + part[:share] + part[share:]).astype(
            out_ref.dtype
        )


def whole(shape):
    return pl.BlockSpec(shape, lambda s, *_: (0,) * len(shape))


def params(mib=60):
    return pltpu.CompilerParams(
        dimension_semantics=("arbitrary",), vmem_limit_bytes=mib * MIB
    )


def ring_gather(own, nxt, prv):
    from_prev = lax.ppermute(own, "exp", nxt)
    from_next = lax.ppermute(own, "exp", prv)
    far_a = lax.ppermute(from_prev[0], "exp", nxt)
    far_b = lax.ppermute(from_next[1], "exp", prv)
    return own, from_next, far_a, far_b, from_prev


def body(
    ssd_input,
    dt_raw,
    dt_bias,
    log_decay,
    input_map,
    output_map,
    head_group,
    d_skip,
    norm_gain,
    w_out,
    residual,
    moe_gain,
    w_router,
    expert_ids,
    w_gate,
    w_up,
    w_down,
):
    length = ssd_input.shape[0]
    heads = dt_raw.shape[1]
    blocks = length // BLOCK
    width = w_out.shape[1]
    share = residual.shape[0]
    me = lax.axis_index("exp")
    ring = lax.axis_size("exp")
    seq_count = lax.axis_size("seq")
    nxt = [(i, (i + 1) % ring) for i in range(ring)]
    prv = [(i, (i - 1) % ring) for i in range(ring)]
    partner = [(i, i ^ 1) for i in range(seq_count)]
    steps = heads // (2 * STEP_PAIRS)
    columns = STEP_PAIRS * PAIR

    in_maps = ring_gather(input_map.transpose(1, 2, 0), nxt, prv)
    slot = (lax.rem(head_group // 2 - me + ring, ring) * 2 + head_group % 2).astype(jnp.int32)

    other_gate = lax.ppermute(w_gate[0], "seq", partner)
    other_up = lax.ppermute(w_up[0], "seq", partner)
    other_down = lax.ppermute(w_down[0], "seq", partner)

    step_size = jax.nn.softplus(dt_raw + dt_bias[None, :])
    running = jnp.cumsum(log_decay.reshape(blocks, BLOCK, heads), axis=1)
    to_end = jnp.exp(running[:, -1:, :] - running).reshape(length, heads) * step_size
    running = running.reshape(length, heads)
    prep = jnp.stack([running, step_size, to_end, jnp.exp(running)], axis=0).transpose(2, 0, 1)
    skip_lanes = jnp.repeat(d_skip, P_SIZE)[None, :]
    gain_lanes = norm_gain[None, :]

    x_spec = pl.BlockSpec((length, columns), lambda s, *_: (0, s))
    prep_spec = pl.BlockSpec((2 * STEP_PAIRS, 4, length), lambda s, *_: (s, 0, 0))
    lane_spec = pl.BlockSpec((1, columns), lambda s, *_: (0, s))
    state_spec = pl.BlockSpec((STEP_PAIRS, NST, PAIR), lambda s, *_: (s, 0, 0))
    in_specs = [whole((2, NST, length))] * 2 + [whole((NST, length))] * 2 + [whole((2, NST, length))]
    out_specs = [whole((2, length, NST))] * 2 + [whole((length, NST))] * 2 + [whole((2, length, NST))]

    fresh, sending = pl.pallas_call(
        states_kernel,
        grid_spec=pltpu.PrefetchScalarGridSpec(
            num_scalar_prefetch=1,
            grid=(steps,),
            in_specs=[x_spec, prep_spec] + in_specs,
            out_specs=[state_spec, pl.BlockSpec((2 * STEP_PAIRS, 72, PAIR), lambda s, *_: (s, 0, 0))],
            scratch_shapes=[pltpu.VMEM((G, NST, length), BF16)],
        ),
        out_shape=[
            jax.ShapeDtypeStruct((heads // 2, NST, PAIR), F32),
            jax.ShapeDtypeStruct((heads, 72, PAIR), BF16),
        ],
        compiler_params=params(16),
        cost_estimate=pl.CostEstimate(
            flops=600_000_000, bytes_accessed=5_000_000, transcendentals=0
        ),
        name="states",
    )(slot, ssd_input, prep, *in_maps)

    output_first, fresh, sending = lax.optimization_barrier(
        (output_map.transpose(1, 0, 2), fresh, sending)
    )
    out_maps = ring_gather(output_first, nxt, prv)

    arrived = lax.all_to_all(sending, "seq", split_axis=0, concat_axis=0, tiled=True)
    prefix = pl.pallas_call(
        scan_kernel,
        out_shape=jax.ShapeDtypeStruct((seq_count, 64, PAIR), BF16),
        compiler_params=pltpu.CompilerParams(vmem_limit_bytes=16 * MIB),
        name="scan",
    )(arrived)
    entering = lax.all_to_all(prefix, "seq", split_axis=0, concat_axis=0, tiled=True)
    entering = entering.reshape(heads // 2, NST, PAIR)

    within = pl.pallas_call(
        within_kernel,
        grid_spec=pltpu.PrefetchScalarGridSpec(
            num_scalar_prefetch=1,
            grid=(steps,),
            in_specs=[x_spec, prep_spec, lane_spec] + in_specs + out_specs,
            out_specs=x_spec,
            scratch_shapes=[pltpu.VMEM((G, 2, BLOCK, BLOCK), F32)],
        ),
        out_shape=jax.ShapeDtypeStruct(ssd_input.shape, F32),
        compiler_params=params(),
        cost_estimate=pl.CostEstimate(
            flops=12_000_000_000, bytes_accessed=8_000_000, transcendentals=4_000_000
        ),
        name="within",
    )(slot, ssd_input, prep, skip_lanes, *in_maps, *out_maps)

    middle = width // 2

    parts = width // columns
    half_wide = jax.ShapeDtypeStruct((share, middle), F32)
    half_sent = jax.ShapeDtypeStruct((share, middle), BF16)
    vmem = pl.BlockSpec(memory_space=pltpu.VMEM)
    smem = pl.BlockSpec(memory_space=pltpu.SMEM)
    hbm = pl.BlockSpec(memory_space=pl.ANY)
    own, far_left, far_right, up_left, up_right, down_left, down_right = pl.pallas_call(
        project_kernel,
        in_specs=[smem] * 2 + [vmem] * 4 + [hbm] * 7,
        out_specs=[vmem] * 7,
        out_shape=[
            jax.ShapeDtypeStruct((share, width), F32),
            half_sent,
            half_sent,
            half_wide,
            half_sent,
            half_sent,
            half_wide,
        ],
        scratch_shapes=[
            pltpu.VMEM((G, length, NST), BF16),
            pltpu.VMEM((parts, length, columns), F32),
            pltpu.VMEM((length, heads * P_SIZE), BF16),
            pltpu.VMEM((parts, heads * P_SIZE, columns), BF16),
            pltpu.VMEM((length, columns), F32),
            pltpu.SemaphoreType.DMA((5,)),
            pltpu.SemaphoreType.DMA((parts,)),
            pltpu.SemaphoreType.DMA((parts,)),
        ],
        compiler_params=pltpu.CompilerParams(vmem_limit_bytes=60 * MIB),
        cost_estimate=pl.CostEstimate(
            flops=6_000_000_000, bytes_accessed=18_000_000, transcendentals=0
        ),
        name="project",
    )(
        slot,
        me[None].astype(jnp.int32),
        prep,
        gain_lanes,
        entering,
        fresh,
        within,
        *out_maps,
        w_out,
    )

    got_left = lax.ppermute(far_left, "exp", nxt)
    got_right = lax.ppermute(far_right, "exp", prv)
    prev_right = lax.ppermute(up_right, "exp", nxt)
    next_left = lax.ppermute(down_left, "exp", prv)
    up_left = (up_left + got_left.astype(F32)).astype(BF16)
    down_right = (down_right + got_right.astype(F32)).astype(BF16)
    prev_left = lax.ppermute(up_left, "exp", nxt)
    next_right = lax.ppermute(down_right, "exp", prv)

    experts = w_router.shape[1]
    per_group = experts // ring
    router = w_router.reshape(-1, ring, per_group).swapaxes(1, 2).reshape(-1, experts)
    chunk = SLOTS // CHUNKS
    count = experts * chunk
    cells = (count * ROW, CELL)
    stage = (2, count * ROW, CELL // 2)
    stream, weights, *outgoing = pl.pallas_call(
        functools.partial(tokens_kernel, ring=ring),
        out_shape=[
            jax.ShapeDtypeStruct((share, width), F32),
            jax.ShapeDtypeStruct((CHUNKS, 2 * share, count), BF16),
        ]
        + [jax.ShapeDtypeStruct(cells, BF16)] * CHUNKS,
        scratch_shapes=[pltpu.VMEM(stage, F32), pltpu.VMEM((share, width), BF16)],
        compiler_params=pltpu.CompilerParams(vmem_limit_bytes=32 * MIB),
        cost_estimate=pl.CostEstimate(
            flops=1_000_000_000, bytes_accessed=8_000_000, transcendentals=0
        ),
        name="tokens",
    )(
        residual,
        own,
        prev_left,
        prev_right,
        next_left,
        next_right,
        moe_gain[None, :],
        router,
        expert_ids,
    )

    cores = [
        [(c // ring * 2 + h) * ring + c % ring for c in range(experts)] for h in range(2)
    ]

    def swap(rows):
        swapped = lax.all_to_all(
            rows.reshape(count, ROW, CELL),
            ("seq", "exp"),
            split_axis=0,
            concat_axis=0,
            tiled=True,
            axis_index_groups=cores,
        )
        return swapped.reshape(cells)

    unit = w_gate.shape[2]
    run_experts = pl.pallas_call(
        experts_kernel,
        in_specs=[vmem] + [hbm] * 6,
        out_specs=vmem,
        out_shape=jax.ShapeDtypeStruct(cells, BF16),
        scratch_shapes=[
            pltpu.VMEM(stage, F32),
            pltpu.VMEM((count, width), BF16),
            pltpu.VMEM((count, 2 * unit), BF16),
            pltpu.VMEM((8, 2, width, unit // 4), BF16),
            pltpu.VMEM((4, 2 * unit, width // 4), BF16),
            pltpu.SemaphoreType.DMA((8, 2)),
            pltpu.SemaphoreType.DMA((4, 2)),
        ],
        compiler_params=pltpu.CompilerParams(vmem_limit_bytes=60 * MIB),
        cost_estimate=pl.CostEstimate(
            flops=12 * count * width * unit,
            bytes_accessed=28_000_000,
            transcendentals=0,
        ),
        name="experts",
    )

    def combine(base, weight, rows, dtype):
        return pl.pallas_call(
            combine_kernel,
            out_shape=jax.ShapeDtypeStruct((share, width), dtype),
            scratch_shapes=[pltpu.VMEM(stage, F32)],
            compiler_params=pltpu.CompilerParams(vmem_limit_bytes=24 * MIB),
            cost_estimate=pl.CostEstimate(
                flops=500_000_000, bytes_accessed=4_000_000, transcendentals=0
            ),
            name="combine",
        )(base, weight, rows)

    arrivals = [swap(rows) for rows in outgoing]
    returned = [
        swap(
            run_experts(
                rows, w_gate[0], w_up[0], w_down[0], other_gate, other_up, other_down
            )
        )
        for rows in arrivals
    ]
    mixed = stream
    for i in range(CHUNKS):
        mixed = combine(mixed, weights[i], returned[i], BF16 if i == CHUNKS - 1 else F32)
    return mixed


def solution(mesh):
    return jax.shard_map(
        body,
        mesh=mesh,
        in_specs=(
            P("seq", "exp"),
            P("seq", "exp"),
            P("exp"),
            P("seq", "exp"),
            P("seq", "exp", None),
            P("seq", "exp", None),
            P("exp"),
            P("exp"),
            P("exp"),
            P("exp", None),
            P(("seq", "exp"), None),
            P(),
            P(),
            P(("seq", "exp"), None),
            P(("seq", "exp"), None, None),
            P(("seq", "exp"), None, None),
            P(("seq", "exp"), None, None),
        ),
        out_specs=P(("seq", "exp"), None),
        check_vma=False,
    )
```

```python
import functools

import jax
import jax.numpy as jnp
from jax import lax
from jax.experimental import pallas as pl
from jax.experimental.pallas import tpu as pltpu
from jax.sharding import PartitionSpec as P

P_SIZE = 64
NST = 128
G = 8
BLOCK = 256
PAIR = 2 * P_SIZE
STEP_PAIRS = 4
SLOTS = 14
CHUNKS = 2
ROW = 8
CELL = 256

EPS = 1e-06
F32 = jnp.float32
BF16 = jnp.bfloat16
MIB = 1024 * 1024


def dot(a, b):
    return jnp.dot(a, b, preferred_element_type=F32)


def lanes_of_first(shape):
    return lax.broadcasted_iota(jnp.int32, shape, 1) < P_SIZE


def columns_of(first_row, second_row):
    length = first_row.shape[1]
    rows = jnp.concatenate(
        [
            jnp.broadcast_to(first_row, (P_SIZE, length)),
            jnp.broadcast_to(second_row, (P_SIZE, length)),
        ],
        axis=0,
    )
    return rows.T


def lane_pair(first, second):
    return jnp.concatenate(
        [jnp.broadcast_to(first, (1, P_SIZE)), jnp.broadcast_to(second, (1, P_SIZE))], axis=1
    )


def split_pair(values):
    first = lanes_of_first(values.shape)
    zero = jnp.zeros_like(values)
    return jnp.concatenate([jnp.where(first, values, zero), jnp.where(first, zero, values)], axis=0)


def prep_kernel(raw_ref, bias_ref, decay_ref, out_ref):
    value = raw_ref[...] + bias_ref[...]
    size = jnp.maximum(value, 0.0) + jnp.log(1.0 + jnp.exp(-jnp.abs(value)))
    upto = jnp.where(
        lax.broadcasted_iota(jnp.int32, (BLOCK, BLOCK), 0)
        <= lax.broadcasted_iota(jnp.int32, (BLOCK, BLOCK), 1),
        1.0,
        0.0,
    ).astype(BF16)
    heads, length = size.shape
    for b in range(length // BLOCK):
        rows = slice(b * BLOCK, (b + 1) * BLOCK)
        rest = decay_ref[:, rows]
        terms = []
        for _ in range(3):
            terms.append(rest.astype(BF16))
            rest = rest - terms[-1].astype(F32)
        sums = dot(jnp.concatenate(terms, axis=0), upto)
        running = sums[:heads] + sums[heads : 2 * heads] + sums[2 * heads :]
        out_ref[0, :, rows] = running
        out_ref[1, :, rows] = size[:, rows]
        out_ref[2, :, rows] = jnp.exp(running[:, BLOCK - 1 :] - running) * size[:, rows]
        out_ref[3, :, rows] = jnp.exp(running)


def states_kernel(
    slot_ref,
    x_ref,
    prep_ref,
    m0,
    m1,
    m2a,
    m2b,
    m3,
    fresh_hbm,
    send_hbm,
    maps,
    fresh_all,
    send_all,
    fresh_sem,
    send_sem,
):
    step = pl.program_id(0)
    steps = fresh_sem.shape[0]

    def out_copies(at):
        pairs = pl.ds(at * STEP_PAIRS, STEP_PAIRS)
        pieces = pl.ds(at * 2 * STEP_PAIRS, 2 * STEP_PAIRS)
        return [
            pltpu.make_async_copy(send_all.at[pieces], send_hbm.at[pieces], send_sem.at[at]),
            pltpu.make_async_copy(fresh_all.at[pairs], fresh_hbm.at[pairs], fresh_sem.at[at]),
        ]

    @pl.when(step == 0)
    def _():
        maps[0:2] = m0[...]
        maps[2:4] = m1[...]
        maps[4] = m2a[...]
        maps[5] = m2b[...]
        maps[6:8] = m3[...]

    for p in range(STEP_PAIRS):
        slots = [slot_ref[step * 2 * STEP_PAIRS + 2 * p + i] for i in range(2)]
        x = x_ref[:, p * PAIR : (p + 1) * PAIR].astype(F32)
        weight = columns_of(prep_ref[2, 2 * p : 2 * p + 1, :], prep_ref[2, 2 * p + 1 : 2 * p + 2, :])
        scaled = (x * weight).astype(BF16)
        fresh = []
        for b in range(2):
            rows = slice(b * BLOCK, (b + 1) * BLOCK)
            both = split_pair(scaled[rows])
            left = jnp.concatenate([maps[slots[0], :, rows], maps[slots[1], :, rows]], axis=1)
            fresh.append(dot(left, both))
        ends = [
            lane_pair(
                prep_ref[3, 2 * p : 2 * p + 1, e - 1 : e],
                prep_ref[3, 2 * p + 1 : 2 * p + 2, e - 1 : e],
            )
            for e in (BLOCK, 2 * BLOCK)
        ]
        fresh_all[step * STEP_PAIRS + p] = fresh[0]
        final = (ends[1] * fresh[0] + fresh[1]).astype(BF16)
        decay = ends[0] * ends[1]
        high = decay.astype(BF16).astype(F32)
        row = lax.broadcasted_iota(jnp.int32, (8, PAIR), 0)
        tail = jnp.where(row == 0, high, jnp.where(row == 1, decay - high, 0.0)).astype(BF16)
        for i in range(2):
            piece = step * 2 * STEP_PAIRS + 2 * p + i
            send_all[piece, 0:64] = final[64 * i : 64 * (i + 1)]
            send_all[piece, 64:72] = tail
    for copy in out_copies(step):
        copy.start()

    @pl.when(step == steps - 1)
    def _():
        for at in range(steps):
            for copy in out_copies(at):
                copy.wait()


def scan_kernel(in_ref, out_ref):
    state = jnp.zeros((64, PAIR), F32)
    for j in range(in_ref.shape[0]):
        out_ref[j] = state.astype(BF16)
        tail = in_ref[j, 64:72].astype(F32)
        decay = tail[0:1] + tail[1:2]
        state = decay * state + in_ref[j, 0:64].astype(F32)


def within_kernel(
    slot_ref, x_ref, prep_ref, skip_ref, i0, i1, i2a, i2b, i3, o0, o1, o2a, o2b, o3, out_ref, scores
):
    step = pl.program_id(0)

    @pl.when(step == 0)
    def _():
        inputs = [i0.at[0], i0.at[1], i1.at[0], i1.at[1], i2a, i2b, i3.at[0], i3.at[1]]
        outputs = [o0.at[0], o0.at[1], o1.at[0], o1.at[1], o2a, o2b, o3.at[0], o3.at[1]]
        for g in range(G):
            for b in range(2):
                rows = slice(b * BLOCK, (b + 1) * BLOCK)
                scores[g, b] = dot(outputs[g][rows, :], inputs[g][:, rows])

    half = BLOCK // 2
    causal = lax.broadcasted_iota(jnp.int32, (half, half), 0) >= lax.broadcasted_iota(
        jnp.int32, (half, half), 1
    )
    for p in range(STEP_PAIRS):
        columns = slice(p * PAIR, (p + 1) * PAIR)
        slots = [slot_ref[step * 2 * STEP_PAIRS + 2 * p + i] for i in range(2)]
        for b in range(2):
            rows = slice(b * BLOCK, (b + 1) * BLOCK)
            x = x_ref[rows, columns]
            early, late = [], []
            for i in range(2):
                running = prep_ref[0, 2 * p + i : 2 * p + i + 1, rows]
                size = prep_ref[1, 2 * p + i : 2 * p + i + 1, rows]
                down = jnp.broadcast_to(running, (half, BLOCK)).T

                def tile(t, s, masked):
                    ts, ss = slice(t * half, (t + 1) * half), slice(s * half, (s + 1) * half)
                    spread = down[ts] - running[:, ss]
                    score = scores[slots[i], b, ts, ss]
                    value = score * jnp.exp(spread) * size[:, ss]
                    return (jnp.where(causal, value, 0.0) if masked else value).astype(BF16)

                early.append(tile(0, 0, True))
                late.append(tile(1, 0, False))
                late.append(tile(1, 1, True))
            both = split_pair(x)
            first = jnp.concatenate([both[0:half], both[BLOCK : BLOCK + half]], axis=0)
            skipped = skip_ref[:, columns] * x.astype(F32)
            top = dot(jnp.concatenate(early, axis=1), first)
            bottom = dot(jnp.concatenate(late, axis=1), both)
            out_ref[b * BLOCK : b * BLOCK + half, columns] = top + skipped[0:half]
            out_ref[b * BLOCK + half : (b + 1) * BLOCK, columns] = bottom + skipped[half:]


def project_kernel(
    slot_ref,
    place_ref,
    prep_ref,
    gain_ref,
    enter_ref,
    fresh_ref,
    within_hbm,
    o0,
    o1,
    o2a,
    o2b,
    o3,
    w_hbm,
    own_ref,
    far_left,
    far_right,
    up_ref,
    down_ref,
    maps,
    within,
    normed,
    weights,
    total,
    map_sem,
    within_sem,
    weight_sem,
):
    parts, length, columns = within.shape
    share = own_ref.shape[0]
    map_copies = [
        pltpu.make_async_copy(o0, maps.at[pl.ds(0, 2)], map_sem.at[0]),
        pltpu.make_async_copy(o1, maps.at[pl.ds(2, 2)], map_sem.at[1]),
        pltpu.make_async_copy(o2a, maps.at[4], map_sem.at[2]),
        pltpu.make_async_copy(o2b, maps.at[5], map_sem.at[3]),
        pltpu.make_async_copy(o3, maps.at[pl.ds(6, 2)], map_sem.at[4]),
    ]
    within_copies = [
        pltpu.make_async_copy(
            within_hbm.at[:, pl.ds(i * columns, columns)], within.at[i], within_sem.at[i]
        )
        for i in range(parts)
    ]
    weight_copies = [
        pltpu.make_async_copy(
            w_hbm.at[pl.ds(i * columns, columns), :], weights.at[i], weight_sem.at[i]
        )
        for i in range(parts)
    ]
    for copy in map_copies:
        copy.start()
    for pair in zip(within_copies, weight_copies, strict=True):
        for copy in pair:
            copy.start()
    for copy in map_copies:
        copy.wait()
    same = (
        lax.broadcasted_iota(jnp.int32, (2 * PAIR, PAIR), 0) % PAIR // P_SIZE
        == lax.broadcasted_iota(jnp.int32, (2 * PAIR, PAIR), 1) // P_SIZE
    )
    summing = jnp.where(same, 1.0, 0.0).astype(BF16)
    per_part = columns // PAIR

    def vector_work(part, q):
        p = part * per_part + q
        here = slice(q * PAIR, (q + 1) * PAIR)
        slots = [slot_ref[2 * p + i] for i in range(2)]
        growth = columns_of(prep_ref[3, 2 * p : 2 * p + 1, :], prep_ref[3, 2 * p + 1 : 2 * p + 2, :])
        first_end = lane_pair(
            prep_ref[3, 2 * p : 2 * p + 1, BLOCK - 1 : BLOCK],
            prep_ref[3, 2 * p + 1 : 2 * p + 2, BLOCK - 1 : BLOCK],
        )
        arriving = enter_ref[p].astype(F32)
        entering = [arriving, first_end * arriving + fresh_ref[p]]
        for b in range(length // BLOCK):
            rows = slice(b * BLOCK, (b + 1) * BLOCK)
            left = jnp.concatenate([maps[slots[0], rows, :], maps[slots[1], rows, :]], axis=1)
            carried = dot(left, split_pair(entering[b].astype(BF16)))
            y = within[part, rows, here] + carried * growth[rows]
            square = y * y
            high = square.astype(BF16)
            low = (square - high.astype(F32)).astype(BF16)
            mean = dot(jnp.concatenate([high, low], axis=1), summing) * (1.0 / P_SIZE)
            gain = gain_ref[:, p * PAIR : (p + 1) * PAIR]
            normed[part, rows, here] = (y * lax.rsqrt(mean + EPS) * gain).astype(BF16)

    def product(part, q):
        there = slice(q * columns, (q + 1) * columns)
        value = dot(normed[part], weights[part, :, there])
        if part == 0:
            total[:, there] = value
        else:
            total[:, there] += value

    for part in range(parts + 1):
        if part < parts:
            within_copies[part].wait()
        if part > 0:
            weight_copies[part - 1].wait()
        for q in range(per_part):
            if part > 0:
                product(part - 1, q)
            if part < parts:
                vector_work(part, q)

    def rows_for(offset):
        place = lax.rem(place_ref[0] + offset, 4)
        return total[pl.ds(pl.multiple_of(place * share, share), share), :]

    middle = total.shape[1] // 2
    far = rows_for(2).astype(BF16)
    far_left[...] = far[:, :middle]
    far_right[...] = far[:, middle:]
    up_ref[...] = rows_for(1)
    down_ref[...] = rows_for(3)
    own_ref[...] = rows_for(0)


def put_cells(stage, j, value):
    for h in range(2):
        stage[h, pl.ds(j, value.shape[0], stride=ROW), :] = value[:, h * 128 : (h + 1) * 128]


def take_cells(stage, j, count):
    return jnp.concatenate(
        [stage[h, pl.ds(j, count, stride=ROW), :] for h in range(2)], axis=1
    ).astype(BF16)


def fill_stage(stage, rows_ref):
    for h in range(2):
        stage[h] = rows_ref[:, h * 128 : (h + 1) * 128].astype(F32)


def drain_stage(stage, rows_ref):
    for h in range(2):
        rows_ref[:, h * 128 : (h + 1) * 128] = stage[h].astype(BF16)


def tokens_kernel(
    residual_ref,
    own_ref,
    prev_ref,
    next_ref,
    gain_ref,
    router_ref,
    ids_ref,
    stream_ref,
    weight_ref,
    *rest,
    ring,
):
    out_refs, (stage, tokens) = rest[:-2], rest[-2:]
    share, width = stream_ref.shape
    stream = (
        residual_ref[...].astype(F32)
        + own_ref[...]
        + prev_ref[...].astype(F32)
        + next_ref[...].astype(F32)
    )
    stream_ref[...] = stream
    square = jnp.mean(stream * stream, axis=-1, keepdims=True)
    tokens[...] = (stream * lax.rsqrt(square + EPS) * gain_ref[...]).astype(BF16)
    experts = router_ref.shape[1]
    place = lax.broadcasted_iota(jnp.int32, (share, experts), 1)
    hosted = place % ring * (experts // ring) + place // ring
    routed = jnp.zeros((share, experts), F32)
    for k in range(ids_ref.shape[1]):
        routed = routed + jnp.where(ids_ref[:, k : k + 1] == hosted, 1.0, 0.0)
    earlier = jnp.where(
        lax.broadcasted_iota(jnp.int32, (share, share), 0)
        > lax.broadcasted_iota(jnp.int32, (share, share), 1),
        1.0,
        0.0,
    ).astype(BF16)
    rank = dot(earlier, routed.astype(BF16))
    key = jnp.where(routed > 0.5, rank, -1.0).astype(BF16)
    logits = dot(tokens[...], router_ref[...])
    weight = 1.0 / (1.0 + jnp.exp(-logits))
    high = weight.astype(BF16)
    low = (weight - high.astype(F32)).astype(BF16)
    chunk = SLOTS // CHUNKS
    rows = experts * chunk
    spread = jnp.where(
        lax.broadcasted_iota(jnp.int32, (experts, rows), 0)
        == lax.broadcasted_iota(jnp.int32, (experts, rows), 1) // chunk,
        1.0,
        0.0,
    ).astype(BF16)
    wide = dot(jnp.concatenate([key, high, low], axis=0), spread)
    ranks, highs, lows = wide[:share], wide[share : 2 * share], wide[2 * share :]
    slot = (lax.broadcasted_iota(jnp.int32, (share, rows), 1) % chunk).astype(F32)
    for i in range(CHUNKS):
        placed = ranks == slot + float(i * chunk)
        weight_ref[i, :share] = jnp.where(placed, highs, 0.0).astype(BF16)
        weight_ref[i, share:] = jnp.where(placed, lows, 0.0).astype(BF16)
        pick = jnp.where(placed, 1.0, 0.0).T.astype(BF16)
        for j in range(ROW):
            put_cells(stage, j, dot(pick, tokens[:, j * CELL : (j + 1) * CELL]))
        drain_stage(stage, out_refs[i])


def experts_kernel(
    x_ref,
    g0,
    u0,
    d0,
    g1,
    u1,
    d1,
    out_hbm,
    stage,
    rows,
    hidden,
    wide,
    deep,
    out,
    wide_sem,
    deep_sem,
    out_sem,
):
    count, width = rows.shape
    unit = g0.shape[1]
    n_wide, n_deep = wide.shape[0], deep.shape[0]
    wide_step, deep_step = 2 * unit // n_wide, width // n_deep
    halves = [(g0, u0, d0), (g1, u1, d1)]

    def copies(s):
        if s < n_wide:
            half = halves[s * wide_step // unit]
            columns = pl.ds(s * wide_step % unit, wide_step)
            return [
                pltpu.make_async_copy(half[i].at[:, columns], wide.at[s, i], wide_sem.at[s, i])
                for i in range(2)
            ]
        s -= n_wide
        columns = pl.ds(s * deep_step, deep_step)
        return [
            pltpu.make_async_copy(
                halves[i][2].at[:, columns], deep.at[s, pl.ds(i * unit, unit)], deep_sem.at[s, i]
            )
            for i in range(2)
        ]

    total_steps = n_wide + n_deep
    ahead = 3
    for s in range(ahead):
        for copy in copies(s):
            copy.start()
    fill_stage(stage, x_ref)
    for j in range(ROW):
        rows[:, j * CELL : (j + 1) * CELL] = take_cells(stage, j, count)
    for s in range(total_steps):
        if s + ahead < total_steps:
            for copy in copies(s + ahead):
                copy.start()
        for copy in copies(s):
            copy.wait()
        if s < n_wide:
            gated = dot(rows[...], wide[s, 0])
            raised = dot(rows[...], wide[s, 1])
            hidden[:, s * wide_step : (s + 1) * wide_step] = (
                gated / (1.0 + jnp.exp(-gated)) * raised
            ).astype(BF16)
        else:
            d = s - n_wide
            for c in range(deep_step // CELL):
                part = dot(hidden[...], deep[d, :, c * CELL : (c + 1) * CELL])
                put_cells(stage, d * (deep_step // CELL) + c, part)
    drain_stage(stage, out)
    copy = pltpu.make_async_copy(out, out_hbm, out_sem)
    copy.start()
    copy.wait()


def combine_kernel(base_ref, weight_ref, rows_ref, out_ref, stage):
    share = base_ref.shape[0]
    count = weight_ref.shape[1]
    fill_stage(stage, rows_ref)
    for j in range(ROW):
        columns = slice(j * CELL, (j + 1) * CELL)
        part = dot(weight_ref[...], take_cells(stage, j, count))
        out_ref[:, columns] = (base_ref[:, columns] + part[:share] + part[share:]).astype(
            out_ref.dtype
        )


def whole(shape):
    return pl.BlockSpec(shape, lambda s, *_: (0,) * len(shape))


def params(mib=60):
    return pltpu.CompilerParams(
        dimension_semantics=("arbitrary",), vmem_limit_bytes=mib * MIB
    )


def body(
    ssd_input,
    dt_raw,
    dt_bias,
    log_decay,
    input_map,
    output_map,
    head_group,
    d_skip,
    norm_gain,
    w_out,
    residual,
    moe_gain,
    w_router,
    expert_ids,
    w_gate,
    w_up,
    w_down,
):
    length = ssd_input.shape[0]
    heads = dt_raw.shape[1]
    width = w_out.shape[1]
    share = residual.shape[0]
    me = lax.axis_index("exp")
    ring = lax.axis_size("exp")
    seq_count = lax.axis_size("seq")
    nxt = [(i, (i + 1) % ring) for i in range(ring)]
    prv = [(i, (i - 1) % ring) for i in range(ring)]
    partner = [(i, i ^ 1) for i in range(seq_count)]
    steps = heads // (2 * STEP_PAIRS)
    columns = STEP_PAIRS * PAIR

    def from_neighbours(own):
        return lax.ppermute(own, "exp", nxt), lax.ppermute(own, "exp", prv)

    def with_far(own, from_prev, from_next):
        far_a = lax.ppermute(from_prev[0], "exp", nxt)
        far_b = lax.ppermute(from_next[1], "exp", prv)
        return own, from_next, far_a, far_b, from_prev

    input_own = input_map.transpose(1, 2, 0)
    output_own = output_map.transpose(1, 0, 2)
    in_maps = with_far(input_own, *from_neighbours(input_own))
    output_near = from_neighbours(output_own)
    slot = (lax.rem(head_group // 2 - me + ring, ring) * 2 + head_group % 2).astype(jnp.int32)

    other_gate = lax.ppermute(w_gate[0], "seq", partner)
    other_up = lax.ppermute(w_up[0], "seq", partner)
    other_down = lax.ppermute(w_down[0], "seq", partner)

    prep = pl.pallas_call(
        prep_kernel,
        out_shape=jax.ShapeDtypeStruct((4, heads, length), F32),
        compiler_params=pltpu.CompilerParams(vmem_limit_bytes=16 * MIB),
        cost_estimate=pl.CostEstimate(
            flops=30_000_000, bytes_accessed=400_000, transcendentals=100_000
        ),
        name="prep",
    )(dt_raw.T, dt_bias[:, None], log_decay.T)
    skip_lanes = jnp.repeat(d_skip, P_SIZE)[None, :]
    gain_lanes = norm_gain[None, :]

    x_spec = pl.BlockSpec((length, columns), lambda s, *_: (0, s))
    prep_spec = pl.BlockSpec((4, 2 * STEP_PAIRS, length), lambda s, *_: (0, s, 0))
    lane_spec = pl.BlockSpec((1, columns), lambda s, *_: (0, s))
    state_spec = pl.BlockSpec((STEP_PAIRS, NST, PAIR), lambda s, *_: (s, 0, 0))
    in_specs = [whole((2, NST, length))] * 2 + [whole((NST, length))] * 2 + [whole((2, NST, length))]
    out_specs = [whole((2, length, NST))] * 2 + [whole((length, NST))] * 2 + [whole((2, length, NST))]

    fresh, sending = pl.pallas_call(
        states_kernel,
        grid_spec=pltpu.PrefetchScalarGridSpec(
            num_scalar_prefetch=1,
            grid=(steps,),
            in_specs=[x_spec, prep_spec] + in_specs,
            out_specs=[pl.BlockSpec(memory_space=pltpu.HBM)] * 2,
            scratch_shapes=[
                pltpu.VMEM((G, NST, length), BF16),
                pltpu.VMEM((heads // 2, NST, PAIR), F32),
                pltpu.VMEM((heads, 72, PAIR), BF16),
                pltpu.SemaphoreType.DMA((steps,)),
                pltpu.SemaphoreType.DMA((steps,)),
            ],
        ),
        out_shape=[
            jax.ShapeDtypeStruct((heads // 2, NST, PAIR), F32),
            jax.ShapeDtypeStruct((heads, 72, PAIR), BF16),
        ],
        compiler_params=params(16),
        cost_estimate=pl.CostEstimate(
            flops=600_000_000, bytes_accessed=5_000_000, transcendentals=0
        ),
        name="states",
    )(slot, ssd_input, prep, *in_maps)

    output_near, fresh, sending = lax.optimization_barrier((output_near, fresh, sending))
    out_maps = with_far(output_own, *output_near)

    arrived = lax.all_to_all(sending, "seq", split_axis=0, concat_axis=0, tiled=True)
    prefix = pl.pallas_call(
        scan_kernel,
        out_shape=jax.ShapeDtypeStruct((seq_count, 64, PAIR), BF16),
        compiler_params=pltpu.CompilerParams(vmem_limit_bytes=16 * MIB),
        name="scan",
    )(arrived)
    entering = lax.all_to_all(prefix, "seq", split_axis=0, concat_axis=0, tiled=True)
    entering = entering.reshape(heads // 2, NST, PAIR)

    within = pl.pallas_call(
        within_kernel,
        grid_spec=pltpu.PrefetchScalarGridSpec(
            num_scalar_prefetch=1,
            grid=(steps,),
            in_specs=[x_spec, prep_spec, lane_spec] + in_specs + out_specs,
            out_specs=x_spec,
            scratch_shapes=[pltpu.VMEM((G, 2, BLOCK, BLOCK), F32)],
        ),
        out_shape=jax.ShapeDtypeStruct(ssd_input.shape, F32),
        compiler_params=params(),
        cost_estimate=pl.CostEstimate(
            flops=12_000_000_000, bytes_accessed=8_000_000, transcendentals=4_000_000
        ),
        name="within",
    )(slot, ssd_input, prep, skip_lanes, *in_maps, *out_maps)

    middle = width // 2

    parts = width // columns
    half_sent = jax.ShapeDtypeStruct((share, middle), BF16)
    full_wide = jax.ShapeDtypeStruct((share, width), F32)
    vmem = pl.BlockSpec(memory_space=pltpu.VMEM)
    smem = pl.BlockSpec(memory_space=pltpu.SMEM)
    hbm = pl.BlockSpec(memory_space=pl.ANY)
    own, far_left, far_right, up, down = pl.pallas_call(
        project_kernel,
        in_specs=[smem] * 2 + [vmem] * 4 + [hbm] * 7,
        out_specs=[vmem] * 5,
        out_shape=[full_wide, half_sent, half_sent, full_wide, full_wide],
        scratch_shapes=[
            pltpu.VMEM((G, length, NST), BF16),
            pltpu.VMEM((parts, length, columns), F32),
            pltpu.VMEM((parts, length, columns), BF16),
            pltpu.VMEM((parts, columns, width), BF16),
            pltpu.VMEM((length, width), F32),
            pltpu.SemaphoreType.DMA((5,)),
            pltpu.SemaphoreType.DMA((parts,)),
            pltpu.SemaphoreType.DMA((parts,)),
        ],
        compiler_params=pltpu.CompilerParams(vmem_limit_bytes=60 * MIB),
        cost_estimate=pl.CostEstimate(
            flops=6_000_000_000, bytes_accessed=18_000_000, transcendentals=0
        ),
        name="project",
    )(
        slot,
        me[None].astype(jnp.int32),
        prep,
        gain_lanes,
        entering,
        fresh,
        within,
        *out_maps,
        w_out,
    )

    got_left = lax.ppermute(far_left, "exp", nxt)
    got_right = lax.ppermute(far_right, "exp", prv)
    up = jnp.concatenate(
        [up[:, :middle] + got_left.astype(F32), up[:, middle:]], axis=1
    ).astype(BF16)
    down = jnp.concatenate(
        [down[:, :middle], down[:, middle:] + got_right.astype(F32)], axis=1
    ).astype(BF16)
    from_prev = lax.ppermute(up, "exp", nxt)
    from_next = lax.ppermute(down, "exp", prv)

    experts = w_router.shape[1]
    per_group = experts // ring
    router = w_router.reshape(-1, ring, per_group).swapaxes(1, 2).reshape(-1, experts)
    chunk = SLOTS // CHUNKS
    count = experts * chunk
    cells = (count * ROW, CELL)
    stage = (2, count * ROW, CELL // 2)
    stream, weights, *outgoing = pl.pallas_call(
        functools.partial(tokens_kernel, ring=ring),
        out_shape=[
            jax.ShapeDtypeStruct((share, width), F32),
            jax.ShapeDtypeStruct((CHUNKS, 2 * share, count), BF16),
        ]
        + [jax.ShapeDtypeStruct(cells, BF16)] * CHUNKS,
        scratch_shapes=[pltpu.VMEM(stage, F32), pltpu.VMEM((share, width), BF16)],
        compiler_params=pltpu.CompilerParams(vmem_limit_bytes=32 * MIB),
        cost_estimate=pl.CostEstimate(
            flops=1_000_000_000, bytes_accessed=8_000_000, transcendentals=0
        ),
        name="tokens",
    )(residual, own, from_prev, from_next, moe_gain[None, :], router, expert_ids)

    cores = [
        [(c // ring * 2 + h) * ring + c % ring for c in range(experts)] for h in range(2)
    ]

    def swap(rows):
        swapped = lax.all_to_all(
            rows.reshape(count, ROW, CELL),
            ("seq", "exp"),
            split_axis=0,
            concat_axis=0,
            tiled=True,
            axis_index_groups=cores,
        )
        return swapped.reshape(cells)

    unit = w_gate.shape[2]
    run_experts = pl.pallas_call(
        experts_kernel,
        in_specs=[vmem] + [hbm] * 6,
        out_specs=pl.BlockSpec(memory_space=pltpu.HBM),
        out_shape=jax.ShapeDtypeStruct(cells, BF16),
        scratch_shapes=[
            pltpu.VMEM(stage, F32),
            pltpu.VMEM((count, width), BF16),
            pltpu.VMEM((count, 2 * unit), BF16),
            pltpu.VMEM((8, 2, width, unit // 4), BF16),
            pltpu.VMEM((4, 2 * unit, width // 4), BF16),
            pltpu.VMEM(cells, BF16),
            pltpu.SemaphoreType.DMA((8, 2)),
            pltpu.SemaphoreType.DMA((4, 2)),
            pltpu.SemaphoreType.DMA,
        ],
        compiler_params=pltpu.CompilerParams(vmem_limit_bytes=40 * MIB),
        cost_estimate=pl.CostEstimate(
            flops=12 * count * width * unit,
            bytes_accessed=28_000_000,
            transcendentals=0,
        ),
        name="experts",
    )

    def combine(base, weight, rows, dtype):
        return pl.pallas_call(
            combine_kernel,
            out_shape=jax.ShapeDtypeStruct((share, width), dtype),
            scratch_shapes=[pltpu.VMEM(stage, F32)],
            compiler_params=pltpu.CompilerParams(vmem_limit_bytes=24 * MIB),
            cost_estimate=pl.CostEstimate(
                flops=500_000_000, bytes_accessed=4_000_000, transcendentals=0
            ),
            name="combine",
        )(base, weight, rows)

    arrivals = [swap(rows) for rows in outgoing]
    returned = [
        swap(
            run_experts(
                rows, w_gate[0], w_up[0], w_down[0], other_gate, other_up, other_down
            )
        )
        for rows in arrivals
    ]
    mixed = stream
    for i in range(CHUNKS):
        mixed = combine(mixed, weights[i], returned[i], BF16 if i == CHUNKS - 1 else F32)
    return mixed


def solution(mesh):
    return jax.shard_map(
        body,
        mesh=mesh,
        in_specs=(
            P("seq", "exp"),
            P("seq", "exp"),
            P("exp"),
            P("seq", "exp"),
            P("seq", "exp", None),
            P("seq", "exp", None),
            P("exp"),
            P("exp"),
            P("exp"),
            P("exp", None),
            P(("seq", "exp"), None),
            P(),
            P(),
            P(("seq", "exp"), None),
            P(("seq", "exp"), None, None),
            P(("seq", "exp"), None, None),
            P(("seq", "exp"), None, None),
        ),
        out_specs=P(("seq", "exp"), None),
        check_vma=False,
    )
```

```python
import functools

import jax
import jax.numpy as jnp
from jax import lax
from jax.experimental import pallas as pl
from jax.experimental.pallas import tpu as pltpu
from jax.sharding import PartitionSpec as P

P_SIZE = 64
NST = 128
G = 8
BLOCK = 256
PAIR = 2 * P_SIZE
STEP_PAIRS = 4
SLOTS = 14
CHUNKS = 2
ROW = 8
CELL = 256

EPS = 1e-06
F32 = jnp.float32
BF16 = jnp.bfloat16
MIB = 1024 * 1024


def dot(a, b):
    return jnp.dot(a, b, preferred_element_type=F32)


def lanes_of_first(shape):
    return lax.broadcasted_iota(jnp.int32, shape, 1) < P_SIZE


def columns_of(first_row, second_row):
    length = first_row.shape[1]
    rows = jnp.concatenate(
        [
            jnp.broadcast_to(first_row, (P_SIZE, length)),
            jnp.broadcast_to(second_row, (P_SIZE, length)),
        ],
        axis=0,
    )
    return rows.T


def lane_pair(first, second):
    return jnp.concatenate(
        [jnp.broadcast_to(first, (1, P_SIZE)), jnp.broadcast_to(second, (1, P_SIZE))], axis=1
    )


def split_pair(values):
    first = lanes_of_first(values.shape)
    zero = jnp.zeros_like(values)
    return jnp.concatenate([jnp.where(first, values, zero), jnp.where(first, zero, values)], axis=0)


def prep_kernel(raw_ref, bias_ref, decay_ref, out_ref):
    value = raw_ref[...] + bias_ref[...]
    size = jnp.maximum(value, 0.0) + jnp.log(1.0 + jnp.exp(-jnp.abs(value)))
    upto = jnp.where(
        lax.broadcasted_iota(jnp.int32, (BLOCK, BLOCK), 0)
        <= lax.broadcasted_iota(jnp.int32, (BLOCK, BLOCK), 1),
        1.0,
        0.0,
    ).astype(BF16)
    heads, length = size.shape
    for b in range(length // BLOCK):
        rows = slice(b * BLOCK, (b + 1) * BLOCK)
        rest = decay_ref[:, rows]
        terms = []
        for _ in range(3):
            terms.append(rest.astype(BF16))
            rest = rest - terms[-1].astype(F32)
        sums = dot(jnp.concatenate(terms, axis=0), upto)
        running = sums[:heads] + sums[heads : 2 * heads] + sums[2 * heads :]
        out_ref[0, :, rows] = running
        out_ref[1, :, rows] = size[:, rows]
        out_ref[2, :, rows] = jnp.exp(running[:, BLOCK - 1 :] - running) * size[:, rows]
        out_ref[3, :, rows] = jnp.exp(running)


def states_kernel(
    slot_ref,
    x_ref,
    prep_ref,
    m0,
    m1,
    m2,
    m3,
    fresh_hbm,
    send_hbm,
    maps,
    fresh_all,
    send_all,
    fresh_sem,
    send_sem,
):
    step = pl.program_id(0)
    steps = fresh_sem.shape[0]

    def out_copies(at):
        pairs = pl.ds(at * STEP_PAIRS, STEP_PAIRS)
        pieces = pl.ds(at * 2 * STEP_PAIRS, 2 * STEP_PAIRS)
        return [
            pltpu.make_async_copy(send_all.at[pieces], send_hbm.at[pieces], send_sem.at[at]),
            pltpu.make_async_copy(fresh_all.at[pairs], fresh_hbm.at[pairs], fresh_sem.at[at]),
        ]

    @pl.when(step == 0)
    def _():
        maps[0:2] = m0[...]
        maps[2:4] = m1[...]
        maps[4:6] = m2[...]
        maps[6:8] = m3[...]

    for p in range(STEP_PAIRS):
        slots = [slot_ref[step * 2 * STEP_PAIRS + 2 * p + i] for i in range(2)]
        x = x_ref[:, p * PAIR : (p + 1) * PAIR].astype(F32)
        weight = columns_of(prep_ref[2, 2 * p : 2 * p + 1, :], prep_ref[2, 2 * p + 1 : 2 * p + 2, :])
        scaled = (x * weight).astype(BF16)
        fresh = []
        for b in range(2):
            rows = slice(b * BLOCK, (b + 1) * BLOCK)
            both = split_pair(scaled[rows])
            left = jnp.concatenate([maps[slots[0], :, rows], maps[slots[1], :, rows]], axis=1)
            fresh.append(dot(left, both))
        ends = [
            lane_pair(
                prep_ref[3, 2 * p : 2 * p + 1, e - 1 : e],
                prep_ref[3, 2 * p + 1 : 2 * p + 2, e - 1 : e],
            )
            for e in (BLOCK, 2 * BLOCK)
        ]
        fresh_all[step * STEP_PAIRS + p] = fresh[0]
        final = (ends[1] * fresh[0] + fresh[1]).astype(BF16)
        decay = ends[0] * ends[1]
        high = decay.astype(BF16).astype(F32)
        row = lax.broadcasted_iota(jnp.int32, (8, PAIR), 0)
        tail = jnp.where(row == 0, high, jnp.where(row == 1, decay - high, 0.0)).astype(BF16)
        for i in range(2):
            piece = step * 2 * STEP_PAIRS + 2 * p + i
            send_all[piece, 0:64] = final[64 * i : 64 * (i + 1)]
            send_all[piece, 64:72] = tail
    for copy in out_copies(step):
        copy.start()

    @pl.when(step == steps - 1)
    def _():
        for at in range(steps):
            for copy in out_copies(at):
                copy.wait()


def scan_kernel(in_ref, out_ref):
    state = jnp.zeros((64, PAIR), F32)
    for j in range(in_ref.shape[0]):
        out_ref[j] = state.astype(BF16)
        tail = in_ref[j, 64:72].astype(F32)
        decay = tail[0:1] + tail[1:2]
        state = decay * state + in_ref[j, 0:64].astype(F32)


def within_kernel(
    slot_ref, x_ref, prep_ref, skip_ref, i0, i1, i2, i3, o0, o1, o2, o3, out_ref, scores
):
    step = pl.program_id(0)

    @pl.when(step == 0)
    def _():
        inputs = [ref.at[i] for ref in (i0, i1, i2, i3) for i in range(2)]
        outputs = [ref.at[i] for ref in (o0, o1, o2, o3) for i in range(2)]
        for g in range(G):
            for b in range(2):
                rows = slice(b * BLOCK, (b + 1) * BLOCK)
                scores[g, b] = dot(outputs[g][rows, :], inputs[g][:, rows])

    half = BLOCK // 2
    causal = lax.broadcasted_iota(jnp.int32, (half, half), 0) >= lax.broadcasted_iota(
        jnp.int32, (half, half), 1
    )
    for p in range(STEP_PAIRS):
        columns = slice(p * PAIR, (p + 1) * PAIR)
        slots = [slot_ref[step * 2 * STEP_PAIRS + 2 * p + i] for i in range(2)]
        for b in range(2):
            rows = slice(b * BLOCK, (b + 1) * BLOCK)
            x = x_ref[rows, columns]
            early, late = [], []
            for i in range(2):
                running = prep_ref[0, 2 * p + i : 2 * p + i + 1, rows]
                size = prep_ref[1, 2 * p + i : 2 * p + i + 1, rows]
                down = jnp.broadcast_to(running, (half, BLOCK)).T

                def tile(t, s, masked):
                    ts, ss = slice(t * half, (t + 1) * half), slice(s * half, (s + 1) * half)
                    spread = down[ts] - running[:, ss]
                    score = scores[slots[i], b, ts, ss]
                    value = score * jnp.exp(spread) * size[:, ss]
                    return (jnp.where(causal, value, 0.0) if masked else value).astype(BF16)

                early.append(tile(0, 0, True))
                late.append(tile(1, 0, False))
                late.append(tile(1, 1, True))
            both = split_pair(x)
            first = jnp.concatenate([both[0:half], both[BLOCK : BLOCK + half]], axis=0)
            skipped = skip_ref[:, columns] * x.astype(F32)
            top = dot(jnp.concatenate(early, axis=1), first)
            bottom = dot(jnp.concatenate(late, axis=1), both)
            out_ref[b * BLOCK : b * BLOCK + half, columns] = (top + skipped[0:half]).astype(BF16)
            out_ref[b * BLOCK + half : (b + 1) * BLOCK, columns] = (bottom + skipped[half:]).astype(
                BF16
            )


def project_kernel(
    slot_ref,
    place_ref,
    within_ref,
    prep_ref,
    gain_ref,
    enter_ref,
    fresh_ref,
    o0,
    o1,
    o2,
    o3,
    w_ref,
    own_ref,
    far_left,
    far_right,
    up_ref,
    down_ref,
    maps,
    normed,
    total,
):
    step = pl.program_id(0)

    @pl.when(step == 0)
    def _():
        maps[0:2] = o0[...]
        maps[2:4] = o1[...]
        maps[4:6] = o2[...]
        maps[6:8] = o3[...]
        total[...] = jnp.zeros_like(total)

    same = (
        lax.broadcasted_iota(jnp.int32, (2 * PAIR, PAIR), 0) % PAIR // P_SIZE
        == lax.broadcasted_iota(jnp.int32, (2 * PAIR, PAIR), 1) // P_SIZE
    )
    summing = jnp.where(same, 1.0, 0.0).astype(BF16)
    for p in range(STEP_PAIRS):
        columns = slice(p * PAIR, (p + 1) * PAIR)
        slots = [slot_ref[step * 2 * STEP_PAIRS + 2 * p + i] for i in range(2)]
        growth = columns_of(prep_ref[3, 2 * p : 2 * p + 1, :], prep_ref[3, 2 * p + 1 : 2 * p + 2, :])
        first_end = lane_pair(
            prep_ref[3, 2 * p : 2 * p + 1, BLOCK - 1 : BLOCK], prep_ref[3, 2 * p + 1 : 2 * p + 2, BLOCK - 1 : BLOCK]
        )
        arriving = enter_ref[p].astype(F32)
        entering = [arriving, first_end * arriving + fresh_ref[p]]
        for b in range(2):
            rows = slice(b * BLOCK, (b + 1) * BLOCK)
            left = jnp.concatenate([maps[slots[0], rows, :], maps[slots[1], rows, :]], axis=1)
            carried = dot(left, split_pair(entering[b].astype(BF16)))
            y = within_ref[rows, columns].astype(F32) + carried * growth[rows]
            square = y * y
            high = square.astype(BF16)
            low = (square - high.astype(F32)).astype(BF16)
            mean = dot(jnp.concatenate([high, low], axis=1), summing) * (1.0 / P_SIZE)
            normed[rows, columns] = (y * lax.rsqrt(mean + EPS) * gain_ref[:, columns]).astype(BF16)
    total[...] += dot(normed[...], w_ref[...])

    @pl.when(step == pl.num_programs(0) - 1)
    def _():
        share = own_ref.shape[0]

        def rows_for(offset):
            place = lax.rem(place_ref[0] + offset, 4)
            return total[pl.ds(pl.multiple_of(place * share, share), share), :]

        own_ref[...] = rows_for(0)
        up_ref[...] = rows_for(1)
        far = rows_for(2).astype(BF16)
        middle = far.shape[1] // 2
        far_left[...] = far[:, :middle]
        far_right[...] = far[:, middle:]
        down_ref[...] = rows_for(3)


def merge_kernel(up_ref, down_ref, left_ref, right_ref, up_out, down_out):
    middle = left_ref.shape[1]
    up_out[:, :middle] = (up_ref[:, :middle] + left_ref[...].astype(F32)).astype(BF16)
    up_out[:, middle:] = up_ref[:, middle:].astype(BF16)
    down_out[:, :middle] = down_ref[:, :middle].astype(BF16)
    down_out[:, middle:] = (down_ref[:, middle:] + right_ref[...].astype(F32)).astype(BF16)


def put_cells(stage, j, value):
    for h in range(2):
        stage[h, pl.ds(j, value.shape[0], stride=ROW), :] = value[:, h * 128 : (h + 1) * 128]


def take_cells(stage, j, count):
    return jnp.concatenate(
        [stage[h, pl.ds(j, count, stride=ROW), :] for h in range(2)], axis=1
    ).astype(BF16)


def fill_stage(stage, rows_ref):
    for h in range(2):
        stage[h] = rows_ref[:, h * 128 : (h + 1) * 128].astype(F32)


def drain_stage(stage, rows_ref):
    for h in range(2):
        rows_ref[:, h * 128 : (h + 1) * 128] = stage[h].astype(BF16)


def tokens_kernel(
    residual_ref,
    own_ref,
    prev_ref,
    next_ref,
    gain_ref,
    router_ref,
    ids_ref,
    stream_ref,
    weight_ref,
    *rest,
    ring,
):
    out_refs, (stage, tokens) = rest[:-2], rest[-2:]
    share, width = stream_ref.shape
    stream = (
        residual_ref[...].astype(F32)
        + own_ref[...]
        + prev_ref[...].astype(F32)
        + next_ref[...].astype(F32)
    )
    stream_ref[...] = stream
    square = jnp.mean(stream * stream, axis=-1, keepdims=True)
    tokens[...] = (stream * lax.rsqrt(square + EPS) * gain_ref[...]).astype(BF16)
    experts = router_ref.shape[1]
    place = lax.broadcasted_iota(jnp.int32, (share, experts), 1)
    hosted = place % ring * (experts // ring) + place // ring
    routed = jnp.zeros((share, experts), F32)
    for k in range(ids_ref.shape[1]):
        routed = routed + jnp.where(ids_ref[:, k : k + 1] == hosted, 1.0, 0.0)
    earlier = jnp.where(
        lax.broadcasted_iota(jnp.int32, (share, share), 0)
        > lax.broadcasted_iota(jnp.int32, (share, share), 1),
        1.0,
        0.0,
    ).astype(BF16)
    rank = dot(earlier, routed.astype(BF16))
    key = jnp.where(routed > 0.5, rank, -1.0).astype(BF16)
    logits = dot(tokens[...], router_ref[...])
    weight = 1.0 / (1.0 + jnp.exp(-logits))
    high = weight.astype(BF16)
    low = (weight - high.astype(F32)).astype(BF16)
    chunk = SLOTS // CHUNKS
    rows = experts * chunk
    spread = jnp.where(
        lax.broadcasted_iota(jnp.int32, (experts, rows), 0)
        == lax.broadcasted_iota(jnp.int32, (experts, rows), 1) // chunk,
        1.0,
        0.0,
    ).astype(BF16)
    wide = dot(jnp.concatenate([key, high, low], axis=0), spread)
    ranks, highs, lows = wide[:share], wide[share : 2 * share], wide[2 * share :]
    slot = (lax.broadcasted_iota(jnp.int32, (share, rows), 1) % chunk).astype(F32)
    for i in range(CHUNKS):
        placed = ranks == slot + float(i * chunk)
        weight_ref[i, :share] = jnp.where(placed, highs, 0.0).astype(BF16)
        weight_ref[i, share:] = jnp.where(placed, lows, 0.0).astype(BF16)
        pick = jnp.where(placed, 1.0, 0.0).T.astype(BF16)
        for j in range(ROW):
            put_cells(stage, j, dot(pick, tokens[:, j * CELL : (j + 1) * CELL]))
        drain_stage(stage, out_refs[i])


def experts_kernel(
    x_ref,
    g0,
    u0,
    d0,
    g1,
    u1,
    d1,
    out_ref,
    stage,
    rows,
    hidden,
    wide,
    deep,
    wide_sem,
    deep_sem,
):
    count, width = rows.shape
    unit = g0.shape[1]
    n_wide, n_deep = wide.shape[0], deep.shape[0]
    wide_step, deep_step = 2 * unit // n_wide, width // n_deep
    halves = [(g0, u0, d0), (g1, u1, d1)]

    def copies(s):
        if s < n_wide:
            half = halves[s * wide_step // unit]
            columns = pl.ds(s * wide_step % unit, wide_step)
            return [
                pltpu.make_async_copy(half[i].at[:, columns], wide.at[s, i], wide_sem.at[s, i])
                for i in range(2)
            ]
        s -= n_wide
        columns = pl.ds(s * deep_step, deep_step)
        return [
            pltpu.make_async_copy(
                halves[i][2].at[:, columns], deep.at[s, pl.ds(i * unit, unit)], deep_sem.at[s, i]
            )
            for i in range(2)
        ]

    total_steps = n_wide + n_deep
    ahead = 3
    for s in range(ahead):
        for copy in copies(s):
            copy.start()
    fill_stage(stage, x_ref)
    for j in range(ROW):
        rows[:, j * CELL : (j + 1) * CELL] = take_cells(stage, j, count)
    for s in range(total_steps):
        if s + ahead < total_steps:
            for copy in copies(s + ahead):
                copy.start()
        for copy in copies(s):
            copy.wait()
        if s < n_wide:
            gated = dot(rows[...], wide[s, 0])
            raised = dot(rows[...], wide[s, 1])
            hidden[:, s * wide_step : (s + 1) * wide_step] = (
                gated / (1.0 + jnp.exp(-gated)) * raised
            ).astype(BF16)
        else:
            d = s - n_wide
            for c in range(deep_step // CELL):
                part = dot(hidden[...], deep[d, :, c * CELL : (c + 1) * CELL])
                put_cells(stage, d * (deep_step // CELL) + c, part)
    drain_stage(stage, out_ref)


def combine_kernel(base_ref, weight_ref, rows_ref, out_ref, stage):
    share = base_ref.shape[0]
    count = weight_ref.shape[1]
    fill_stage(stage, rows_ref)
    for j in range(ROW):
        columns = slice(j * CELL, (j + 1) * CELL)
        part = dot(weight_ref[...], take_cells(stage, j, count))
        out_ref[:, columns] = (base_ref[:, columns] + part[:share] + part[share:]).astype(
            out_ref.dtype
        )


def whole(shape):
    return pl.BlockSpec(shape, lambda s, *_: (0,) * len(shape))


def params(mib=60):
    return pltpu.CompilerParams(
        dimension_semantics=("arbitrary",), vmem_limit_bytes=mib * MIB
    )


def body(
    ssd_input,
    dt_raw,
    dt_bias,
    log_decay,
    input_map,
    output_map,
    head_group,
    d_skip,
    norm_gain,
    w_out,
    residual,
    moe_gain,
    w_router,
    expert_ids,
    w_gate,
    w_up,
    w_down,
):
    length = ssd_input.shape[0]
    heads = dt_raw.shape[1]
    width = w_out.shape[1]
    share = residual.shape[0]
    me = lax.axis_index("exp")
    ring = lax.axis_size("exp")
    seq_count = lax.axis_size("seq")
    nxt = [(i, (i + 1) % ring) for i in range(ring)]
    prv = [(i, (i - 1) % ring) for i in range(ring)]
    partner = [(i, i ^ 1) for i in range(seq_count)]
    steps = heads // (2 * STEP_PAIRS)
    columns = STEP_PAIRS * PAIR

    opposite = [(i, (i + 2) % ring) for i in range(ring)]

    def gather_maps(own):
        far = lax.ppermute(own, "exp", opposite)
        return own, lax.ppermute(own, "exp", prv), far, lax.ppermute(own, "exp", nxt)

    in_maps = gather_maps(input_map.transpose(1, 2, 0))
    out_maps = gather_maps(output_map.transpose(1, 0, 2))
    slot = (lax.rem(head_group // 2 - me + ring, ring) * 2 + head_group % 2).astype(jnp.int32)

    other_gate = lax.ppermute(w_gate[0], "seq", partner)
    other_up = lax.ppermute(w_up[0], "seq", partner)
    other_down = lax.ppermute(w_down[0], "seq", partner)

    prep = pl.pallas_call(
        prep_kernel,
        out_shape=jax.ShapeDtypeStruct((4, heads, length), F32),
        compiler_params=pltpu.CompilerParams(vmem_limit_bytes=16 * MIB),
        cost_estimate=pl.CostEstimate(
            flops=30_000_000, bytes_accessed=400_000, transcendentals=100_000
        ),
        name="prep",
    )(dt_raw.T, dt_bias[:, None], log_decay.T)
    skip_lanes = jnp.repeat(d_skip, P_SIZE)[None, :]
    gain_lanes = norm_gain[None, :]

    x_spec = pl.BlockSpec((length, columns), lambda s, *_: (0, s))
    prep_spec = pl.BlockSpec((4, 2 * STEP_PAIRS, length), lambda s, *_: (0, s, 0))
    lane_spec = pl.BlockSpec((1, columns), lambda s, *_: (0, s))
    state_spec = pl.BlockSpec((STEP_PAIRS, NST, PAIR), lambda s, *_: (s, 0, 0))
    in_specs = [whole((2, NST, length))] * 4
    out_specs = [whole((2, length, NST))] * 4

    fresh, sending = pl.pallas_call(
        states_kernel,
        grid_spec=pltpu.PrefetchScalarGridSpec(
            num_scalar_prefetch=1,
            grid=(steps,),
            in_specs=[x_spec, prep_spec] + in_specs,
            out_specs=[pl.BlockSpec(memory_space=pltpu.HBM)] * 2,
            scratch_shapes=[
                pltpu.VMEM((G, NST, length), BF16),
                pltpu.VMEM((heads // 2, NST, PAIR), F32),
                pltpu.VMEM((heads, 72, PAIR), BF16),
                pltpu.SemaphoreType.DMA((steps,)),
                pltpu.SemaphoreType.DMA((steps,)),
            ],
        ),
        out_shape=[
            jax.ShapeDtypeStruct((heads // 2, NST, PAIR), F32),
            jax.ShapeDtypeStruct((heads, 72, PAIR), BF16),
        ],
        compiler_params=params(16),
        cost_estimate=pl.CostEstimate(
            flops=600_000_000, bytes_accessed=5_000_000, transcendentals=0
        ),
        name="states",
    )(slot, ssd_input, prep, *in_maps)

    arrived = lax.all_to_all(sending, "seq", split_axis=0, concat_axis=0, tiled=True)
    prefix = pl.pallas_call(
        scan_kernel,
        out_shape=jax.ShapeDtypeStruct((seq_count, 64, PAIR), BF16),
        compiler_params=pltpu.CompilerParams(vmem_limit_bytes=16 * MIB),
        name="scan",
    )(arrived)
    entering = lax.all_to_all(prefix, "seq", split_axis=0, concat_axis=0, tiled=True)
    entering = entering.reshape(heads // 2, NST, PAIR)

    within = pl.pallas_call(
        within_kernel,
        grid_spec=pltpu.PrefetchScalarGridSpec(
            num_scalar_prefetch=1,
            grid=(steps,),
            in_specs=[x_spec, prep_spec, lane_spec] + in_specs + out_specs,
            out_specs=x_spec,
            scratch_shapes=[pltpu.VMEM((G, 2, BLOCK, BLOCK), F32)],
        ),
        out_shape=jax.ShapeDtypeStruct(ssd_input.shape, BF16),
        compiler_params=params(),
        cost_estimate=pl.CostEstimate(
            flops=12_000_000_000, bytes_accessed=8_000_000, transcendentals=4_000_000
        ),
        name="within",
    )(slot, ssd_input, prep, skip_lanes, *in_maps, *out_maps)

    middle = width // 2
    vmem = pl.BlockSpec(memory_space=pltpu.VMEM)
    hbm = pl.BlockSpec(memory_space=pl.ANY)
    half_sent = jax.ShapeDtypeStruct((share, middle), BF16)
    full_sent = jax.ShapeDtypeStruct((share, width), BF16)
    full_wide = jax.ShapeDtypeStruct((share, width), F32)
    own, far_left, far_right, up, down = pl.pallas_call(
        project_kernel,
        grid_spec=pltpu.PrefetchScalarGridSpec(
            num_scalar_prefetch=2,
            grid=(steps,),
            in_specs=[x_spec, prep_spec, lane_spec, state_spec, state_spec]
            + out_specs
            + [pl.BlockSpec((columns, width), lambda s, *_: (s, 0))],
            out_specs=[whole((share, width))]
            + [whole((share, middle))] * 2
            + [whole((share, width))] * 2,
            scratch_shapes=[
                pltpu.VMEM((G, length, NST), BF16),
                pltpu.VMEM((length, columns), BF16),
                pltpu.VMEM((length, width), F32),
            ],
        ),
        out_shape=[full_wide, half_sent, half_sent, full_wide, full_wide],
        compiler_params=params(),
        cost_estimate=pl.CostEstimate(
            flops=6_000_000_000, bytes_accessed=16_000_000, transcendentals=0
        ),
        name="project",
    )(slot, me[None].astype(jnp.int32), within, prep, gain_lanes, entering, fresh, *out_maps, w_out)

    got_left = lax.ppermute(far_left, "exp", nxt)
    got_right = lax.ppermute(far_right, "exp", prv)
    up, down = pl.pallas_call(
        merge_kernel,
        out_shape=[full_sent, full_sent],
        compiler_params=pltpu.CompilerParams(vmem_limit_bytes=16 * MIB),
        cost_estimate=pl.CostEstimate(flops=500_000, bytes_accessed=4_000_000, transcendentals=0),
        name="merge",
    )(up, down, got_left, got_right)
    from_prev = lax.ppermute(up, "exp", nxt)
    from_next = lax.ppermute(down, "exp", prv)

    experts = w_router.shape[1]
    per_group = experts // ring
    router = w_router.reshape(-1, ring, per_group).swapaxes(1, 2).reshape(-1, experts)
    chunk = SLOTS // CHUNKS
    count = experts * chunk
    cells = (count * ROW, CELL)
    stage = (2, count * ROW, CELL // 2)
    stream, weights, *outgoing = pl.pallas_call(
        functools.partial(tokens_kernel, ring=ring),
        out_shape=[
            jax.ShapeDtypeStruct((share, width), F32),
            jax.ShapeDtypeStruct((CHUNKS, 2 * share, count), BF16),
        ]
        + [jax.ShapeDtypeStruct(cells, BF16)] * CHUNKS,
        scratch_shapes=[pltpu.VMEM(stage, F32), pltpu.VMEM((share, width), BF16)],
        compiler_params=pltpu.CompilerParams(vmem_limit_bytes=32 * MIB),
        cost_estimate=pl.CostEstimate(
            flops=1_000_000_000, bytes_accessed=8_000_000, transcendentals=0
        ),
        name="tokens",
    )(residual, own, from_prev, from_next, moe_gain[None, :], router, expert_ids)

    cores = [
        [(c // ring * 2 + h) * ring + c % ring for c in range(experts)] for h in range(2)
    ]

    def swap(rows):
        swapped = lax.all_to_all(
            rows.reshape(count, ROW, CELL),
            ("seq", "exp"),
            split_axis=0,
            concat_axis=0,
            tiled=True,
            axis_index_groups=cores,
        )
        return swapped.reshape(cells)

    unit = w_gate.shape[2]
    run_experts = pl.pallas_call(
        experts_kernel,
        in_specs=[vmem] + [hbm] * 6,
        out_specs=vmem,
        out_shape=jax.ShapeDtypeStruct(cells, BF16),
        scratch_shapes=[
            pltpu.VMEM(stage, F32),
            pltpu.VMEM((count, width), BF16),
            pltpu.VMEM((count, 2 * unit), BF16),
            pltpu.VMEM((8, 2, width, unit // 4), BF16),
            pltpu.VMEM((4, 2 * unit, width // 4), BF16),
            pltpu.SemaphoreType.DMA((8, 2)),
            pltpu.SemaphoreType.DMA((4, 2)),
        ],
        compiler_params=pltpu.CompilerParams(vmem_limit_bytes=59 * MIB),
        cost_estimate=pl.CostEstimate(
            flops=12 * count * width * unit,
            bytes_accessed=28_000_000,
            transcendentals=0,
        ),
        name="experts",
    )

    def combine(base, weight, rows, dtype):
        return pl.pallas_call(
            combine_kernel,
            out_shape=jax.ShapeDtypeStruct((share, width), dtype),
            scratch_shapes=[pltpu.VMEM(stage, F32)],
            compiler_params=pltpu.CompilerParams(vmem_limit_bytes=24 * MIB),
            cost_estimate=pl.CostEstimate(
                flops=500_000_000, bytes_accessed=4_000_000, transcendentals=0
            ),
            name="combine",
        )(base, weight, rows)

    arrivals = [swap(rows) for rows in outgoing]
    returned = [
        swap(
            run_experts(
                rows, w_gate[0], w_up[0], w_down[0], other_gate, other_up, other_down
            )
        )
        for rows in arrivals
    ]
    mixed = stream
    for i in range(CHUNKS):
        mixed = combine(mixed, weights[i], returned[i], BF16 if i == CHUNKS - 1 else F32)
    return mixed


def solution(mesh):
    return jax.shard_map(
        body,
        mesh=mesh,
        in_specs=(
            P("seq", "exp"),
            P("seq", "exp"),
            P("exp"),
            P("seq", "exp"),
            P("seq", "exp", None),
            P("seq", "exp", None),
            P("exp"),
            P("exp"),
            P("exp"),
            P("exp", None),
            P(("seq", "exp"), None),
            P(),
            P(),
            P(("seq", "exp"), None),
            P(("seq", "exp"), None, None),
            P(("seq", "exp"), None, None),
            P(("seq", "exp"), None, None),
        ),
        out_specs=P(("seq", "exp"), None),
        check_vma=False,
    )
```

```python
import functools

import jax
import jax.numpy as jnp
from jax import lax
from jax.experimental import pallas as pl
from jax.experimental.pallas import tpu as pltpu
from jax.sharding import PartitionSpec as P

P_SIZE = 64
NST = 128
G = 8
BLOCK = 256
PAIR = 2 * P_SIZE
STEP_PAIRS = 4
SLOTS = 14
CHUNKS = 2
ROW = 8
CELL = 256

EPS = 1e-06
F32 = jnp.float32
BF16 = jnp.bfloat16
MIB = 1024 * 1024


def dot(a, b):
    return jnp.dot(a, b, preferred_element_type=F32)


def lanes_of_first(shape):
    return lax.broadcasted_iota(jnp.int32, shape, 1) < P_SIZE


def columns_of(first_row, second_row):
    length = first_row.shape[1]
    rows = jnp.concatenate(
        [
            jnp.broadcast_to(first_row, (P_SIZE, length)),
            jnp.broadcast_to(second_row, (P_SIZE, length)),
        ],
        axis=0,
    )
    return rows.T


def lane_pair(first, second):
    return jnp.concatenate(
        [jnp.broadcast_to(first, (1, P_SIZE)), jnp.broadcast_to(second, (1, P_SIZE))], axis=1
    )


def split_pair(values):
    first = lanes_of_first(values.shape)
    zero = jnp.zeros_like(values)
    return jnp.concatenate([jnp.where(first, values, zero), jnp.where(first, zero, values)], axis=0)


def prep_kernel(raw_ref, bias_ref, decay_ref, out_ref):
    value = raw_ref[...] + bias_ref[...]
    size = jnp.maximum(value, 0.0) + jnp.log(1.0 + jnp.exp(-jnp.abs(value)))
    upto = jnp.where(
        lax.broadcasted_iota(jnp.int32, (BLOCK, BLOCK), 0)
        <= lax.broadcasted_iota(jnp.int32, (BLOCK, BLOCK), 1),
        1.0,
        0.0,
    ).astype(BF16)
    heads, length = size.shape
    for b in range(length // BLOCK):
        rows = slice(b * BLOCK, (b + 1) * BLOCK)
        rest = decay_ref[:, rows]
        terms = []
        for _ in range(3):
            terms.append(rest.astype(BF16))
            rest = rest - terms[-1].astype(F32)
        sums = dot(jnp.concatenate(terms, axis=0), upto)
        running = sums[:heads] + sums[heads : 2 * heads] + sums[2 * heads :]
        out_ref[0, :, rows] = running
        out_ref[1, :, rows] = size[:, rows]
        out_ref[2, :, rows] = jnp.exp(running[:, BLOCK - 1 :] - running) * size[:, rows]
        out_ref[3, :, rows] = jnp.exp(running)


def states_kernel(
    slot_ref,
    x_ref,
    prep_ref,
    m0,
    m1,
    m2,
    m3,
    fresh_hbm,
    send_hbm,
    maps,
    fresh_all,
    send_all,
    fresh_sem,
    send_sem,
):
    step = pl.program_id(0)
    steps = fresh_sem.shape[0]

    def out_copies(at):
        pairs = pl.ds(at * STEP_PAIRS, STEP_PAIRS)
        pieces = pl.ds(at * 2 * STEP_PAIRS, 2 * STEP_PAIRS)
        return [
            pltpu.make_async_copy(send_all.at[pieces], send_hbm.at[pieces], send_sem.at[at]),
            pltpu.make_async_copy(fresh_all.at[pairs], fresh_hbm.at[pairs], fresh_sem.at[at]),
        ]

    @pl.when(step == 0)
    def _():
        maps[0:2] = m0[...]
        maps[2:4] = m1[...]
        maps[4:6] = m2[...]
        maps[6:8] = m3[...]

    for p in range(STEP_PAIRS):
        slots = [slot_ref[step * 2 * STEP_PAIRS + 2 * p + i] for i in range(2)]
        x = x_ref[:, p * PAIR : (p + 1) * PAIR].astype(F32)
        weight = columns_of(prep_ref[2, 2 * p : 2 * p + 1, :], prep_ref[2, 2 * p + 1 : 2 * p + 2, :])
        scaled = (x * weight).astype(BF16)
        fresh = []
        for b in range(2):
            rows = slice(b * BLOCK, (b + 1) * BLOCK)
            both = split_pair(scaled[rows])
            left = jnp.concatenate([maps[slots[0], :, rows], maps[slots[1], :, rows]], axis=1)
            fresh.append(dot(left, both))
        ends = [
            lane_pair(
                prep_ref[3, 2 * p : 2 * p + 1, e - 1 : e],
                prep_ref[3, 2 * p + 1 : 2 * p + 2, e - 1 : e],
            )
            for e in (BLOCK, 2 * BLOCK)
        ]
        fresh_all[step * STEP_PAIRS + p] = fresh[0]
        final = (ends[1] * fresh[0] + fresh[1]).astype(BF16)
        decay = ends[0] * ends[1]
        high = decay.astype(BF16).astype(F32)
        row = lax.broadcasted_iota(jnp.int32, (8, PAIR), 0)
        tail = jnp.where(row == 0, high, jnp.where(row == 1, decay - high, 0.0)).astype(BF16)
        for i in range(2):
            piece = step * 2 * STEP_PAIRS + 2 * p + i
            send_all[piece, 0:64] = final[64 * i : 64 * (i + 1)]
            send_all[piece, 64:72] = tail
    for copy in out_copies(step):
        copy.start()

    @pl.when(step == steps - 1)
    def _():
        for at in range(steps):
            for copy in out_copies(at):
                copy.wait()


def scan_kernel(in_ref, out_ref):
    state = jnp.zeros((64, PAIR), F32)
    for j in range(in_ref.shape[0]):
        out_ref[j] = state.astype(BF16)
        tail = in_ref[j, 64:72].astype(F32)
        decay = tail[0:1] + tail[1:2]
        state = decay * state + in_ref[j, 0:64].astype(F32)


def within_kernel(
    slot_ref, x_ref, prep_ref, skip_ref, i0, i1, i2, i3, o0, o1, o2, o3, out_ref, scores
):
    step = pl.program_id(0)

    @pl.when(step == 0)
    def _():
        inputs = [ref.at[i] for ref in (i0, i1, i2, i3) for i in range(2)]
        outputs = [ref.at[i] for ref in (o0, o1, o2, o3) for i in range(2)]
        for g in range(G):
            for b in range(2):
                rows = slice(b * BLOCK, (b + 1) * BLOCK)
                scores[g, b] = dot(outputs[g][rows, :], inputs[g][:, rows])

    half = BLOCK // 2
    causal = lax.broadcasted_iota(jnp.int32, (half, half), 0) >= lax.broadcasted_iota(
        jnp.int32, (half, half), 1
    )
    for p in range(STEP_PAIRS):
        columns = slice(p * PAIR, (p + 1) * PAIR)
        slots = [slot_ref[step * 2 * STEP_PAIRS + 2 * p + i] for i in range(2)]
        for b in range(2):
            rows = slice(b * BLOCK, (b + 1) * BLOCK)
            x = x_ref[rows, columns]
            early, late = [], []
            for i in range(2):
                running = prep_ref[0, 2 * p + i : 2 * p + i + 1, rows]
                size = prep_ref[1, 2 * p + i : 2 * p + i + 1, rows]
                down = jnp.broadcast_to(running, (half, BLOCK)).T

                def tile(t, s, masked):
                    ts, ss = slice(t * half, (t + 1) * half), slice(s * half, (s + 1) * half)
                    spread = down[ts] - running[:, ss]
                    score = scores[slots[i], b, ts, ss]
                    value = score * jnp.exp(spread) * size[:, ss]
                    return (jnp.where(causal, value, 0.0) if masked else value).astype(BF16)

                early.append(tile(0, 0, True))
                late.append(tile(1, 0, False))
                late.append(tile(1, 1, True))
            both = split_pair(x)
            first = jnp.concatenate([both[0:half], both[BLOCK : BLOCK + half]], axis=0)
            skipped = skip_ref[:, columns] * x.astype(F32)
            top = dot(jnp.concatenate(early, axis=1), first)
            bottom = dot(jnp.concatenate(late, axis=1), both)
            out_ref[b * BLOCK : b * BLOCK + half, columns] = (top + skipped[0:half]).astype(BF16)
            out_ref[b * BLOCK + half : (b + 1) * BLOCK, columns] = (bottom + skipped[half:]).astype(
                BF16
            )


def project_kernel(
    slot_ref,
    place_ref,
    within_ref,
    prep_ref,
    gain_ref,
    enter_ref,
    fresh_ref,
    o0,
    o1,
    o2,
    o3,
    w_ref,
    own_ref,
    up_ref,
    far_ref,
    down_ref,
    maps,
    normed,
    total,
):
    step = pl.program_id(0)

    @pl.when(step == 0)
    def _():
        maps[0:2] = o0[...]
        maps[2:4] = o1[...]
        maps[4:6] = o2[...]
        maps[6:8] = o3[...]
        total[...] = jnp.zeros_like(total)

    same = (
        lax.broadcasted_iota(jnp.int32, (2 * PAIR, PAIR), 0) % PAIR // P_SIZE
        == lax.broadcasted_iota(jnp.int32, (2 * PAIR, PAIR), 1) // P_SIZE
    )
    summing = jnp.where(same, 1.0, 0.0).astype(BF16)
    for p in range(STEP_PAIRS):
        columns = slice(p * PAIR, (p + 1) * PAIR)
        slots = [slot_ref[step * 2 * STEP_PAIRS + 2 * p + i] for i in range(2)]
        growth = columns_of(prep_ref[3, 2 * p : 2 * p + 1, :], prep_ref[3, 2 * p + 1 : 2 * p + 2, :])
        first_end = lane_pair(
            prep_ref[3, 2 * p : 2 * p + 1, BLOCK - 1 : BLOCK], prep_ref[3, 2 * p + 1 : 2 * p + 2, BLOCK - 1 : BLOCK]
        )
        arriving = enter_ref[p].astype(F32)
        entering = [arriving, first_end * arriving + fresh_ref[p]]
        for b in range(2):
            rows = slice(b * BLOCK, (b + 1) * BLOCK)
            left = jnp.concatenate([maps[slots[0], rows, :], maps[slots[1], rows, :]], axis=1)
            carried = dot(left, split_pair(entering[b].astype(BF16)))
            y = within_ref[rows, columns].astype(F32) + carried * growth[rows]
            square = y * y
            high = square.astype(BF16)
            low = (square - high.astype(F32)).astype(BF16)
            mean = dot(jnp.concatenate([high, low], axis=1), summing) * (1.0 / P_SIZE)
            normed[rows, columns] = (y * lax.rsqrt(mean + EPS) * gain_ref[:, columns]).astype(BF16)
    total[...] += dot(normed[...], w_ref[...])

    @pl.when(step == pl.num_programs(0) - 1)
    def _():
        share = own_ref.shape[0]

        def rows_for(offset):
            place = lax.rem(place_ref[0] + offset, 4)
            rows = total[pl.ds(pl.multiple_of(place * share, share), share), :]
            return rows.astype(BF16)

        own_ref[...] = rows_for(0)
        up_ref[...] = rows_for(1)
        far_ref[...] = rows_for(2)
        down_ref[...] = rows_for(3)


def put_cells(stage, j, value):
    for h in range(2):
        stage[h, pl.ds(j, value.shape[0], stride=ROW), :] = value[:, h * 128 : (h + 1) * 128]


def take_cells(stage, j, count):
    return jnp.concatenate(
        [stage[h, pl.ds(j, count, stride=ROW), :] for h in range(2)], axis=1
    ).astype(BF16)


def fill_stage(stage, rows_ref):
    for h in range(2):
        stage[h] = rows_ref[:, h * 128 : (h + 1) * 128].astype(F32)


def drain_stage(stage, rows_ref):
    for h in range(2):
        rows_ref[:, h * 128 : (h + 1) * 128] = stage[h].astype(BF16)


def tokens_kernel(
    residual_ref,
    own_ref,
    prev_ref,
    far_ref,
    next_ref,
    gain_ref,
    router_ref,
    ids_ref,
    stream_ref,
    weight_ref,
    *rest,
    ring,
):
    out_refs, (stage, tokens) = rest[:-2], rest[-2:]
    share, width = stream_ref.shape
    stream = (
        residual_ref[...].astype(F32)
        + own_ref[...].astype(F32)
        + prev_ref[...].astype(F32)
        + far_ref[...].astype(F32)
        + next_ref[...].astype(F32)
    )
    stream_ref[...] = stream
    square = jnp.mean(stream * stream, axis=-1, keepdims=True)
    tokens[...] = (stream * lax.rsqrt(square + EPS) * gain_ref[...]).astype(BF16)
    experts = router_ref.shape[1]
    place = lax.broadcasted_iota(jnp.int32, (share, experts), 1)
    hosted = place % ring * (experts // ring) + place // ring
    routed = jnp.zeros((share, experts), F32)
    for k in range(ids_ref.shape[1]):
        routed = routed + jnp.where(ids_ref[:, k : k + 1] == hosted, 1.0, 0.0)
    earlier = jnp.where(
        lax.broadcasted_iota(jnp.int32, (share, share), 0)
        > lax.broadcasted_iota(jnp.int32, (share, share), 1),
        1.0,
        0.0,
    ).astype(BF16)
    rank = dot(earlier, routed.astype(BF16))
    key = jnp.where(routed > 0.5, rank, -1.0).astype(BF16)
    logits = dot(tokens[...], router_ref[...])
    weight = 1.0 / (1.0 + jnp.exp(-logits))
    high = weight.astype(BF16)
    low = (weight - high.astype(F32)).astype(BF16)
    chunk = SLOTS // CHUNKS
    rows = experts * chunk
    spread = jnp.where(
        lax.broadcasted_iota(jnp.int32, (experts, rows), 0)
        == lax.broadcasted_iota(jnp.int32, (experts, rows), 1) // chunk,
        1.0,
        0.0,
    ).astype(BF16)
    wide = dot(jnp.concatenate([key, high, low], axis=0), spread)
    ranks, highs, lows = wide[:share], wide[share : 2 * share], wide[2 * share :]
    slot = (lax.broadcasted_iota(jnp.int32, (share, rows), 1) % chunk).astype(F32)
    for i in range(CHUNKS):
        placed = ranks == slot + float(i * chunk)
        weight_ref[i, :share] = jnp.where(placed, highs, 0.0).astype(BF16)
        weight_ref[i, share:] = jnp.where(placed, lows, 0.0).astype(BF16)
        pick = jnp.where(placed, 1.0, 0.0).T.astype(BF16)
        for j in range(ROW):
            put_cells(stage, j, dot(pick, tokens[:, j * CELL : (j + 1) * CELL]))
        drain_stage(stage, out_refs[i])


def experts_kernel(
    x_ref,
    g0,
    u0,
    d0,
    g1,
    u1,
    d1,
    out_ref,
    stage,
    rows,
    hidden,
    wide,
    deep,
    wide_sem,
    deep_sem,
):
    count, width = rows.shape
    unit = g0.shape[1]
    n_wide, n_deep = wide.shape[0], deep.shape[0]
    wide_step, deep_step = 2 * unit // n_wide, width // n_deep
    halves = [(g0, u0, d0), (g1, u1, d1)]

    def copies(s):
        if s < n_wide:
            half = halves[s * wide_step // unit]
            columns = pl.ds(s * wide_step % unit, wide_step)
            return [
                pltpu.make_async_copy(half[i].at[:, columns], wide.at[s, i], wide_sem.at[s, i])
                for i in range(2)
            ]
        s -= n_wide
        columns = pl.ds(s * deep_step, deep_step)
        return [
            pltpu.make_async_copy(
                halves[i][2].at[:, columns], deep.at[s, pl.ds(i * unit, unit)], deep_sem.at[s, i]
            )
            for i in range(2)
        ]

    total_steps = n_wide + n_deep
    ahead = 3
    for s in range(ahead):
        for copy in copies(s):
            copy.start()
    fill_stage(stage, x_ref)
    for j in range(ROW):
        rows[:, j * CELL : (j + 1) * CELL] = take_cells(stage, j, count)
    for s in range(total_steps):
        if s + ahead < total_steps:
            for copy in copies(s + ahead):
                copy.start()
        for copy in copies(s):
            copy.wait()
        if s < n_wide:
            gated = dot(rows[...], wide[s, 0])
            raised = dot(rows[...], wide[s, 1])
            hidden[:, s * wide_step : (s + 1) * wide_step] = (
                gated / (1.0 + jnp.exp(-gated)) * raised
            ).astype(BF16)
        else:
            d = s - n_wide
            for c in range(deep_step // CELL):
                part = dot(hidden[...], deep[d, :, c * CELL : (c + 1) * CELL])
                put_cells(stage, d * (deep_step // CELL) + c, part)
    drain_stage(stage, out_ref)


def combine_kernel(base_ref, weight_ref, rows_ref, out_ref, stage):
    share = base_ref.shape[0]
    count = weight_ref.shape[1]
    fill_stage(stage, rows_ref)
    for j in range(ROW):
        columns = slice(j * CELL, (j + 1) * CELL)
        part = dot(weight_ref[...], take_cells(stage, j, count))
        out_ref[:, columns] = (base_ref[:, columns] + part[:share] + part[share:]).astype(
            out_ref.dtype
        )


def whole(shape):
    return pl.BlockSpec(shape, lambda s, *_: (0,) * len(shape))


def params(mib=60):
    return pltpu.CompilerParams(
        dimension_semantics=("arbitrary",), vmem_limit_bytes=mib * MIB
    )


def body(
    ssd_input,
    dt_raw,
    dt_bias,
    log_decay,
    input_map,
    output_map,
    head_group,
    d_skip,
    norm_gain,
    w_out,
    residual,
    moe_gain,
    w_router,
    expert_ids,
    w_gate,
    w_up,
    w_down,
):
    length = ssd_input.shape[0]
    heads = dt_raw.shape[1]
    width = w_out.shape[1]
    share = residual.shape[0]
    me = lax.axis_index("exp")
    ring = lax.axis_size("exp")
    seq_count = lax.axis_size("seq")
    nxt = [(i, (i + 1) % ring) for i in range(ring)]
    prv = [(i, (i - 1) % ring) for i in range(ring)]
    partner = [(i, i ^ 1) for i in range(seq_count)]
    steps = heads // (2 * STEP_PAIRS)
    columns = STEP_PAIRS * PAIR

    opposite = [(i, (i + 2) % ring) for i in range(ring)]

    def gather_maps(own):
        far = lax.ppermute(own, "exp", opposite)
        return own, lax.ppermute(own, "exp", prv), far, lax.ppermute(own, "exp", nxt)

    in_maps = gather_maps(input_map.transpose(1, 2, 0))
    out_maps = gather_maps(output_map.transpose(1, 0, 2))
    slot = (lax.rem(head_group // 2 - me + ring, ring) * 2 + head_group % 2).astype(jnp.int32)

    other_gate = lax.ppermute(w_gate[0], "seq", partner)
    other_up = lax.ppermute(w_up[0], "seq", partner)
    other_down = lax.ppermute(w_down[0], "seq", partner)

    prep = pl.pallas_call(
        prep_kernel,
        out_shape=jax.ShapeDtypeStruct((4, heads, length), F32),
        compiler_params=pltpu.CompilerParams(vmem_limit_bytes=16 * MIB),
        cost_estimate=pl.CostEstimate(
            flops=30_000_000, bytes_accessed=400_000, transcendentals=100_000
        ),
        name="prep",
    )(dt_raw.T, dt_bias[:, None], log_decay.T)
    skip_lanes = jnp.repeat(d_skip, P_SIZE)[None, :]
    gain_lanes = norm_gain[None, :]

    x_spec = pl.BlockSpec((length, columns), lambda s, *_: (0, s))
    prep_spec = pl.BlockSpec((4, 2 * STEP_PAIRS, length), lambda s, *_: (0, s, 0))
    lane_spec = pl.BlockSpec((1, columns), lambda s, *_: (0, s))
    state_spec = pl.BlockSpec((STEP_PAIRS, NST, PAIR), lambda s, *_: (s, 0, 0))
    in_specs = [whole((2, NST, length))] * 4
    out_specs = [whole((2, length, NST))] * 4

    fresh, sending = pl.pallas_call(
        states_kernel,
        grid_spec=pltpu.PrefetchScalarGridSpec(
            num_scalar_prefetch=1,
            grid=(steps,),
            in_specs=[x_spec, prep_spec] + in_specs,
            out_specs=[pl.BlockSpec(memory_space=pltpu.HBM)] * 2,
            scratch_shapes=[
                pltpu.VMEM((G, NST, length), BF16),
                pltpu.VMEM((heads // 2, NST, PAIR), F32),
                pltpu.VMEM((heads, 72, PAIR), BF16),
                pltpu.SemaphoreType.DMA((steps,)),
                pltpu.SemaphoreType.DMA((steps,)),
            ],
        ),
        out_shape=[
            jax.ShapeDtypeStruct((heads // 2, NST, PAIR), F32),
            jax.ShapeDtypeStruct((heads, 72, PAIR), BF16),
        ],
        compiler_params=params(16),
        cost_estimate=pl.CostEstimate(
            flops=600_000_000, bytes_accessed=5_000_000, transcendentals=0
        ),
        name="states",
    )(slot, ssd_input, prep, *in_maps)

    arrived = lax.all_to_all(sending, "seq", split_axis=0, concat_axis=0, tiled=True)
    prefix = pl.pallas_call(
        scan_kernel,
        out_shape=jax.ShapeDtypeStruct((seq_count, 64, PAIR), BF16),
        compiler_params=pltpu.CompilerParams(vmem_limit_bytes=16 * MIB),
        name="scan",
    )(arrived)
    entering = lax.all_to_all(prefix, "seq", split_axis=0, concat_axis=0, tiled=True)
    entering = entering.reshape(heads // 2, NST, PAIR)

    within = pl.pallas_call(
        within_kernel,
        grid_spec=pltpu.PrefetchScalarGridSpec(
            num_scalar_prefetch=1,
            grid=(steps,),
            in_specs=[x_spec, prep_spec, lane_spec] + in_specs + out_specs,
            out_specs=x_spec,
            scratch_shapes=[pltpu.VMEM((G, 2, BLOCK, BLOCK), F32)],
        ),
        out_shape=jax.ShapeDtypeStruct(ssd_input.shape, BF16),
        compiler_params=params(),
        cost_estimate=pl.CostEstimate(
            flops=12_000_000_000, bytes_accessed=8_000_000, transcendentals=4_000_000
        ),
        name="within",
    )(slot, ssd_input, prep, skip_lanes, *in_maps, *out_maps)

    vmem = pl.BlockSpec(memory_space=pltpu.VMEM)
    hbm = pl.BlockSpec(memory_space=pl.ANY)
    own, up, far, down = pl.pallas_call(
        project_kernel,
        grid_spec=pltpu.PrefetchScalarGridSpec(
            num_scalar_prefetch=2,
            grid=(steps,),
            in_specs=[x_spec, prep_spec, lane_spec, state_spec, state_spec]
            + out_specs
            + [pl.BlockSpec((columns, width), lambda s, *_: (s, 0))],
            out_specs=[whole((share, width))] * 4,
            scratch_shapes=[
                pltpu.VMEM((G, length, NST), BF16),
                pltpu.VMEM((length, columns), BF16),
                pltpu.VMEM((length, width), F32),
            ],
        ),
        out_shape=[jax.ShapeDtypeStruct((share, width), BF16)] * 4,
        compiler_params=params(),
        cost_estimate=pl.CostEstimate(
            flops=6_000_000_000, bytes_accessed=16_000_000, transcendentals=0
        ),
        name="project",
    )(slot, me[None].astype(jnp.int32), within, prep, gain_lanes, entering, fresh, *out_maps, w_out)

    from_prev = lax.ppermute(up, "exp", nxt)
    from_far = lax.ppermute(far, "exp", opposite)
    from_next = lax.ppermute(down, "exp", prv)

    experts = w_router.shape[1]
    per_group = experts // ring
    router = w_router.reshape(-1, ring, per_group).swapaxes(1, 2).reshape(-1, experts)
    chunk = SLOTS // CHUNKS
    count = experts * chunk
    cells = (count * ROW, CELL)
    stage = (2, count * ROW, CELL // 2)
    stream, weights, *outgoing = pl.pallas_call(
        functools.partial(tokens_kernel, ring=ring),
        out_shape=[
            jax.ShapeDtypeStruct((share, width), F32),
            jax.ShapeDtypeStruct((CHUNKS, 2 * share, count), BF16),
        ]
        + [jax.ShapeDtypeStruct(cells, BF16)] * CHUNKS,
        scratch_shapes=[pltpu.VMEM(stage, F32), pltpu.VMEM((share, width), BF16)],
        compiler_params=pltpu.CompilerParams(vmem_limit_bytes=32 * MIB),
        cost_estimate=pl.CostEstimate(
            flops=1_000_000_000, bytes_accessed=8_000_000, transcendentals=0
        ),
        name="tokens",
    )(residual, own, from_prev, from_far, from_next, moe_gain[None, :], router, expert_ids)

    cores = [
        [(c // ring * 2 + h) * ring + c % ring for c in range(experts)] for h in range(2)
    ]

    def swap(rows):
        swapped = lax.all_to_all(
            rows.reshape(count, ROW, CELL),
            ("seq", "exp"),
            split_axis=0,
            concat_axis=0,
            tiled=True,
            axis_index_groups=cores,
        )
        return swapped.reshape(cells)

    unit = w_gate.shape[2]
    run_experts = pl.pallas_call(
        experts_kernel,
        in_specs=[vmem] + [hbm] * 6,
        out_specs=vmem,
        out_shape=jax.ShapeDtypeStruct(cells, BF16),
        scratch_shapes=[
            pltpu.VMEM(stage, F32),
            pltpu.VMEM((count, width), BF16),
            pltpu.VMEM((count, 2 * unit), BF16),
            pltpu.VMEM((8, 2, width, unit // 4), BF16),
            pltpu.VMEM((4, 2 * unit, width // 4), BF16),
            pltpu.SemaphoreType.DMA((8, 2)),
            pltpu.SemaphoreType.DMA((4, 2)),
        ],
        compiler_params=pltpu.CompilerParams(vmem_limit_bytes=60 * MIB),
        cost_estimate=pl.CostEstimate(
            flops=12 * count * width * unit,
            bytes_accessed=28_000_000,
            transcendentals=0,
        ),
        name="experts",
    )

    def combine(base, weight, rows, dtype):
        return pl.pallas_call(
            combine_kernel,
            out_shape=jax.ShapeDtypeStruct((share, width), dtype),
            scratch_shapes=[pltpu.VMEM(stage, F32)],
            compiler_params=pltpu.CompilerParams(vmem_limit_bytes=24 * MIB),
            cost_estimate=pl.CostEstimate(
                flops=500_000_000, bytes_accessed=4_000_000, transcendentals=0
            ),
            name="combine",
        )(base, weight, rows)

    arrivals = [swap(rows) for rows in outgoing]
    returned = [
        swap(
            run_experts(
                rows, w_gate[0], w_up[0], w_down[0], other_gate, other_up, other_down
            )
        )
        for rows in arrivals
    ]
    mixed = stream
    for i in range(CHUNKS):
        mixed = combine(mixed, weights[i], returned[i], BF16 if i == CHUNKS - 1 else F32)
    return mixed


def solution(mesh):
    return jax.shard_map(
        body,
        mesh=mesh,
        in_specs=(
            P("seq", "exp"),
            P("seq", "exp"),
            P("exp"),
            P("seq", "exp"),
            P("seq", "exp", None),
            P("seq", "exp", None),
            P("exp"),
            P("exp"),
            P("exp"),
            P("exp", None),
            P(("seq", "exp"), None),
            P(),
            P(),
            P(("seq", "exp"), None),
            P(("seq", "exp"), None, None),
            P(("seq", "exp"), None, None),
            P(("seq", "exp"), None, None),
        ),
        out_specs=P(("seq", "exp"), None),
        check_vma=False,
    )
```

```python
import functools

import jax
import jax.numpy as jnp
from jax import lax
from jax.experimental import pallas as pl
from jax.experimental.pallas import tpu as pltpu
from jax.sharding import PartitionSpec as P

P_SIZE = 64
NST = 128
G = 8
BLOCK = 256
PAIR = 2 * P_SIZE
STEP_PAIRS = 4
SLOTS = 14
CHUNKS = 2
ROW = 8
CELL = 256

EPS = 1e-06
F32 = jnp.float32
BF16 = jnp.bfloat16
MIB = 1024 * 1024


def dot(a, b):
    return jnp.dot(a, b, preferred_element_type=F32)


def lanes_of_first(shape):
    return lax.broadcasted_iota(jnp.int32, shape, 1) < P_SIZE


def columns_of(first_row, second_row):
    length = first_row.shape[1]
    rows = jnp.concatenate(
        [
            jnp.broadcast_to(first_row, (P_SIZE, length)),
            jnp.broadcast_to(second_row, (P_SIZE, length)),
        ],
        axis=0,
    )
    return rows.T


def lane_pair(first, second):
    return jnp.concatenate(
        [jnp.broadcast_to(first, (1, P_SIZE)), jnp.broadcast_to(second, (1, P_SIZE))], axis=1
    )


def split_pair(values):
    first = lanes_of_first(values.shape)
    zero = jnp.zeros_like(values)
    return jnp.concatenate([jnp.where(first, values, zero), jnp.where(first, zero, values)], axis=0)


def prep_kernel(raw_ref, bias_ref, decay_ref, out_ref):
    value = raw_ref[...] + bias_ref[...]
    size = jnp.maximum(value, 0.0) + jnp.log(1.0 + jnp.exp(-jnp.abs(value)))
    upto = jnp.where(
        lax.broadcasted_iota(jnp.int32, (BLOCK, BLOCK), 0)
        <= lax.broadcasted_iota(jnp.int32, (BLOCK, BLOCK), 1),
        1.0,
        0.0,
    ).astype(BF16)
    heads, length = size.shape
    for b in range(length // BLOCK):
        rows = slice(b * BLOCK, (b + 1) * BLOCK)
        rest = decay_ref[:, rows]
        terms = []
        for _ in range(3):
            terms.append(rest.astype(BF16))
            rest = rest - terms[-1].astype(F32)
        sums = dot(jnp.concatenate(terms, axis=0), upto)
        running = sums[:heads] + sums[heads : 2 * heads] + sums[2 * heads :]
        out_ref[0, :, rows] = running
        out_ref[1, :, rows] = size[:, rows]
        out_ref[2, :, rows] = jnp.exp(running[:, BLOCK - 1 :] - running) * size[:, rows]
        out_ref[3, :, rows] = jnp.exp(running)


def states_kernel(
    slot_ref,
    x_ref,
    prep_ref,
    m0,
    m1,
    m2,
    m3,
    fresh_hbm,
    send_hbm,
    maps,
    fresh_all,
    send_all,
    fresh_sem,
    send_sem,
):
    step = pl.program_id(0)
    steps = fresh_sem.shape[0]

    def out_copies(at):
        pairs = pl.ds(at * STEP_PAIRS, STEP_PAIRS)
        pieces = pl.ds(at * 2 * STEP_PAIRS, 2 * STEP_PAIRS)
        return [
            pltpu.make_async_copy(send_all.at[pieces], send_hbm.at[pieces], send_sem.at[at]),
            pltpu.make_async_copy(fresh_all.at[pairs], fresh_hbm.at[pairs], fresh_sem.at[at]),
        ]

    @pl.when(step == 0)
    def _():
        maps[0:2] = m0[...]
        maps[2:4] = m1[...]
        maps[4:6] = m2[...]
        maps[6:8] = m3[...]

    for p in range(STEP_PAIRS):
        slots = [slot_ref[step * 2 * STEP_PAIRS + 2 * p + i] for i in range(2)]
        x = x_ref[:, p * PAIR : (p + 1) * PAIR].astype(F32)
        weight = columns_of(prep_ref[2, 2 * p : 2 * p + 1, :], prep_ref[2, 2 * p + 1 : 2 * p + 2, :])
        scaled = (x * weight).astype(BF16)
        fresh = []
        for b in range(2):
            rows = slice(b * BLOCK, (b + 1) * BLOCK)
            both = split_pair(scaled[rows])
            left = jnp.concatenate([maps[slots[0], :, rows], maps[slots[1], :, rows]], axis=1)
            fresh.append(dot(left, both))
        ends = [
            lane_pair(
                prep_ref[3, 2 * p : 2 * p + 1, e - 1 : e],
                prep_ref[3, 2 * p + 1 : 2 * p + 2, e - 1 : e],
            )
            for e in (BLOCK, 2 * BLOCK)
        ]
        fresh_all[step * STEP_PAIRS + p] = fresh[0]
        final = (ends[1] * fresh[0] + fresh[1]).astype(BF16)
        decay = ends[0] * ends[1]
        high = decay.astype(BF16).astype(F32)
        row = lax.broadcasted_iota(jnp.int32, (8, PAIR), 0)
        tail = jnp.where(row == 0, high, jnp.where(row == 1, decay - high, 0.0)).astype(BF16)
        for i in range(2):
            piece = step * 2 * STEP_PAIRS + 2 * p + i
            send_all[piece, 0:64] = final[64 * i : 64 * (i + 1)]
            send_all[piece, 64:72] = tail
    for copy in out_copies(step):
        copy.start()

    @pl.when(step == steps - 1)
    def _():
        for at in range(steps):
            for copy in out_copies(at):
                copy.wait()


def scan_kernel(in_ref, out_ref):
    state = jnp.zeros((64, PAIR), F32)
    for j in range(in_ref.shape[0]):
        out_ref[j] = state.astype(BF16)
        tail = in_ref[j, 64:72].astype(F32)
        decay = tail[0:1] + tail[1:2]
        state = decay * state + in_ref[j, 0:64].astype(F32)


def within_kernel(
    slot_ref, x_ref, prep_ref, skip_ref, i0, i1, i2, i3, o0, o1, o2, o3, out_ref, scores
):
    step = pl.program_id(0)

    @pl.when(step == 0)
    def _():
        inputs = [ref.at[i] for ref in (i0, i1, i2, i3) for i in range(2)]
        outputs = [ref.at[i] for ref in (o0, o1, o2, o3) for i in range(2)]
        for g in range(G):
            for b in range(2):
                rows = slice(b * BLOCK, (b + 1) * BLOCK)
                scores[g, b] = dot(outputs[g][rows, :], inputs[g][:, rows])

    half = BLOCK // 2
    causal = lax.broadcasted_iota(jnp.int32, (half, half), 0) >= lax.broadcasted_iota(
        jnp.int32, (half, half), 1
    )
    for p in range(STEP_PAIRS):
        columns = slice(p * PAIR, (p + 1) * PAIR)
        slots = [slot_ref[step * 2 * STEP_PAIRS + 2 * p + i] for i in range(2)]
        for b in range(2):
            rows = slice(b * BLOCK, (b + 1) * BLOCK)
            x = x_ref[rows, columns]
            early, late = [], []
            for i in range(2):
                running = prep_ref[0, 2 * p + i : 2 * p + i + 1, rows]
                size = prep_ref[1, 2 * p + i : 2 * p + i + 1, rows]
                down = jnp.broadcast_to(running, (half, BLOCK)).T

                def tile(t, s, masked):
                    ts, ss = slice(t * half, (t + 1) * half), slice(s * half, (s + 1) * half)
                    spread = down[ts] - running[:, ss]
                    score = scores[slots[i], b, ts, ss]
                    value = score * jnp.exp(spread) * size[:, ss]
                    return (jnp.where(causal, value, 0.0) if masked else value).astype(BF16)

                early.append(tile(0, 0, True))
                late.append(tile(1, 0, False))
                late.append(tile(1, 1, True))
            both = split_pair(x)
            first = jnp.concatenate([both[0:half], both[BLOCK : BLOCK + half]], axis=0)
            skipped = skip_ref[:, columns] * x.astype(F32)
            top = dot(jnp.concatenate(early, axis=1), first)
            bottom = dot(jnp.concatenate(late, axis=1), both)
            out_ref[b * BLOCK : b * BLOCK + half, columns] = (top + skipped[0:half]).astype(BF16)
            out_ref[b * BLOCK + half : (b + 1) * BLOCK, columns] = (bottom + skipped[half:]).astype(
                BF16
            )


def project_kernel(
    slot_ref,
    place_ref,
    within_ref,
    prep_ref,
    gain_ref,
    enter_ref,
    fresh_ref,
    o0,
    o1,
    o2,
    o3,
    w_ref,
    own_ref,
    up_ref,
    far_ref,
    down_ref,
    maps,
    normed,
    total,
):
    step = pl.program_id(0)

    @pl.when(step == 0)
    def _():
        maps[0:2] = o0[...]
        maps[2:4] = o1[...]
        maps[4:6] = o2[...]
        maps[6:8] = o3[...]
        total[...] = jnp.zeros_like(total)

    same = (
        lax.broadcasted_iota(jnp.int32, (2 * PAIR, PAIR), 0) % PAIR // P_SIZE
        == lax.broadcasted_iota(jnp.int32, (2 * PAIR, PAIR), 1) // P_SIZE
    )
    summing = jnp.where(same, 1.0, 0.0).astype(BF16)
    for p in range(STEP_PAIRS):
        columns = slice(p * PAIR, (p + 1) * PAIR)
        slots = [slot_ref[step * 2 * STEP_PAIRS + 2 * p + i] for i in range(2)]
        growth = columns_of(prep_ref[3, 2 * p : 2 * p + 1, :], prep_ref[3, 2 * p + 1 : 2 * p + 2, :])
        first_end = lane_pair(
            prep_ref[3, 2 * p : 2 * p + 1, BLOCK - 1 : BLOCK], prep_ref[3, 2 * p + 1 : 2 * p + 2, BLOCK - 1 : BLOCK]
        )
        arriving = enter_ref[p].astype(F32)
        entering = [arriving, first_end * arriving + fresh_ref[p]]
        for b in range(2):
            rows = slice(b * BLOCK, (b + 1) * BLOCK)
            left = jnp.concatenate([maps[slots[0], rows, :], maps[slots[1], rows, :]], axis=1)
            carried = dot(left, split_pair(entering[b].astype(BF16)))
            y = within_ref[rows, columns].astype(F32) + carried * growth[rows]
            square = y * y
            high = square.astype(BF16)
            low = (square - high.astype(F32)).astype(BF16)
            mean = dot(jnp.concatenate([high, low], axis=1), summing) * (1.0 / P_SIZE)
            normed[rows, columns] = (y * lax.rsqrt(mean + EPS) * gain_ref[:, columns]).astype(BF16)
    total[...] += dot(normed[...], w_ref[...])

    @pl.when(step == pl.num_programs(0) - 1)
    def _():
        share = own_ref.shape[0]

        def rows_for(offset):
            place = lax.rem(place_ref[0] + offset, 4)
            rows = total[pl.ds(pl.multiple_of(place * share, share), share), :]
            return rows.astype(BF16)

        own_ref[...] = rows_for(0)
        up_ref[...] = rows_for(1)
        far_ref[...] = rows_for(2)
        down_ref[...] = rows_for(3)


def put_cells(stage, j, value):
    for h in range(2):
        stage[h, pl.ds(j, value.shape[0], stride=ROW), :] = value[:, h * 128 : (h + 1) * 128]


def take_cells(stage, j, count):
    return jnp.concatenate(
        [stage[h, pl.ds(j, count, stride=ROW), :] for h in range(2)], axis=1
    ).astype(BF16)


def fill_stage(stage, rows_ref):
    for h in range(2):
        stage[h] = rows_ref[:, h * 128 : (h + 1) * 128].astype(F32)


def drain_stage(stage, rows_ref):
    for h in range(2):
        rows_ref[:, h * 128 : (h + 1) * 128] = stage[h].astype(BF16)


def tokens_kernel(
    residual_ref,
    own_ref,
    prev_ref,
    far_ref,
    next_ref,
    gain_ref,
    router_ref,
    ids_ref,
    stream_ref,
    weight_ref,
    *rest,
    ring,
):
    out_refs, (stage, tokens) = rest[:-2], rest[-2:]
    share, width = stream_ref.shape
    stream = (
        residual_ref[...].astype(F32)
        + own_ref[...].astype(F32)
        + prev_ref[...].astype(F32)
        + far_ref[...].astype(F32)
        + next_ref[...].astype(F32)
    )
    stream_ref[...] = stream
    square = jnp.mean(stream * stream, axis=-1, keepdims=True)
    tokens[...] = (stream * lax.rsqrt(square + EPS) * gain_ref[...]).astype(BF16)
    experts = router_ref.shape[1]
    place = lax.broadcasted_iota(jnp.int32, (share, experts), 1)
    hosted = place % ring * (experts // ring) + place // ring
    routed = jnp.zeros((share, experts), F32)
    for k in range(ids_ref.shape[1]):
        routed = routed + jnp.where(ids_ref[:, k : k + 1] == hosted, 1.0, 0.0)
    earlier = jnp.where(
        lax.broadcasted_iota(jnp.int32, (share, share), 0)
        > lax.broadcasted_iota(jnp.int32, (share, share), 1),
        1.0,
        0.0,
    ).astype(BF16)
    rank = dot(earlier, routed.astype(BF16))
    key = jnp.where(routed > 0.5, rank, -1.0).astype(BF16)
    logits = dot(tokens[...], router_ref[...])
    weight = 1.0 / (1.0 + jnp.exp(-logits))
    high = weight.astype(BF16)
    low = (weight - high.astype(F32)).astype(BF16)
    chunk = SLOTS // CHUNKS
    rows = experts * chunk
    spread = jnp.where(
        lax.broadcasted_iota(jnp.int32, (experts, rows), 0)
        == lax.broadcasted_iota(jnp.int32, (experts, rows), 1) // chunk,
        1.0,
        0.0,
    ).astype(BF16)
    wide = dot(jnp.concatenate([key, high, low], axis=0), spread)
    ranks, highs, lows = wide[:share], wide[share : 2 * share], wide[2 * share :]
    slot = (lax.broadcasted_iota(jnp.int32, (share, rows), 1) % chunk).astype(F32)
    for i in range(CHUNKS):
        placed = ranks == slot + float(i * chunk)
        weight_ref[i, :share] = jnp.where(placed, highs, 0.0).astype(BF16)
        weight_ref[i, share:] = jnp.where(placed, lows, 0.0).astype(BF16)
        pick = jnp.where(placed, 1.0, 0.0).T.astype(BF16)
        for j in range(ROW):
            put_cells(stage, j, dot(pick, tokens[:, j * CELL : (j + 1) * CELL]))
        drain_stage(stage, out_refs[i])


def experts_kernel(
    x_ref,
    g0,
    u0,
    d0,
    g1,
    u1,
    d1,
    out_ref,
    stage,
    rows,
    hidden,
    wide,
    deep,
    wide_sem,
    deep_sem,
):
    count, width = rows.shape
    unit = g0.shape[1]
    n_wide, n_deep = wide.shape[0], deep.shape[0]
    wide_step, deep_step = 2 * unit // n_wide, width // n_deep
    halves = [(g0, u0, d0), (g1, u1, d1)]

    def copies(s):
        if s < n_wide:
            half = halves[s * wide_step // unit]
            columns = pl.ds(s * wide_step % unit, wide_step)
            return [
                pltpu.make_async_copy(half[i].at[:, columns], wide.at[s, i], wide_sem.at[s, i])
                for i in range(2)
            ]
        s -= n_wide
        columns = pl.ds(s * deep_step, deep_step)
        return [
            pltpu.make_async_copy(
                halves[i][2].at[:, columns], deep.at[s, pl.ds(i * unit, unit)], deep_sem.at[s, i]
            )
            for i in range(2)
        ]

    total_steps = n_wide + n_deep
    ahead = 3
    for s in range(ahead):
        for copy in copies(s):
            copy.start()
    fill_stage(stage, x_ref)
    for j in range(ROW):
        rows[:, j * CELL : (j + 1) * CELL] = take_cells(stage, j, count)
    for s in range(total_steps):
        if s + ahead < total_steps:
            for copy in copies(s + ahead):
                copy.start()
        for copy in copies(s):
            copy.wait()
        if s < n_wide:
            gated = dot(rows[...], wide[s, 0])
            raised = dot(rows[...], wide[s, 1])
            hidden[:, s * wide_step : (s + 1) * wide_step] = (
                gated / (1.0 + jnp.exp(-gated)) * raised
            ).astype(BF16)
        else:
            d = s - n_wide
            for c in range(deep_step // CELL):
                part = dot(hidden[...], deep[d, :, c * CELL : (c + 1) * CELL])
                put_cells(stage, d * (deep_step // CELL) + c, part)
    drain_stage(stage, out_ref)


def combine_kernel(base_ref, weight_ref, rows_ref, out_ref, stage):
    share = base_ref.shape[0]
    count = weight_ref.shape[1]
    fill_stage(stage, rows_ref)
    for j in range(ROW):
        columns = slice(j * CELL, (j + 1) * CELL)
        part = dot(weight_ref[...], take_cells(stage, j, count))
        out_ref[:, columns] = (base_ref[:, columns] + part[:share] + part[share:]).astype(
            out_ref.dtype
        )


def whole(shape):
    return pl.BlockSpec(shape, lambda s, *_: (0,) * len(shape))


def params(mib=60):
    return pltpu.CompilerParams(
        dimension_semantics=("arbitrary",), vmem_limit_bytes=mib * MIB
    )


def body(
    ssd_input,
    dt_raw,
    dt_bias,
    log_decay,
    input_map,
    output_map,
    head_group,
    d_skip,
    norm_gain,
    w_out,
    residual,
    moe_gain,
    w_router,
    expert_ids,
    w_gate,
    w_up,
    w_down,
):
    length = ssd_input.shape[0]
    heads = dt_raw.shape[1]
    width = w_out.shape[1]
    share = residual.shape[0]
    me = lax.axis_index("exp")
    ring = lax.axis_size("exp")
    seq_count = lax.axis_size("seq")
    nxt = [(i, (i + 1) % ring) for i in range(ring)]
    prv = [(i, (i - 1) % ring) for i in range(ring)]
    partner = [(i, i ^ 1) for i in range(seq_count)]
    steps = heads // (2 * STEP_PAIRS)
    columns = STEP_PAIRS * PAIR

    opposite = [(i, (i + 2) % ring) for i in range(ring)]

    def gather_maps(own):
        far = lax.ppermute(own, "exp", opposite)
        return own, lax.ppermute(own, "exp", prv), far, lax.ppermute(own, "exp", nxt)

    in_maps = gather_maps(input_map.transpose(1, 2, 0))
    out_maps = gather_maps(output_map.transpose(1, 0, 2))
    slot = (lax.rem(head_group // 2 - me + ring, ring) * 2 + head_group % 2).astype(jnp.int32)

    prep = pl.pallas_call(
        prep_kernel,
        out_shape=jax.ShapeDtypeStruct((4, heads, length), F32),
        compiler_params=pltpu.CompilerParams(vmem_limit_bytes=16 * MIB),
        cost_estimate=pl.CostEstimate(
            flops=30_000_000, bytes_accessed=400_000, transcendentals=100_000
        ),
        name="prep",
    )(dt_raw.T, dt_bias[:, None], log_decay.T)
    skip_lanes = jnp.repeat(d_skip, P_SIZE)[None, :]
    gain_lanes = norm_gain[None, :]

    x_spec = pl.BlockSpec((length, columns), lambda s, *_: (0, s))
    prep_spec = pl.BlockSpec((4, 2 * STEP_PAIRS, length), lambda s, *_: (0, s, 0))
    lane_spec = pl.BlockSpec((1, columns), lambda s, *_: (0, s))
    state_spec = pl.BlockSpec((STEP_PAIRS, NST, PAIR), lambda s, *_: (s, 0, 0))
    in_specs = [whole((2, NST, length))] * 4
    out_specs = [whole((2, length, NST))] * 4

    fresh, sending = pl.pallas_call(
        states_kernel,
        grid_spec=pltpu.PrefetchScalarGridSpec(
            num_scalar_prefetch=1,
            grid=(steps,),
            in_specs=[x_spec, prep_spec] + in_specs,
            out_specs=[pl.BlockSpec(memory_space=pltpu.HBM)] * 2,
            scratch_shapes=[
                pltpu.VMEM((G, NST, length), BF16),
                pltpu.VMEM((heads // 2, NST, PAIR), F32),
                pltpu.VMEM((heads, 72, PAIR), BF16),
                pltpu.SemaphoreType.DMA((steps,)),
                pltpu.SemaphoreType.DMA((steps,)),
            ],
        ),
        out_shape=[
            jax.ShapeDtypeStruct((heads // 2, NST, PAIR), F32),
            jax.ShapeDtypeStruct((heads, 72, PAIR), BF16),
        ],
        compiler_params=params(16),
        cost_estimate=pl.CostEstimate(
            flops=600_000_000, bytes_accessed=5_000_000, transcendentals=0
        ),
        name="states",
    )(slot, ssd_input, prep, *in_maps)

    sending, own_gate, own_up, own_down = lax.optimization_barrier(
        (sending, w_gate[0], w_up[0], w_down[0])
    )
    other_gate = lax.ppermute(own_gate, "seq", partner)
    other_up = lax.ppermute(own_up, "seq", partner)
    other_down = lax.ppermute(own_down, "seq", partner)

    arrived = lax.all_to_all(sending, "seq", split_axis=0, concat_axis=0, tiled=True)
    prefix = pl.pallas_call(
        scan_kernel,
        out_shape=jax.ShapeDtypeStruct((seq_count, 64, PAIR), BF16),
        compiler_params=pltpu.CompilerParams(vmem_limit_bytes=16 * MIB),
        name="scan",
    )(arrived)
    entering = lax.all_to_all(prefix, "seq", split_axis=0, concat_axis=0, tiled=True)
    entering = entering.reshape(heads // 2, NST, PAIR)

    within = pl.pallas_call(
        within_kernel,
        grid_spec=pltpu.PrefetchScalarGridSpec(
            num_scalar_prefetch=1,
            grid=(steps,),
            in_specs=[x_spec, prep_spec, lane_spec] + in_specs + out_specs,
            out_specs=x_spec,
            scratch_shapes=[pltpu.VMEM((G, 2, BLOCK, BLOCK), F32)],
        ),
        out_shape=jax.ShapeDtypeStruct(ssd_input.shape, BF16),
        compiler_params=params(),
        cost_estimate=pl.CostEstimate(
            flops=12_000_000_000, bytes_accessed=8_000_000, transcendentals=4_000_000
        ),
        name="within",
    )(slot, ssd_input, prep, skip_lanes, *in_maps, *out_maps)

    vmem = pl.BlockSpec(memory_space=pltpu.VMEM)
    hbm = pl.BlockSpec(memory_space=pl.ANY)
    within, other_gate, other_up, other_down = lax.optimization_barrier(
        (within, other_gate, other_up, other_down)
    )
    own, up, far, down = pl.pallas_call(
        project_kernel,
        grid_spec=pltpu.PrefetchScalarGridSpec(
            num_scalar_prefetch=2,
            grid=(steps,),
            in_specs=[x_spec, prep_spec, lane_spec, state_spec, state_spec]
            + out_specs
            + [pl.BlockSpec((columns, width), lambda s, *_: (s, 0))],
            out_specs=[whole((share, width))] * 4,
            scratch_shapes=[
                pltpu.VMEM((G, length, NST), BF16),
                pltpu.VMEM((length, columns), BF16),
                pltpu.VMEM((length, width), F32),
            ],
        ),
        out_shape=[jax.ShapeDtypeStruct((share, width), BF16)] * 4,
        compiler_params=params(),
        cost_estimate=pl.CostEstimate(
            flops=6_000_000_000, bytes_accessed=16_000_000, transcendentals=0
        ),
        name="project",
    )(slot, me[None].astype(jnp.int32), within, prep, gain_lanes, entering, fresh, *out_maps, w_out)

    from_prev = lax.ppermute(up, "exp", nxt)
    from_far = lax.ppermute(far, "exp", opposite)
    from_next = lax.ppermute(down, "exp", prv)

    experts = w_router.shape[1]
    per_group = experts // ring
    router = w_router.reshape(-1, ring, per_group).swapaxes(1, 2).reshape(-1, experts)
    chunk = SLOTS // CHUNKS
    count = experts * chunk
    cells = (count * ROW, CELL)
    stage = (2, count * ROW, CELL // 2)
    stream, weights, *outgoing = pl.pallas_call(
        functools.partial(tokens_kernel, ring=ring),
        out_shape=[
            jax.ShapeDtypeStruct((share, width), F32),
            jax.ShapeDtypeStruct((CHUNKS, 2 * share, count), BF16),
        ]
        + [jax.ShapeDtypeStruct(cells, BF16)] * CHUNKS,
        scratch_shapes=[pltpu.VMEM(stage, F32), pltpu.VMEM((share, width), BF16)],
        compiler_params=pltpu.CompilerParams(vmem_limit_bytes=32 * MIB),
        cost_estimate=pl.CostEstimate(
            flops=1_000_000_000, bytes_accessed=8_000_000, transcendentals=0
        ),
        name="tokens",
    )(residual, own, from_prev, from_far, from_next, moe_gain[None, :], router, expert_ids)

    cores = [
        [(c // ring * 2 + h) * ring + c % ring for c in range(experts)] for h in range(2)
    ]

    def swap(rows):
        swapped = lax.all_to_all(
            rows.reshape(count, ROW, CELL),
            ("seq", "exp"),
            split_axis=0,
            concat_axis=0,
            tiled=True,
            axis_index_groups=cores,
        )
        return swapped.reshape(cells)

    unit = w_gate.shape[2]
    run_experts = pl.pallas_call(
        experts_kernel,
        in_specs=[vmem] + [hbm] * 6,
        out_specs=vmem,
        out_shape=jax.ShapeDtypeStruct(cells, BF16),
        scratch_shapes=[
            pltpu.VMEM(stage, F32),
            pltpu.VMEM((count, width), BF16),
            pltpu.VMEM((count, 2 * unit), BF16),
            pltpu.VMEM((8, 2, width, unit // 4), BF16),
            pltpu.VMEM((4, 2 * unit, width // 4), BF16),
            pltpu.SemaphoreType.DMA((8, 2)),
            pltpu.SemaphoreType.DMA((4, 2)),
        ],
        compiler_params=pltpu.CompilerParams(vmem_limit_bytes=60 * MIB),
        cost_estimate=pl.CostEstimate(
            flops=12 * count * width * unit,
            bytes_accessed=28_000_000,
            transcendentals=0,
        ),
        name="experts",
    )

    def combine(base, weight, rows, dtype):
        return pl.pallas_call(
            combine_kernel,
            out_shape=jax.ShapeDtypeStruct((share, width), dtype),
            scratch_shapes=[pltpu.VMEM(stage, F32)],
            compiler_params=pltpu.CompilerParams(vmem_limit_bytes=24 * MIB),
            cost_estimate=pl.CostEstimate(
                flops=500_000_000, bytes_accessed=4_000_000, transcendentals=0
            ),
            name="combine",
        )(base, weight, rows)

    arrivals = [swap(rows) for rows in outgoing]
    returned = [
        swap(
            run_experts(
                rows, w_gate[0], w_up[0], w_down[0], other_gate, other_up, other_down
            )
        )
        for rows in arrivals
    ]
    mixed = stream
    for i in range(CHUNKS):
        mixed = combine(mixed, weights[i], returned[i], BF16 if i == CHUNKS - 1 else F32)
    return mixed


def solution(mesh):
    return jax.shard_map(
        body,
        mesh=mesh,
        in_specs=(
            P("seq", "exp"),
            P("seq", "exp"),
            P("exp"),
            P("seq", "exp"),
            P("seq", "exp", None),
            P("seq", "exp", None),
            P("exp"),
            P("exp"),
            P("exp"),
            P("exp", None),
            P(("seq", "exp"), None),
            P(),
            P(),
            P(("seq", "exp"), None),
            P(("seq", "exp"), None, None),
            P(("seq", "exp"), None, None),
            P(("seq", "exp"), None, None),
        ),
        out_specs=P(("seq", "exp"), None),
        check_vma=False,
    )
```

```python
import functools

import jax
import jax.numpy as jnp
from jax import lax
from jax.experimental import pallas as pl
from jax.experimental.pallas import tpu as pltpu
from jax.sharding import PartitionSpec as P

P_SIZE = 64
NST = 128
G = 8
BLOCK = 256
PAIR = 2 * P_SIZE
STEP_PAIRS = 4
SLOTS = 14
CHUNKS = 2
ROW = 8
CELL = 256

EPS = 1e-06
F32 = jnp.float32
BF16 = jnp.bfloat16
MIB = 1024 * 1024


def dot(a, b):
    return jnp.dot(a, b, preferred_element_type=F32)


def lanes_of_first(shape):
    return lax.broadcasted_iota(jnp.int32, shape, 1) < P_SIZE


def columns_of(first_row, second_row):
    length = first_row.shape[1]
    rows = jnp.concatenate(
        [
            jnp.broadcast_to(first_row, (P_SIZE, length)),
            jnp.broadcast_to(second_row, (P_SIZE, length)),
        ],
        axis=0,
    )
    return rows.T


def lane_pair(first, second):
    return jnp.concatenate(
        [jnp.broadcast_to(first, (1, P_SIZE)), jnp.broadcast_to(second, (1, P_SIZE))], axis=1
    )


def split_pair(values):
    first = lanes_of_first(values.shape)
    zero = jnp.zeros_like(values)
    return jnp.concatenate([jnp.where(first, values, zero), jnp.where(first, zero, values)], axis=0)


def prep_kernel(raw_ref, bias_ref, decay_ref, out_ref):
    value = raw_ref[...] + bias_ref[...]
    size = jnp.maximum(value, 0.0) + jnp.log(1.0 + jnp.exp(-jnp.abs(value)))
    upto = jnp.where(
        lax.broadcasted_iota(jnp.int32, (BLOCK, BLOCK), 0)
        <= lax.broadcasted_iota(jnp.int32, (BLOCK, BLOCK), 1),
        1.0,
        0.0,
    ).astype(BF16)
    heads, length = size.shape
    for b in range(length // BLOCK):
        rows = slice(b * BLOCK, (b + 1) * BLOCK)
        rest = decay_ref[:, rows]
        terms = []
        for _ in range(3):
            terms.append(rest.astype(BF16))
            rest = rest - terms[-1].astype(F32)
        sums = dot(jnp.concatenate(terms, axis=0), upto)
        running = sums[:heads] + sums[heads : 2 * heads] + sums[2 * heads :]
        out_ref[0, :, rows] = running
        out_ref[1, :, rows] = size[:, rows]
        out_ref[2, :, rows] = jnp.exp(running[:, BLOCK - 1 :] - running) * size[:, rows]
        out_ref[3, :, rows] = jnp.exp(running)


def states_kernel(
    slot_ref,
    x_ref,
    prep_ref,
    m0,
    m1,
    m2,
    m3,
    fresh_hbm,
    send_hbm,
    maps,
    fresh_all,
    send_all,
    fresh_sem,
    send_sem,
):
    step = pl.program_id(0)
    steps = fresh_sem.shape[0]

    def out_copies(at):
        pairs = pl.ds(at * STEP_PAIRS, STEP_PAIRS)
        pieces = pl.ds(at * 2 * STEP_PAIRS, 2 * STEP_PAIRS)
        return [
            pltpu.make_async_copy(send_all.at[pieces], send_hbm.at[pieces], send_sem.at[at]),
            pltpu.make_async_copy(fresh_all.at[pairs], fresh_hbm.at[pairs], fresh_sem.at[at]),
        ]

    @pl.when(step == 0)
    def _():
        maps[0:2] = m0[...]
        maps[2:4] = m1[...]
        maps[4:6] = m2[...]
        maps[6:8] = m3[...]

    for p in range(STEP_PAIRS):
        slots = [slot_ref[step * 2 * STEP_PAIRS + 2 * p + i] for i in range(2)]
        x = x_ref[:, p * PAIR : (p + 1) * PAIR].astype(F32)
        weight = columns_of(prep_ref[2, 2 * p : 2 * p + 1, :], prep_ref[2, 2 * p + 1 : 2 * p + 2, :])
        scaled = (x * weight).astype(BF16)
        fresh = []
        for b in range(2):
            rows = slice(b * BLOCK, (b + 1) * BLOCK)
            both = split_pair(scaled[rows])
            left = jnp.concatenate([maps[slots[0], :, rows], maps[slots[1], :, rows]], axis=1)
            fresh.append(dot(left, both))
        ends = [
            lane_pair(
                prep_ref[3, 2 * p : 2 * p + 1, e - 1 : e],
                prep_ref[3, 2 * p + 1 : 2 * p + 2, e - 1 : e],
            )
            for e in (BLOCK, 2 * BLOCK)
        ]
        fresh_all[step * STEP_PAIRS + p] = fresh[0]
        final = (ends[1] * fresh[0] + fresh[1]).astype(BF16)
        decay = ends[0] * ends[1]
        high = decay.astype(BF16).astype(F32)
        row = lax.broadcasted_iota(jnp.int32, (8, PAIR), 0)
        tail = jnp.where(row == 0, high, jnp.where(row == 1, decay - high, 0.0)).astype(BF16)
        for i in range(2):
            piece = step * 2 * STEP_PAIRS + 2 * p + i
            send_all[piece, 0:64] = final[64 * i : 64 * (i + 1)]
            send_all[piece, 64:72] = tail
    for copy in out_copies(step):
        copy.start()

    @pl.when(step == steps - 1)
    def _():
        for at in range(steps):
            for copy in out_copies(at):
                copy.wait()


def scan_kernel(in_ref, out_ref):
    state = jnp.zeros((64, PAIR), F32)
    for j in range(in_ref.shape[0]):
        out_ref[j] = state.astype(BF16)
        tail = in_ref[j, 64:72].astype(F32)
        decay = tail[0:1] + tail[1:2]
        state = decay * state + in_ref[j, 0:64].astype(F32)


def within_kernel(
    slot_ref, x_ref, prep_ref, skip_ref, i0, i1, i2, i3, o0, o1, o2, o3, out_ref, scores
):
    step = pl.program_id(0)

    @pl.when(step == 0)
    def _():
        inputs = [ref.at[i] for ref in (i0, i1, i2, i3) for i in range(2)]
        outputs = [ref.at[i] for ref in (o0, o1, o2, o3) for i in range(2)]
        for g in range(G):
            for b in range(2):
                rows = slice(b * BLOCK, (b + 1) * BLOCK)
                scores[g, b] = dot(outputs[g][rows, :], inputs[g][:, rows])

    half = BLOCK // 2
    causal = lax.broadcasted_iota(jnp.int32, (half, half), 0) >= lax.broadcasted_iota(
        jnp.int32, (half, half), 1
    )
    for p in range(STEP_PAIRS):
        columns = slice(p * PAIR, (p + 1) * PAIR)
        slots = [slot_ref[step * 2 * STEP_PAIRS + 2 * p + i] for i in range(2)]
        for b in range(2):
            rows = slice(b * BLOCK, (b + 1) * BLOCK)
            x = x_ref[rows, columns]
            early, late = [], []
            for i in range(2):
                running = prep_ref[0, 2 * p + i : 2 * p + i + 1, rows]
                size = prep_ref[1, 2 * p + i : 2 * p + i + 1, rows]
                down = jnp.broadcast_to(running, (half, BLOCK)).T

                def tile(t, s, masked):
                    ts, ss = slice(t * half, (t + 1) * half), slice(s * half, (s + 1) * half)
                    spread = down[ts] - running[:, ss]
                    score = scores[slots[i], b, ts, ss]
                    value = score * jnp.exp(spread) * size[:, ss]
                    return (jnp.where(causal, value, 0.0) if masked else value).astype(BF16)

                early.append(tile(0, 0, True))
                late.append(tile(1, 0, False))
                late.append(tile(1, 1, True))
            both = split_pair(x)
            first = jnp.concatenate([both[0:half], both[BLOCK : BLOCK + half]], axis=0)
            skipped = skip_ref[:, columns] * x.astype(F32)
            top = dot(jnp.concatenate(early, axis=1), first)
            bottom = dot(jnp.concatenate(late, axis=1), both)
            out_ref[b * BLOCK : b * BLOCK + half, columns] = (top + skipped[0:half]).astype(BF16)
            out_ref[b * BLOCK + half : (b + 1) * BLOCK, columns] = (bottom + skipped[half:]).astype(
                BF16
            )


def project_kernel(
    slot_ref,
    place_ref,
    within_ref,
    prep_ref,
    gain_ref,
    enter_ref,
    fresh_ref,
    o0,
    o1,
    o2,
    o3,
    w_ref,
    own_ref,
    up_ref,
    far_ref,
    down_ref,
    maps,
    normed,
    total,
):
    step = pl.program_id(0)

    @pl.when(step == 0)
    def _():
        maps[0:2] = o0[...]
        maps[2:4] = o1[...]
        maps[4:6] = o2[...]
        maps[6:8] = o3[...]
        total[...] = jnp.zeros_like(total)

    same = (
        lax.broadcasted_iota(jnp.int32, (2 * PAIR, PAIR), 0) % PAIR // P_SIZE
        == lax.broadcasted_iota(jnp.int32, (2 * PAIR, PAIR), 1) // P_SIZE
    )
    summing = jnp.where(same, 1.0, 0.0).astype(BF16)
    for p in range(STEP_PAIRS):
        columns = slice(p * PAIR, (p + 1) * PAIR)
        slots = [slot_ref[step * 2 * STEP_PAIRS + 2 * p + i] for i in range(2)]
        growth = columns_of(prep_ref[3, 2 * p : 2 * p + 1, :], prep_ref[3, 2 * p + 1 : 2 * p + 2, :])
        first_end = lane_pair(
            prep_ref[3, 2 * p : 2 * p + 1, BLOCK - 1 : BLOCK], prep_ref[3, 2 * p + 1 : 2 * p + 2, BLOCK - 1 : BLOCK]
        )
        arriving = enter_ref[p].astype(F32)
        entering = [arriving, first_end * arriving + fresh_ref[p]]
        for b in range(2):
            rows = slice(b * BLOCK, (b + 1) * BLOCK)
            left = jnp.concatenate([maps[slots[0], rows, :], maps[slots[1], rows, :]], axis=1)
            carried = dot(left, split_pair(entering[b].astype(BF16)))
            y = within_ref[rows, columns].astype(F32) + carried * growth[rows]
            square = y * y
            high = square.astype(BF16)
            low = (square - high.astype(F32)).astype(BF16)
            mean = dot(jnp.concatenate([high, low], axis=1), summing) * (1.0 / P_SIZE)
            normed[rows, columns] = (y * lax.rsqrt(mean + EPS) * gain_ref[:, columns]).astype(BF16)
    total[...] += dot(normed[...], w_ref[...])

    @pl.when(step == pl.num_programs(0) - 1)
    def _():
        share = own_ref.shape[0]

        def rows_for(offset):
            place = lax.rem(place_ref[0] + offset, 4)
            rows = total[pl.ds(pl.multiple_of(place * share, share), share), :]
            return rows.astype(BF16)

        own_ref[...] = rows_for(0)
        up_ref[...] = rows_for(1)
        far_ref[...] = rows_for(2)
        down_ref[...] = rows_for(3)


def put_cells(stage, j, value):
    for h in range(2):
        stage[h, pl.ds(j, value.shape[0], stride=ROW), :] = value[:, h * 128 : (h + 1) * 128]


def take_cells(stage, j, count):
    return jnp.concatenate(
        [stage[h, pl.ds(j, count, stride=ROW), :] for h in range(2)], axis=1
    ).astype(BF16)


def fill_stage(stage, rows_ref):
    for h in range(2):
        stage[h] = rows_ref[:, h * 128 : (h + 1) * 128].astype(F32)


def drain_stage(stage, rows_ref):
    for h in range(2):
        rows_ref[:, h * 128 : (h + 1) * 128] = stage[h].astype(BF16)


def tokens_kernel(
    residual_ref,
    own_ref,
    prev_ref,
    far_ref,
    next_ref,
    gain_ref,
    router_ref,
    ids_ref,
    stream_ref,
    weight_ref,
    *rest,
    ring,
):
    out_refs, (stage, tokens) = rest[:-2], rest[-2:]
    share, width = stream_ref.shape
    stream = (
        residual_ref[...].astype(F32)
        + own_ref[...].astype(F32)
        + prev_ref[...].astype(F32)
        + far_ref[...].astype(F32)
        + next_ref[...].astype(F32)
    )
    stream_ref[...] = stream
    square = jnp.mean(stream * stream, axis=-1, keepdims=True)
    tokens[...] = (stream * lax.rsqrt(square + EPS) * gain_ref[...]).astype(BF16)
    experts = router_ref.shape[1]
    place = lax.broadcasted_iota(jnp.int32, (share, experts), 1)
    hosted = place % ring * (experts // ring) + place // ring
    routed = jnp.zeros((share, experts), F32)
    for k in range(ids_ref.shape[1]):
        routed = routed + jnp.where(ids_ref[:, k : k + 1] == hosted, 1.0, 0.0)
    earlier = jnp.where(
        lax.broadcasted_iota(jnp.int32, (share, share), 0)
        > lax.broadcasted_iota(jnp.int32, (share, share), 1),
        1.0,
        0.0,
    ).astype(BF16)
    rank = dot(earlier, routed.astype(BF16))
    key = jnp.where(routed > 0.5, rank, -1.0).astype(BF16)
    logits = dot(tokens[...], router_ref[...])
    weight = 1.0 / (1.0 + jnp.exp(-logits))
    high = weight.astype(BF16)
    low = (weight - high.astype(F32)).astype(BF16)
    chunk = SLOTS // CHUNKS
    rows = experts * chunk
    spread = jnp.where(
        lax.broadcasted_iota(jnp.int32, (experts, rows), 0)
        == lax.broadcasted_iota(jnp.int32, (experts, rows), 1) // chunk,
        1.0,
        0.0,
    ).astype(BF16)
    wide = dot(jnp.concatenate([key, high, low], axis=0), spread)
    ranks, highs, lows = wide[:share], wide[share : 2 * share], wide[2 * share :]
    slot = (lax.broadcasted_iota(jnp.int32, (share, rows), 1) % chunk).astype(F32)
    for i in range(CHUNKS):
        placed = ranks == slot + float(i * chunk)
        weight_ref[i, :share] = jnp.where(placed, highs, 0.0).astype(BF16)
        weight_ref[i, share:] = jnp.where(placed, lows, 0.0).astype(BF16)
        pick = jnp.where(placed, 1.0, 0.0).T.astype(BF16)
        for j in range(ROW):
            put_cells(stage, j, dot(pick, tokens[:, j * CELL : (j + 1) * CELL]))
        drain_stage(stage, out_refs[i])


def experts_kernel(
    x_ref,
    g0,
    u0,
    d0,
    g1,
    u1,
    d1,
    out_ref,
    stage,
    rows,
    hidden,
    wide,
    deep,
    wide_sem,
    deep_sem,
):
    count, width = rows.shape
    unit = g0.shape[1]
    n_wide, n_deep = wide.shape[0], deep.shape[0]
    wide_step, deep_step = 2 * unit // n_wide, width // n_deep
    halves = [(g0, u0, d0), (g1, u1, d1)]

    def copies(s):
        if s < n_wide:
            half = halves[s * wide_step // unit]
            columns = pl.ds(s * wide_step % unit, wide_step)
            return [
                pltpu.make_async_copy(half[i].at[:, columns], wide.at[s, i], wide_sem.at[s, i])
                for i in range(2)
            ]
        s -= n_wide
        columns = pl.ds(s * deep_step, deep_step)
        return [
            pltpu.make_async_copy(
                halves[i][2].at[:, columns], deep.at[s, pl.ds(i * unit, unit)], deep_sem.at[s, i]
            )
            for i in range(2)
        ]

    total_steps = n_wide + n_deep
    ahead = 3
    for s in range(ahead):
        for copy in copies(s):
            copy.start()
    fill_stage(stage, x_ref)
    for j in range(ROW):
        rows[:, j * CELL : (j + 1) * CELL] = take_cells(stage, j, count)
    for s in range(total_steps):
        if s + ahead < total_steps:
            for copy in copies(s + ahead):
                copy.start()
        for copy in copies(s):
            copy.wait()
        if s < n_wide:
            gated = dot(rows[...], wide[s, 0])
            raised = dot(rows[...], wide[s, 1])
            hidden[:, s * wide_step : (s + 1) * wide_step] = (
                gated / (1.0 + jnp.exp(-gated)) * raised
            ).astype(BF16)
        else:
            d = s - n_wide
            for c in range(deep_step // CELL):
                part = dot(hidden[...], deep[d, :, c * CELL : (c + 1) * CELL])
                put_cells(stage, d * (deep_step // CELL) + c, part)
    drain_stage(stage, out_ref)


def combine_kernel(base_ref, weight_ref, rows_ref, out_ref, stage):
    share = base_ref.shape[0]
    count = weight_ref.shape[1]
    fill_stage(stage, rows_ref)
    for j in range(ROW):
        columns = slice(j * CELL, (j + 1) * CELL)
        part = dot(weight_ref[...], take_cells(stage, j, count))
        out_ref[:, columns] = (base_ref[:, columns] + part[:share] + part[share:]).astype(
            out_ref.dtype
        )


def whole(shape):
    return pl.BlockSpec(shape, lambda s, *_: (0,) * len(shape))


def params(mib=60):
    return pltpu.CompilerParams(
        dimension_semantics=("arbitrary",), vmem_limit_bytes=mib * MIB
    )


def body(
    ssd_input,
    dt_raw,
    dt_bias,
    log_decay,
    input_map,
    output_map,
    head_group,
    d_skip,
    norm_gain,
    w_out,
    residual,
    moe_gain,
    w_router,
    expert_ids,
    w_gate,
    w_up,
    w_down,
):
    length = ssd_input.shape[0]
    heads = dt_raw.shape[1]
    width = w_out.shape[1]
    share = residual.shape[0]
    me = lax.axis_index("exp")
    ring = lax.axis_size("exp")
    seq_count = lax.axis_size("seq")
    nxt = [(i, (i + 1) % ring) for i in range(ring)]
    prv = [(i, (i - 1) % ring) for i in range(ring)]
    partner = [(i, i ^ 1) for i in range(seq_count)]
    steps = heads // (2 * STEP_PAIRS)
    columns = STEP_PAIRS * PAIR

    opposite = [(i, (i + 2) % ring) for i in range(ring)]

    def gather_maps(own):
        far = lax.ppermute(own, "exp", opposite)
        return own, lax.ppermute(own, "exp", prv), far, lax.ppermute(own, "exp", nxt)

    in_maps = gather_maps(input_map.transpose(1, 2, 0))
    out_maps = gather_maps(output_map.transpose(1, 0, 2))
    slot = (lax.rem(head_group // 2 - me + ring, ring) * 2 + head_group % 2).astype(jnp.int32)

    prep = pl.pallas_call(
        prep_kernel,
        out_shape=jax.ShapeDtypeStruct((4, heads, length), F32),
        compiler_params=pltpu.CompilerParams(vmem_limit_bytes=16 * MIB),
        cost_estimate=pl.CostEstimate(
            flops=30_000_000, bytes_accessed=400_000, transcendentals=100_000
        ),
        name="prep",
    )(dt_raw.T, dt_bias[:, None], log_decay.T)
    skip_lanes = jnp.repeat(d_skip, P_SIZE)[None, :]
    gain_lanes = norm_gain[None, :]

    x_spec = pl.BlockSpec((length, columns), lambda s, *_: (0, s))
    prep_spec = pl.BlockSpec((4, 2 * STEP_PAIRS, length), lambda s, *_: (0, s, 0))
    lane_spec = pl.BlockSpec((1, columns), lambda s, *_: (0, s))
    state_spec = pl.BlockSpec((STEP_PAIRS, NST, PAIR), lambda s, *_: (s, 0, 0))
    in_specs = [whole((2, NST, length))] * 4
    out_specs = [whole((2, length, NST))] * 4

    fresh, sending = pl.pallas_call(
        states_kernel,
        grid_spec=pltpu.PrefetchScalarGridSpec(
            num_scalar_prefetch=1,
            grid=(steps,),
            in_specs=[x_spec, prep_spec] + in_specs,
            out_specs=[pl.BlockSpec(memory_space=pltpu.HBM)] * 2,
            scratch_shapes=[
                pltpu.VMEM((G, NST, length), BF16),
                pltpu.VMEM((heads // 2, NST, PAIR), F32),
                pltpu.VMEM((heads, 72, PAIR), BF16),
                pltpu.SemaphoreType.DMA((steps,)),
                pltpu.SemaphoreType.DMA((steps,)),
            ],
        ),
        out_shape=[
            jax.ShapeDtypeStruct((heads // 2, NST, PAIR), F32),
            jax.ShapeDtypeStruct((heads, 72, PAIR), BF16),
        ],
        compiler_params=params(16),
        cost_estimate=pl.CostEstimate(
            flops=600_000_000, bytes_accessed=5_000_000, transcendentals=0
        ),
        name="states",
    )(slot, ssd_input, prep, *in_maps)

    sending, own_gate = lax.optimization_barrier((sending, w_gate[0]))
    other_gate = lax.ppermute(own_gate, "seq", partner)
    other_up = lax.ppermute(w_up[0], "seq", partner)
    other_down = lax.ppermute(w_down[0], "seq", partner)

    arrived = lax.all_to_all(sending, "seq", split_axis=0, concat_axis=0, tiled=True)
    prefix = pl.pallas_call(
        scan_kernel,
        out_shape=jax.ShapeDtypeStruct((seq_count, 64, PAIR), BF16),
        compiler_params=pltpu.CompilerParams(vmem_limit_bytes=16 * MIB),
        name="scan",
    )(arrived)
    entering = lax.all_to_all(prefix, "seq", split_axis=0, concat_axis=0, tiled=True)
    entering = entering.reshape(heads // 2, NST, PAIR)

    within = pl.pallas_call(
        within_kernel,
        grid_spec=pltpu.PrefetchScalarGridSpec(
            num_scalar_prefetch=1,
            grid=(steps,),
            in_specs=[x_spec, prep_spec, lane_spec] + in_specs + out_specs,
            out_specs=x_spec,
            scratch_shapes=[pltpu.VMEM((G, 2, BLOCK, BLOCK), F32)],
        ),
        out_shape=jax.ShapeDtypeStruct(ssd_input.shape, BF16),
        compiler_params=params(),
        cost_estimate=pl.CostEstimate(
            flops=12_000_000_000, bytes_accessed=8_000_000, transcendentals=4_000_000
        ),
        name="within",
    )(slot, ssd_input, prep, skip_lanes, *in_maps, *out_maps)

    vmem = pl.BlockSpec(memory_space=pltpu.VMEM)
    hbm = pl.BlockSpec(memory_space=pl.ANY)
    within, other_gate = lax.optimization_barrier((within, other_gate))
    own, up, far, down = pl.pallas_call(
        project_kernel,
        grid_spec=pltpu.PrefetchScalarGridSpec(
            num_scalar_prefetch=2,
            grid=(steps,),
            in_specs=[x_spec, prep_spec, lane_spec, state_spec, state_spec]
            + out_specs
            + [pl.BlockSpec((columns, width), lambda s, *_: (s, 0))],
            out_specs=[whole((share, width))] * 4,
            scratch_shapes=[
                pltpu.VMEM((G, length, NST), BF16),
                pltpu.VMEM((length, columns), BF16),
                pltpu.VMEM((length, width), F32),
            ],
        ),
        out_shape=[jax.ShapeDtypeStruct((share, width), BF16)] * 4,
        compiler_params=params(),
        cost_estimate=pl.CostEstimate(
            flops=6_000_000_000, bytes_accessed=16_000_000, transcendentals=0
        ),
        name="project",
    )(slot, me[None].astype(jnp.int32), within, prep, gain_lanes, entering, fresh, *out_maps, w_out)

    from_prev = lax.ppermute(up, "exp", nxt)
    from_far = lax.ppermute(far, "exp", opposite)
    from_next = lax.ppermute(down, "exp", prv)

    experts = w_router.shape[1]
    per_group = experts // ring
    router = w_router.reshape(-1, ring, per_group).swapaxes(1, 2).reshape(-1, experts)
    chunk = SLOTS // CHUNKS
    count = experts * chunk
    cells = (count * ROW, CELL)
    stage = (2, count * ROW, CELL // 2)
    stream, weights, *outgoing = pl.pallas_call(
        functools.partial(tokens_kernel, ring=ring),
        out_shape=[
            jax.ShapeDtypeStruct((share, width), F32),
            jax.ShapeDtypeStruct((CHUNKS, 2 * share, count), BF16),
        ]
        + [jax.ShapeDtypeStruct(cells, BF16)] * CHUNKS,
        scratch_shapes=[pltpu.VMEM(stage, F32), pltpu.VMEM((share, width), BF16)],
        compiler_params=pltpu.CompilerParams(vmem_limit_bytes=32 * MIB),
        cost_estimate=pl.CostEstimate(
            flops=1_000_000_000, bytes_accessed=8_000_000, transcendentals=0
        ),
        name="tokens",
    )(residual, own, from_prev, from_far, from_next, moe_gain[None, :], router, expert_ids)

    cores = [
        [(c // ring * 2 + h) * ring + c % ring for c in range(experts)] for h in range(2)
    ]

    def swap(rows):
        swapped = lax.all_to_all(
            rows.reshape(count, ROW, CELL),
            ("seq", "exp"),
            split_axis=0,
            concat_axis=0,
            tiled=True,
            axis_index_groups=cores,
        )
        return swapped.reshape(cells)

    unit = w_gate.shape[2]
    run_experts = pl.pallas_call(
        experts_kernel,
        in_specs=[vmem] + [hbm] * 6,
        out_specs=vmem,
        out_shape=jax.ShapeDtypeStruct(cells, BF16),
        scratch_shapes=[
            pltpu.VMEM(stage, F32),
            pltpu.VMEM((count, width), BF16),
            pltpu.VMEM((count, 2 * unit), BF16),
            pltpu.VMEM((8, 2, width, unit // 4), BF16),
            pltpu.VMEM((4, 2 * unit, width // 4), BF16),
            pltpu.SemaphoreType.DMA((8, 2)),
            pltpu.SemaphoreType.DMA((4, 2)),
        ],
        compiler_params=pltpu.CompilerParams(vmem_limit_bytes=60 * MIB),
        cost_estimate=pl.CostEstimate(
            flops=12 * count * width * unit,
            bytes_accessed=28_000_000,
            transcendentals=0,
        ),
        name="experts",
    )

    def combine(base, weight, rows, dtype):
        return pl.pallas_call(
            combine_kernel,
            out_shape=jax.ShapeDtypeStruct((share, width), dtype),
            scratch_shapes=[pltpu.VMEM(stage, F32)],
            compiler_params=pltpu.CompilerParams(vmem_limit_bytes=24 * MIB),
            cost_estimate=pl.CostEstimate(
                flops=500_000_000, bytes_accessed=4_000_000, transcendentals=0
            ),
            name="combine",
        )(base, weight, rows)

    arrivals = [swap(rows) for rows in outgoing]
    returned = [
        swap(
            run_experts(
                rows, w_gate[0], w_up[0], w_down[0], other_gate, other_up, other_down
            )
        )
        for rows in arrivals
    ]
    mixed = stream
    for i in range(CHUNKS):
        mixed = combine(mixed, weights[i], returned[i], BF16 if i == CHUNKS - 1 else F32)
    return mixed


def solution(mesh):
    return jax.shard_map(
        body,
        mesh=mesh,
        in_specs=(
            P("seq", "exp"),
            P("seq", "exp"),
            P("exp"),
            P("seq", "exp"),
            P("seq", "exp", None),
            P("seq", "exp", None),
            P("exp"),
            P("exp"),
            P("exp"),
            P("exp", None),
            P(("seq", "exp"), None),
            P(),
            P(),
            P(("seq", "exp"), None),
            P(("seq", "exp"), None, None),
            P(("seq", "exp"), None, None),
            P(("seq", "exp"), None, None),
        ),
        out_specs=P(("seq", "exp"), None),
        check_vma=False,
    )
```

```python
import functools

import jax
import jax.numpy as jnp
from jax import lax
from jax.experimental import pallas as pl
from jax.experimental.pallas import tpu as pltpu
from jax.sharding import PartitionSpec as P

P_SIZE = 64
NST = 128
G = 8
BLOCK = 256
PAIR = 2 * P_SIZE
STEP_PAIRS = 4
SLOTS = 14
CHUNKS = 2
ROW = 8
CELL = 256

EPS = 1e-06
F32 = jnp.float32
BF16 = jnp.bfloat16
MIB = 1024 * 1024


def dot(a, b):
    return jnp.dot(a, b, preferred_element_type=F32)


def lanes_of_first(shape):
    return lax.broadcasted_iota(jnp.int32, shape, 1) < P_SIZE


def columns_of(first_row, second_row):
    length = first_row.shape[1]
    rows = jnp.concatenate(
        [
            jnp.broadcast_to(first_row, (P_SIZE, length)),
            jnp.broadcast_to(second_row, (P_SIZE, length)),
        ],
        axis=0,
    )
    return rows.T


def lane_pair(first, second):
    return jnp.concatenate(
        [jnp.broadcast_to(first, (1, P_SIZE)), jnp.broadcast_to(second, (1, P_SIZE))], axis=1
    )


def split_pair(values):
    first = lanes_of_first(values.shape)
    zero = jnp.zeros_like(values)
    return jnp.concatenate([jnp.where(first, values, zero), jnp.where(first, zero, values)], axis=0)


def prep_kernel(raw_ref, bias_ref, decay_ref, out_ref):
    value = raw_ref[...] + bias_ref[...]
    size = jnp.maximum(value, 0.0) + jnp.log(1.0 + jnp.exp(-jnp.abs(value)))
    upto = jnp.where(
        lax.broadcasted_iota(jnp.int32, (BLOCK, BLOCK), 0)
        <= lax.broadcasted_iota(jnp.int32, (BLOCK, BLOCK), 1),
        1.0,
        0.0,
    ).astype(BF16)
    heads, length = size.shape
    for b in range(length // BLOCK):
        rows = slice(b * BLOCK, (b + 1) * BLOCK)
        rest = decay_ref[:, rows]
        terms = []
        for _ in range(3):
            terms.append(rest.astype(BF16))
            rest = rest - terms[-1].astype(F32)
        sums = dot(jnp.concatenate(terms, axis=0), upto)
        running = sums[:heads] + sums[heads : 2 * heads] + sums[2 * heads :]
        out_ref[0, :, rows] = running
        out_ref[1, :, rows] = size[:, rows]
        out_ref[2, :, rows] = jnp.exp(running[:, BLOCK - 1 :] - running) * size[:, rows]
        out_ref[3, :, rows] = jnp.exp(running)


def states_kernel(
    slot_ref,
    x_ref,
    prep_ref,
    m0,
    m1,
    m2,
    m3,
    fresh_hbm,
    send_hbm,
    maps,
    fresh_all,
    send_all,
    fresh_sem,
    send_sem,
):
    step = pl.program_id(0)
    steps = fresh_sem.shape[0]

    def out_copies(at):
        pairs = pl.ds(at * STEP_PAIRS, STEP_PAIRS)
        pieces = pl.ds(at * 2 * STEP_PAIRS, 2 * STEP_PAIRS)
        return [
            pltpu.make_async_copy(send_all.at[pieces], send_hbm.at[pieces], send_sem.at[at]),
            pltpu.make_async_copy(fresh_all.at[pairs], fresh_hbm.at[pairs], fresh_sem.at[at]),
        ]

    @pl.when(step == 0)
    def _():
        maps[0:2] = m0[...]
        maps[2:4] = m1[...]
        maps[4:6] = m2[...]
        maps[6:8] = m3[...]

    for p in range(STEP_PAIRS):
        slots = [slot_ref[step * 2 * STEP_PAIRS + 2 * p + i] for i in range(2)]
        x = x_ref[:, p * PAIR : (p + 1) * PAIR].astype(F32)
        weight = columns_of(prep_ref[2, 2 * p : 2 * p + 1, :], prep_ref[2, 2 * p + 1 : 2 * p + 2, :])
        scaled = (x * weight).astype(BF16)
        fresh = []
        for b in range(2):
            rows = slice(b * BLOCK, (b + 1) * BLOCK)
            both = split_pair(scaled[rows])
            left = jnp.concatenate([maps[slots[0], :, rows], maps[slots[1], :, rows]], axis=1)
            fresh.append(dot(left, both))
        ends = [
            lane_pair(
                prep_ref[3, 2 * p : 2 * p + 1, e - 1 : e],
                prep_ref[3, 2 * p + 1 : 2 * p + 2, e - 1 : e],
            )
            for e in (BLOCK, 2 * BLOCK)
        ]
        fresh_all[step * STEP_PAIRS + p] = fresh[0]
        final = (ends[1] * fresh[0] + fresh[1]).astype(BF16)
        decay = ends[0] * ends[1]
        high = decay.astype(BF16).astype(F32)
        row = lax.broadcasted_iota(jnp.int32, (8, PAIR), 0)
        tail = jnp.where(row == 0, high, jnp.where(row == 1, decay - high, 0.0)).astype(BF16)
        for i in range(2):
            piece = step * 2 * STEP_PAIRS + 2 * p + i
            send_all[piece, 0:64] = final[64 * i : 64 * (i + 1)]
            send_all[piece, 64:72] = tail
    for copy in out_copies(step):
        copy.start()

    @pl.when(step == steps - 1)
    def _():
        for at in range(steps):
            for copy in out_copies(at):
                copy.wait()


def scan_kernel(in_ref, out_ref):
    state = jnp.zeros((64, PAIR), F32)
    for j in range(in_ref.shape[0]):
        out_ref[j] = state.astype(BF16)
        tail = in_ref[j, 64:72].astype(F32)
        decay = tail[0:1] + tail[1:2]
        state = decay * state + in_ref[j, 0:64].astype(F32)


def within_kernel(
    slot_ref, x_ref, prep_ref, skip_ref, i0, i1, i2, i3, o0, o1, o2, o3, out_ref, scores
):
    step = pl.program_id(0)

    @pl.when(step == 0)
    def _():
        inputs = [ref.at[i] for ref in (i0, i1, i2, i3) for i in range(2)]
        outputs = [ref.at[i] for ref in (o0, o1, o2, o3) for i in range(2)]
        for g in range(G):
            for b in range(2):
                rows = slice(b * BLOCK, (b + 1) * BLOCK)
                scores[g, b] = dot(outputs[g][rows, :], inputs[g][:, rows])

    half = BLOCK // 2
    causal = lax.broadcasted_iota(jnp.int32, (half, half), 0) >= lax.broadcasted_iota(
        jnp.int32, (half, half), 1
    )
    for p in range(STEP_PAIRS):
        columns = slice(p * PAIR, (p + 1) * PAIR)
        slots = [slot_ref[step * 2 * STEP_PAIRS + 2 * p + i] for i in range(2)]
        for b in range(2):
            rows = slice(b * BLOCK, (b + 1) * BLOCK)
            x = x_ref[rows, columns]
            early, late = [], []
            for i in range(2):
                running = prep_ref[0, 2 * p + i : 2 * p + i + 1, rows]
                size = prep_ref[1, 2 * p + i : 2 * p + i + 1, rows]
                down = jnp.broadcast_to(running, (half, BLOCK)).T

                def tile(t, s, masked):
                    ts, ss = slice(t * half, (t + 1) * half), slice(s * half, (s + 1) * half)
                    spread = down[ts] - running[:, ss]
                    score = scores[slots[i], b, ts, ss]
                    value = score * jnp.exp(spread) * size[:, ss]
                    return (jnp.where(causal, value, 0.0) if masked else value).astype(BF16)

                early.append(tile(0, 0, True))
                late.append(tile(1, 0, False))
                late.append(tile(1, 1, True))
            both = split_pair(x)
            first = jnp.concatenate([both[0:half], both[BLOCK : BLOCK + half]], axis=0)
            skipped = skip_ref[:, columns] * x.astype(F32)
            top = dot(jnp.concatenate(early, axis=1), first)
            bottom = dot(jnp.concatenate(late, axis=1), both)
            out_ref[b * BLOCK : b * BLOCK + half, columns] = (top + skipped[0:half]).astype(BF16)
            out_ref[b * BLOCK + half : (b + 1) * BLOCK, columns] = (bottom + skipped[half:]).astype(
                BF16
            )


def project_kernel(
    slot_ref,
    place_ref,
    within_ref,
    prep_ref,
    gain_ref,
    enter_ref,
    fresh_ref,
    o0,
    o1,
    o2,
    o3,
    w_ref,
    own_ref,
    up_ref,
    far_ref,
    down_ref,
    maps,
    normed,
    total,
):
    step = pl.program_id(0)

    @pl.when(step == 0)
    def _():
        maps[0:2] = o0[...]
        maps[2:4] = o1[...]
        maps[4:6] = o2[...]
        maps[6:8] = o3[...]
        total[...] = jnp.zeros_like(total)

    same = (
        lax.broadcasted_iota(jnp.int32, (2 * PAIR, PAIR), 0) % PAIR // P_SIZE
        == lax.broadcasted_iota(jnp.int32, (2 * PAIR, PAIR), 1) // P_SIZE
    )
    summing = jnp.where(same, 1.0, 0.0).astype(BF16)
    for p in range(STEP_PAIRS):
        columns = slice(p * PAIR, (p + 1) * PAIR)
        slots = [slot_ref[step * 2 * STEP_PAIRS + 2 * p + i] for i in range(2)]
        growth = columns_of(prep_ref[3, 2 * p : 2 * p + 1, :], prep_ref[3, 2 * p + 1 : 2 * p + 2, :])
        first_end = lane_pair(
            prep_ref[3, 2 * p : 2 * p + 1, BLOCK - 1 : BLOCK], prep_ref[3, 2 * p + 1 : 2 * p + 2, BLOCK - 1 : BLOCK]
        )
        arriving = enter_ref[p].astype(F32)
        entering = [arriving, first_end * arriving + fresh_ref[p]]
        for b in range(2):
            rows = slice(b * BLOCK, (b + 1) * BLOCK)
            left = jnp.concatenate([maps[slots[0], rows, :], maps[slots[1], rows, :]], axis=1)
            carried = dot(left, split_pair(entering[b].astype(BF16)))
            y = within_ref[rows, columns].astype(F32) + carried * growth[rows]
            square = y * y
            high = square.astype(BF16)
            low = (square - high.astype(F32)).astype(BF16)
            mean = dot(jnp.concatenate([high, low], axis=1), summing) * (1.0 / P_SIZE)
            normed[rows, columns] = (y * lax.rsqrt(mean + EPS) * gain_ref[:, columns]).astype(BF16)
    total[...] += dot(normed[...], w_ref[...])

    @pl.when(step == pl.num_programs(0) - 1)
    def _():
        share = own_ref.shape[0]

        def rows_for(offset):
            place = lax.rem(place_ref[0] + offset, 4)
            rows = total[pl.ds(pl.multiple_of(place * share, share), share), :]
            return rows.astype(BF16)

        own_ref[...] = rows_for(0)
        up_ref[...] = rows_for(1)
        far_ref[...] = rows_for(2)
        down_ref[...] = rows_for(3)


def put_cells(stage, j, value):
    for h in range(2):
        stage[h, pl.ds(j, value.shape[0], stride=ROW), :] = value[:, h * 128 : (h + 1) * 128]


def take_cells(stage, j, count):
    return jnp.concatenate(
        [stage[h, pl.ds(j, count, stride=ROW), :] for h in range(2)], axis=1
    ).astype(BF16)


def fill_stage(stage, rows_ref):
    for h in range(2):
        stage[h] = rows_ref[:, h * 128 : (h + 1) * 128].astype(F32)


def drain_stage(stage, rows_ref):
    for h in range(2):
        rows_ref[:, h * 128 : (h + 1) * 128] = stage[h].astype(BF16)


def placed_in(ranks, i):
    chunk = SLOTS // CHUNKS
    slot = (lax.broadcasted_iota(jnp.int32, ranks.shape, 1) % chunk).astype(F32)
    return ranks == slot + float(i * chunk)


def send_rows(ranks, tokens, i, stage, out_ref):
    pick = jnp.where(placed_in(ranks, i), 1.0, 0.0).T.astype(BF16)
    for j in range(ROW):
        put_cells(stage, j, dot(pick, tokens[:, j * CELL : (j + 1) * CELL]))
    drain_stage(stage, out_ref)


def tokens_kernel(
    residual_ref,
    own_ref,
    prev_ref,
    far_ref,
    next_ref,
    gain_ref,
    router_ref,
    ids_ref,
    stream_ref,
    tokens,
    wide_ref,
    out_ref,
    stage,
    *,
    ring,
):
    share, width = stream_ref.shape
    stream = (
        residual_ref[...].astype(F32)
        + own_ref[...].astype(F32)
        + prev_ref[...].astype(F32)
        + far_ref[...].astype(F32)
        + next_ref[...].astype(F32)
    )
    stream_ref[...] = stream
    square = jnp.mean(stream * stream, axis=-1, keepdims=True)
    tokens[...] = (stream * lax.rsqrt(square + EPS) * gain_ref[...]).astype(BF16)
    experts = router_ref.shape[1]
    place = lax.broadcasted_iota(jnp.int32, (share, experts), 1)
    hosted = place % ring * (experts // ring) + place // ring
    routed = jnp.zeros((share, experts), F32)
    for k in range(ids_ref.shape[1]):
        routed = routed + jnp.where(ids_ref[:, k : k + 1] == hosted, 1.0, 0.0)
    earlier = jnp.where(
        lax.broadcasted_iota(jnp.int32, (share, share), 0)
        > lax.broadcasted_iota(jnp.int32, (share, share), 1),
        1.0,
        0.0,
    ).astype(BF16)
    rank = dot(earlier, routed.astype(BF16))
    key = jnp.where(routed > 0.5, rank, -1.0).astype(BF16)
    logits = dot(tokens[...], router_ref[...])
    weight = 1.0 / (1.0 + jnp.exp(-logits))
    high = weight.astype(BF16)
    low = (weight - high.astype(F32)).astype(BF16)
    chunk = SLOTS // CHUNKS
    rows = experts * chunk
    spread = jnp.where(
        lax.broadcasted_iota(jnp.int32, (experts, rows), 0)
        == lax.broadcasted_iota(jnp.int32, (experts, rows), 1) // chunk,
        1.0,
        0.0,
    ).astype(BF16)
    wide = dot(jnp.concatenate([key, high, low], axis=0), spread)
    wide_ref[...] = wide
    send_rows(wide[:share], tokens, 0, stage, out_ref)


def later_kernel(tokens, wide_ref, weight_ref, *rest):
    out_refs, stage = rest[:-1], rest[-1]
    share = tokens.shape[0]
    ranks = wide_ref[:share]
    for i in range(CHUNKS):
        placed = placed_in(ranks, i)
        weight_ref[i, :share] = jnp.where(placed, wide_ref[share : 2 * share], 0.0).astype(BF16)
        weight_ref[i, share:] = jnp.where(placed, wide_ref[2 * share :], 0.0).astype(BF16)
    for i, out_ref in enumerate(out_refs):
        send_rows(ranks, tokens, i + 1, stage, out_ref)


def experts_kernel(
    x_ref,
    g0,
    u0,
    d0,
    g1,
    u1,
    d1,
    out_ref,
    stage,
    rows,
    hidden,
    wide,
    deep,
    wide_sem,
    deep_sem,
):
    count, width = rows.shape
    unit = g0.shape[1]
    n_wide, n_deep = wide.shape[0], deep.shape[0]
    wide_step, deep_step = 2 * unit // n_wide, width // n_deep
    halves = [(g0, u0, d0), (g1, u1, d1)]

    def copies(s):
        if s < n_wide:
            half = halves[s * wide_step // unit]
            columns = pl.ds(s * wide_step % unit, wide_step)
            return [
                pltpu.make_async_copy(half[i].at[:, columns], wide.at[s, i], wide_sem.at[s, i])
                for i in range(2)
            ]
        s -= n_wide
        columns = pl.ds(s * deep_step, deep_step)
        return [
            pltpu.make_async_copy(
                halves[i][2].at[:, columns], deep.at[s, pl.ds(i * unit, unit)], deep_sem.at[s, i]
            )
            for i in range(2)
        ]

    total_steps = n_wide + n_deep
    ahead = 3
    for s in range(ahead):
        for copy in copies(s):
            copy.start()
    fill_stage(stage, x_ref)
    for j in range(ROW):
        rows[:, j * CELL : (j + 1) * CELL] = take_cells(stage, j, count)
    for s in range(total_steps):
        if s + ahead < total_steps:
            for copy in copies(s + ahead):
                copy.start()
        for copy in copies(s):
            copy.wait()
        if s < n_wide:
            gated = dot(rows[...], wide[s, 0])
            raised = dot(rows[...], wide[s, 1])
            hidden[:, s * wide_step : (s + 1) * wide_step] = (
                gated / (1.0 + jnp.exp(-gated)) * raised
            ).astype(BF16)
        else:
            d = s - n_wide
            for c in range(deep_step // CELL):
                part = dot(hidden[...], deep[d, :, c * CELL : (c + 1) * CELL])
                put_cells(stage, d * (deep_step // CELL) + c, part)
    drain_stage(stage, out_ref)


def combine_kernel(base_ref, weight_ref, rows_ref, out_ref, stage):
    share = base_ref.shape[0]
    count = weight_ref.shape[1]
    fill_stage(stage, rows_ref)
    for j in range(ROW):
        columns = slice(j * CELL, (j + 1) * CELL)
        part = dot(weight_ref[...], take_cells(stage, j, count))
        out_ref[:, columns] = (base_ref[:, columns] + part[:share] + part[share:]).astype(
            out_ref.dtype
        )


def whole(shape):
    return pl.BlockSpec(shape, lambda s, *_: (0,) * len(shape))


def params(mib=60):
    return pltpu.CompilerParams(
        dimension_semantics=("arbitrary",), vmem_limit_bytes=mib * MIB
    )


def body(
    ssd_input,
    dt_raw,
    dt_bias,
    log_decay,
    input_map,
    output_map,
    head_group,
    d_skip,
    norm_gain,
    w_out,
    residual,
    moe_gain,
    w_router,
    expert_ids,
    w_gate,
    w_up,
    w_down,
):
    length = ssd_input.shape[0]
    heads = dt_raw.shape[1]
    width = w_out.shape[1]
    share = residual.shape[0]
    me = lax.axis_index("exp")
    ring = lax.axis_size("exp")
    seq_count = lax.axis_size("seq")
    nxt = [(i, (i + 1) % ring) for i in range(ring)]
    prv = [(i, (i - 1) % ring) for i in range(ring)]
    partner = [(i, i ^ 1) for i in range(seq_count)]
    steps = heads // (2 * STEP_PAIRS)
    columns = STEP_PAIRS * PAIR

    opposite = [(i, (i + 2) % ring) for i in range(ring)]

    def gather_maps(own):
        far = lax.ppermute(own, "exp", opposite)
        return own, lax.ppermute(own, "exp", prv), far, lax.ppermute(own, "exp", nxt)

    in_maps = gather_maps(input_map.transpose(1, 2, 0))
    out_maps = gather_maps(output_map.transpose(1, 0, 2))
    slot = (lax.rem(head_group // 2 - me + ring, ring) * 2 + head_group % 2).astype(jnp.int32)

    prep = pl.pallas_call(
        prep_kernel,
        out_shape=jax.ShapeDtypeStruct((4, heads, length), F32),
        compiler_params=pltpu.CompilerParams(vmem_limit_bytes=16 * MIB),
        cost_estimate=pl.CostEstimate(
            flops=30_000_000, bytes_accessed=400_000, transcendentals=100_000
        ),
        name="prep",
    )(dt_raw.T, dt_bias[:, None], log_decay.T)
    skip_lanes = jnp.repeat(d_skip, P_SIZE)[None, :]
    gain_lanes = norm_gain[None, :]

    x_spec = pl.BlockSpec((length, columns), lambda s, *_: (0, s))
    prep_spec = pl.BlockSpec((4, 2 * STEP_PAIRS, length), lambda s, *_: (0, s, 0))
    lane_spec = pl.BlockSpec((1, columns), lambda s, *_: (0, s))
    state_spec = pl.BlockSpec((STEP_PAIRS, NST, PAIR), lambda s, *_: (s, 0, 0))
    in_specs = [whole((2, NST, length))] * 4
    out_specs = [whole((2, length, NST))] * 4

    fresh, sending = pl.pallas_call(
        states_kernel,
        grid_spec=pltpu.PrefetchScalarGridSpec(
            num_scalar_prefetch=1,
            grid=(steps,),
            in_specs=[x_spec, prep_spec] + in_specs,
            out_specs=[pl.BlockSpec(memory_space=pltpu.HBM)] * 2,
            scratch_shapes=[
                pltpu.VMEM((G, NST, length), BF16),
                pltpu.VMEM((heads // 2, NST, PAIR), F32),
                pltpu.VMEM((heads, 72, PAIR), BF16),
                pltpu.SemaphoreType.DMA((steps,)),
                pltpu.SemaphoreType.DMA((steps,)),
            ],
        ),
        out_shape=[
            jax.ShapeDtypeStruct((heads // 2, NST, PAIR), F32),
            jax.ShapeDtypeStruct((heads, 72, PAIR), BF16),
        ],
        compiler_params=params(16),
        cost_estimate=pl.CostEstimate(
            flops=600_000_000, bytes_accessed=5_000_000, transcendentals=0
        ),
        name="states",
    )(slot, ssd_input, prep, *in_maps)

    sending, own_gate = lax.optimization_barrier((sending, w_gate[0]))
    other_gate = lax.ppermute(own_gate, "seq", partner)
    other_up = lax.ppermute(w_up[0], "seq", partner)
    other_down = lax.ppermute(w_down[0], "seq", partner)

    arrived = lax.all_to_all(sending, "seq", split_axis=0, concat_axis=0, tiled=True)
    prefix = pl.pallas_call(
        scan_kernel,
        out_shape=jax.ShapeDtypeStruct((seq_count, 64, PAIR), BF16),
        compiler_params=pltpu.CompilerParams(vmem_limit_bytes=16 * MIB),
        name="scan",
    )(arrived)
    entering = lax.all_to_all(prefix, "seq", split_axis=0, concat_axis=0, tiled=True)
    entering = entering.reshape(heads // 2, NST, PAIR)

    within = pl.pallas_call(
        within_kernel,
        grid_spec=pltpu.PrefetchScalarGridSpec(
            num_scalar_prefetch=1,
            grid=(steps,),
            in_specs=[x_spec, prep_spec, lane_spec] + in_specs + out_specs,
            out_specs=x_spec,
            scratch_shapes=[pltpu.VMEM((G, 2, BLOCK, BLOCK), F32)],
        ),
        out_shape=jax.ShapeDtypeStruct(ssd_input.shape, BF16),
        compiler_params=params(),
        cost_estimate=pl.CostEstimate(
            flops=12_000_000_000, bytes_accessed=8_000_000, transcendentals=4_000_000
        ),
        name="within",
    )(slot, ssd_input, prep, skip_lanes, *in_maps, *out_maps)

    vmem = pl.BlockSpec(memory_space=pltpu.VMEM)
    hbm = pl.BlockSpec(memory_space=pl.ANY)
    within, other_gate = lax.optimization_barrier((within, other_gate))
    own, up, far, down = pl.pallas_call(
        project_kernel,
        grid_spec=pltpu.PrefetchScalarGridSpec(
            num_scalar_prefetch=2,
            grid=(steps,),
            in_specs=[x_spec, prep_spec, lane_spec, state_spec, state_spec]
            + out_specs
            + [pl.BlockSpec((columns, width), lambda s, *_: (s, 0))],
            out_specs=[whole((share, width))] * 4,
            scratch_shapes=[
                pltpu.VMEM((G, length, NST), BF16),
                pltpu.VMEM((length, columns), BF16),
                pltpu.VMEM((length, width), F32),
            ],
        ),
        out_shape=[jax.ShapeDtypeStruct((share, width), BF16)] * 4,
        compiler_params=params(),
        cost_estimate=pl.CostEstimate(
            flops=6_000_000_000, bytes_accessed=16_000_000, transcendentals=0
        ),
        name="project",
    )(slot, me[None].astype(jnp.int32), within, prep, gain_lanes, entering, fresh, *out_maps, w_out)

    from_prev = lax.ppermute(up, "exp", nxt)
    from_far = lax.ppermute(far, "exp", opposite)
    from_next = lax.ppermute(down, "exp", prv)

    experts = w_router.shape[1]
    per_group = experts // ring
    router = w_router.reshape(-1, ring, per_group).swapaxes(1, 2).reshape(-1, experts)
    chunk = SLOTS // CHUNKS
    count = experts * chunk
    cells = (count * ROW, CELL)
    stage = (2, count * ROW, CELL // 2)
    stream, tokens, wide, first_rows = pl.pallas_call(
        functools.partial(tokens_kernel, ring=ring),
        out_shape=[
            jax.ShapeDtypeStruct((share, width), F32),
            jax.ShapeDtypeStruct((share, width), BF16),
            jax.ShapeDtypeStruct((3 * share, count), F32),
            jax.ShapeDtypeStruct(cells, BF16),
        ],
        scratch_shapes=[pltpu.VMEM(stage, F32)],
        compiler_params=pltpu.CompilerParams(vmem_limit_bytes=32 * MIB),
        cost_estimate=pl.CostEstimate(
            flops=600_000_000, bytes_accessed=6_000_000, transcendentals=0
        ),
        name="tokens",
    )(residual, own, from_prev, from_far, from_next, moe_gain[None, :], router, expert_ids)
    weights, *later_rows = pl.pallas_call(
        later_kernel,
        out_shape=[jax.ShapeDtypeStruct((CHUNKS, 2 * share, count), BF16)]
        + [jax.ShapeDtypeStruct(cells, BF16)] * (CHUNKS - 1),
        scratch_shapes=[pltpu.VMEM(stage, F32)],
        compiler_params=pltpu.CompilerParams(vmem_limit_bytes=32 * MIB),
        cost_estimate=pl.CostEstimate(
            flops=500_000_000, bytes_accessed=6_000_000, transcendentals=0
        ),
        name="later",
    )(tokens, wide)
    outgoing = [first_rows, *later_rows]

    cores = [
        [(c // ring * 2 + h) * ring + c % ring for c in range(experts)] for h in range(2)
    ]

    def swap(rows):
        swapped = lax.all_to_all(
            rows.reshape(count, ROW, CELL),
            ("seq", "exp"),
            split_axis=0,
            concat_axis=0,
            tiled=True,
            axis_index_groups=cores,
        )
        return swapped.reshape(cells)

    unit = w_gate.shape[2]
    run_experts = pl.pallas_call(
        experts_kernel,
        in_specs=[vmem] + [hbm] * 6,
        out_specs=vmem,
        out_shape=jax.ShapeDtypeStruct(cells, BF16),
        scratch_shapes=[
            pltpu.VMEM(stage, F32),
            pltpu.VMEM((count, width), BF16),
            pltpu.VMEM((count, 2 * unit), BF16),
            pltpu.VMEM((8, 2, width, unit // 4), BF16),
            pltpu.VMEM((4, 2 * unit, width // 4), BF16),
            pltpu.SemaphoreType.DMA((8, 2)),
            pltpu.SemaphoreType.DMA((4, 2)),
        ],
        compiler_params=pltpu.CompilerParams(vmem_limit_bytes=60 * MIB),
        cost_estimate=pl.CostEstimate(
            flops=12 * count * width * unit,
            bytes_accessed=28_000_000,
            transcendentals=0,
        ),
        name="experts",
    )

    def combine(base, weight, rows, dtype):
        return pl.pallas_call(
            combine_kernel,
            out_shape=jax.ShapeDtypeStruct((share, width), dtype),
            scratch_shapes=[pltpu.VMEM(stage, F32)],
            compiler_params=pltpu.CompilerParams(vmem_limit_bytes=24 * MIB),
            cost_estimate=pl.CostEstimate(
                flops=500_000_000, bytes_accessed=4_000_000, transcendentals=0
            ),
            name="combine",
        )(base, weight, rows)

    arrivals = [swap(rows) for rows in outgoing]
    returned = [
        swap(
            run_experts(
                rows, w_gate[0], w_up[0], w_down[0], other_gate, other_up, other_down
            )
        )
        for rows in arrivals
    ]
    mixed = stream
    for i in range(CHUNKS):
        mixed = combine(mixed, weights[i], returned[i], BF16 if i == CHUNKS - 1 else F32)
    return mixed


def solution(mesh):
    return jax.shard_map(
        body,
        mesh=mesh,
        in_specs=(
            P("seq", "exp"),
            P("seq", "exp"),
            P("exp"),
            P("seq", "exp"),
            P("seq", "exp", None),
            P("seq", "exp", None),
            P("exp"),
            P("exp"),
            P("exp"),
            P("exp", None),
            P(("seq", "exp"), None),
            P(),
            P(),
            P(("seq", "exp"), None),
            P(("seq", "exp"), None, None),
            P(("seq", "exp"), None, None),
            P(("seq", "exp"), None, None),
        ),
        out_specs=P(("seq", "exp"), None),
        check_vma=False,
    )
```

```python
import functools

import jax
import jax.numpy as jnp
from jax import lax
from jax.experimental import pallas as pl
from jax.experimental.pallas import tpu as pltpu
from jax.sharding import PartitionSpec as P

P_SIZE = 64
NST = 128
G = 8
BLOCK = 256
PAIR = 2 * P_SIZE
STEP_PAIRS = 4
SLOTS = 14
CHUNKS = 2
ROW = 8
CELL = 256

EPS = 1e-06
F32 = jnp.float32
BF16 = jnp.bfloat16
MIB = 1024 * 1024


def dot(a, b):
    return jnp.dot(a, b, preferred_element_type=F32)


def lanes_of_first(shape):
    return lax.broadcasted_iota(jnp.int32, shape, 1) < P_SIZE


def columns_of(first_row, second_row):
    length = first_row.shape[1]
    rows = jnp.concatenate(
        [
            jnp.broadcast_to(first_row, (P_SIZE, length)),
            jnp.broadcast_to(second_row, (P_SIZE, length)),
        ],
        axis=0,
    )
    return rows.T


def lane_pair(first, second):
    return jnp.concatenate(
        [jnp.broadcast_to(first, (1, P_SIZE)), jnp.broadcast_to(second, (1, P_SIZE))], axis=1
    )


def split_pair(values):
    first = lanes_of_first(values.shape)
    zero = jnp.zeros_like(values)
    return jnp.concatenate([jnp.where(first, values, zero), jnp.where(first, zero, values)], axis=0)


def prep_kernel(raw_ref, bias_ref, decay_ref, out_ref):
    value = raw_ref[...] + bias_ref[...]
    size = jnp.maximum(value, 0.0) + jnp.log(1.0 + jnp.exp(-jnp.abs(value)))
    upto = jnp.where(
        lax.broadcasted_iota(jnp.int32, (BLOCK, BLOCK), 0)
        <= lax.broadcasted_iota(jnp.int32, (BLOCK, BLOCK), 1),
        1.0,
        0.0,
    ).astype(BF16)
    heads, length = size.shape
    for b in range(length // BLOCK):
        rows = slice(b * BLOCK, (b + 1) * BLOCK)
        rest = decay_ref[:, rows]
        terms = []
        for _ in range(3):
            terms.append(rest.astype(BF16))
            rest = rest - terms[-1].astype(F32)
        sums = dot(jnp.concatenate(terms, axis=0), upto)
        running = sums[:heads] + sums[heads : 2 * heads] + sums[2 * heads :]
        out_ref[0, :, rows] = running
        out_ref[1, :, rows] = size[:, rows]
        out_ref[2, :, rows] = jnp.exp(running[:, BLOCK - 1 :] - running) * size[:, rows]
        out_ref[3, :, rows] = jnp.exp(running)


def states_kernel(
    slot_ref,
    x_ref,
    prep_ref,
    m0,
    m1,
    m2,
    m3,
    fresh_hbm,
    send_hbm,
    maps,
    fresh_all,
    send_all,
    fresh_sem,
    send_sem,
):
    step = pl.program_id(0)
    steps = fresh_sem.shape[0]

    def out_copies(at):
        pairs = pl.ds(at * STEP_PAIRS, STEP_PAIRS)
        pieces = pl.ds(at * 2 * STEP_PAIRS, 2 * STEP_PAIRS)
        return [
            pltpu.make_async_copy(send_all.at[pieces], send_hbm.at[pieces], send_sem.at[at]),
            pltpu.make_async_copy(fresh_all.at[pairs], fresh_hbm.at[pairs], fresh_sem.at[at]),
        ]

    @pl.when(step == 0)
    def _():
        maps[0:2] = m0[...]
        maps[2:4] = m1[...]
        maps[4:6] = m2[...]
        maps[6:8] = m3[...]

    for p in range(STEP_PAIRS):
        slots = [slot_ref[step * 2 * STEP_PAIRS + 2 * p + i] for i in range(2)]
        x = x_ref[:, p * PAIR : (p + 1) * PAIR].astype(F32)
        weight = columns_of(prep_ref[2, 2 * p : 2 * p + 1, :], prep_ref[2, 2 * p + 1 : 2 * p + 2, :])
        scaled = (x * weight).astype(BF16)
        fresh = []
        for b in range(2):
            rows = slice(b * BLOCK, (b + 1) * BLOCK)
            both = split_pair(scaled[rows])
            left = jnp.concatenate([maps[slots[0], :, rows], maps[slots[1], :, rows]], axis=1)
            fresh.append(dot(left, both))
        ends = [
            lane_pair(
                prep_ref[3, 2 * p : 2 * p + 1, e - 1 : e],
                prep_ref[3, 2 * p + 1 : 2 * p + 2, e - 1 : e],
            )
            for e in (BLOCK, 2 * BLOCK)
        ]
        fresh_all[step * STEP_PAIRS + p] = fresh[0].astype(BF16)
        final = (ends[1] * fresh[0] + fresh[1]).astype(BF16)
        decay = ends[0] * ends[1]
        high = decay.astype(BF16).astype(F32)
        row = lax.broadcasted_iota(jnp.int32, (8, PAIR), 0)
        tail = jnp.where(row == 0, high, jnp.where(row == 1, decay - high, 0.0)).astype(BF16)
        for i in range(2):
            piece = step * 2 * STEP_PAIRS + 2 * p + i
            send_all[piece, 0:64] = final[64 * i : 64 * (i + 1)]
            send_all[piece, 64:72] = tail
    for copy in out_copies(step):
        copy.start()

    @pl.when(step == steps - 1)
    def _():
        for at in range(steps):
            for copy in out_copies(at):
                copy.wait()


def scan_kernel(in_ref, out_ref):
    state = jnp.zeros((64, PAIR), F32)
    for j in range(in_ref.shape[0]):
        out_ref[j] = state.astype(BF16)
        tail = in_ref[j, 64:72].astype(F32)
        decay = tail[0:1] + tail[1:2]
        state = decay * state + in_ref[j, 0:64].astype(F32)


def within_kernel(
    slot_ref, x_ref, prep_ref, skip_ref, i0, i1, i2, i3, o0, o1, o2, o3, out_ref, scores
):
    step = pl.program_id(0)

    @pl.when(step == 0)
    def _():
        inputs = [ref.at[i] for ref in (i0, i1, i2, i3) for i in range(2)]
        outputs = [ref.at[i] for ref in (o0, o1, o2, o3) for i in range(2)]
        for g in range(G):
            for b in range(2):
                rows = slice(b * BLOCK, (b + 1) * BLOCK)
                scores[g, b] = dot(outputs[g][rows, :], inputs[g][:, rows])

    half = BLOCK // 2
    causal = lax.broadcasted_iota(jnp.int32, (half, half), 0) >= lax.broadcasted_iota(
        jnp.int32, (half, half), 1
    )
    for p in range(STEP_PAIRS):
        columns = slice(p * PAIR, (p + 1) * PAIR)
        slots = [slot_ref[step * 2 * STEP_PAIRS + 2 * p + i] for i in range(2)]
        for b in range(2):
            rows = slice(b * BLOCK, (b + 1) * BLOCK)
            x = x_ref[rows, columns]
            early, late = [], []
            for i in range(2):
                running = prep_ref[0, 2 * p + i : 2 * p + i + 1, rows]
                size = prep_ref[1, 2 * p + i : 2 * p + i + 1, rows]
                down = jnp.broadcast_to(running, (half, BLOCK)).T

                def tile(t, s, masked):
                    ts, ss = slice(t * half, (t + 1) * half), slice(s * half, (s + 1) * half)
                    spread = down[ts] - running[:, ss]
                    score = scores[slots[i], b, ts, ss]
                    value = score * jnp.exp(spread) * size[:, ss]
                    return (jnp.where(causal, value, 0.0) if masked else value).astype(BF16)

                early.append(tile(0, 0, True))
                late.append(tile(1, 0, False))
                late.append(tile(1, 1, True))
            both = split_pair(x)
            first = jnp.concatenate([both[0:half], both[BLOCK : BLOCK + half]], axis=0)
            skipped = skip_ref[:, columns] * x.astype(F32)
            top = dot(jnp.concatenate(early, axis=1), first)
            bottom = dot(jnp.concatenate(late, axis=1), both)
            out_ref[b * BLOCK : b * BLOCK + half, columns] = (top + skipped[0:half]).astype(BF16)
            out_ref[b * BLOCK + half : (b + 1) * BLOCK, columns] = (bottom + skipped[half:]).astype(
                BF16
            )


def project_kernel(
    slot_ref,
    place_ref,
    within_ref,
    prep_ref,
    gain_ref,
    enter_ref,
    fresh_ref,
    o0,
    o1,
    o2,
    o3,
    w_ref,
    own_ref,
    up_ref,
    far_ref,
    down_ref,
    maps,
    normed,
    total,
):
    step = pl.program_id(0)

    @pl.when(step == 0)
    def _():
        maps[0:2] = o0[...]
        maps[2:4] = o1[...]
        maps[4:6] = o2[...]
        maps[6:8] = o3[...]
        total[...] = jnp.zeros_like(total)

    same = (
        lax.broadcasted_iota(jnp.int32, (2 * PAIR, PAIR), 0) % PAIR // P_SIZE
        == lax.broadcasted_iota(jnp.int32, (2 * PAIR, PAIR), 1) // P_SIZE
    )
    summing = jnp.where(same, 1.0, 0.0).astype(BF16)
    for p in range(STEP_PAIRS):
        columns = slice(p * PAIR, (p + 1) * PAIR)
        slots = [slot_ref[step * 2 * STEP_PAIRS + 2 * p + i] for i in range(2)]
        growth = columns_of(prep_ref[3, 2 * p : 2 * p + 1, :], prep_ref[3, 2 * p + 1 : 2 * p + 2, :])
        first_end = lane_pair(
            prep_ref[3, 2 * p : 2 * p + 1, BLOCK - 1 : BLOCK], prep_ref[3, 2 * p + 1 : 2 * p + 2, BLOCK - 1 : BLOCK]
        )
        arriving = enter_ref[p].astype(F32)
        entering = [arriving, first_end * arriving + fresh_ref[p].astype(F32)]
        for b in range(2):
            rows = slice(b * BLOCK, (b + 1) * BLOCK)
            left = jnp.concatenate([maps[slots[0], rows, :], maps[slots[1], rows, :]], axis=1)
            carried = dot(left, split_pair(entering[b].astype(BF16)))
            y = within_ref[rows, columns].astype(F32) + carried * growth[rows]
            square = y * y
            high = square.astype(BF16)
            low = (square - high.astype(F32)).astype(BF16)
            mean = dot(jnp.concatenate([high, low], axis=1), summing) * (1.0 / P_SIZE)
            normed[rows, columns] = (y * lax.rsqrt(mean + EPS) * gain_ref[:, columns]).astype(BF16)
    total[...] += dot(normed[...], w_ref[...])

    @pl.when(step == pl.num_programs(0) - 1)
    def _():
        share = own_ref.shape[0]

        def rows_for(offset):
            place = lax.rem(place_ref[0] + offset, 4)
            rows = total[pl.ds(pl.multiple_of(place * share, share), share), :]
            return rows.astype(BF16)

        own_ref[...] = rows_for(0)
        up_ref[...] = rows_for(1)
        far_ref[...] = rows_for(2)
        down_ref[...] = rows_for(3)


def put_cells(stage, j, value):
    for h in range(2):
        stage[h, pl.ds(j, value.shape[0], stride=ROW), :] = value[:, h * 128 : (h + 1) * 128]


def take_cells(stage, j, count):
    return jnp.concatenate(
        [stage[h, pl.ds(j, count, stride=ROW), :] for h in range(2)], axis=1
    ).astype(BF16)


def fill_stage(stage, rows_ref):
    for h in range(2):
        stage[h] = rows_ref[:, h * 128 : (h + 1) * 128].astype(F32)


def drain_stage(stage, rows_ref):
    for h in range(2):
        rows_ref[:, h * 128 : (h + 1) * 128] = stage[h].astype(BF16)


def tokens_kernel(
    residual_ref,
    own_ref,
    prev_ref,
    next_ref,
    far_ref,
    gain_ref,
    router_ref,
    ids_ref,
    stream_ref,
    weight_ref,
    *rest,
    ring,
):
    out_refs, (stage, tokens) = rest[:-2], rest[-2:]
    share, width = stream_ref.shape
    stream = (
        residual_ref[...].astype(F32)
        + own_ref[...].astype(F32)
        + prev_ref[...].astype(F32)
        + far_ref[...].astype(F32)
        + next_ref[...].astype(F32)
    )
    stream_ref[...] = stream
    square = jnp.mean(stream * stream, axis=-1, keepdims=True)
    tokens[...] = (stream * lax.rsqrt(square + EPS) * gain_ref[...]).astype(BF16)
    experts = router_ref.shape[1]
    place = lax.broadcasted_iota(jnp.int32, (share, experts), 1)
    hosted = place % ring * (experts // ring) + place // ring
    routed = jnp.zeros((share, experts), F32)
    for k in range(ids_ref.shape[1]):
        routed = routed + jnp.where(ids_ref[:, k : k + 1] == hosted, 1.0, 0.0)
    earlier = jnp.where(
        lax.broadcasted_iota(jnp.int32, (share, share), 0)
        > lax.broadcasted_iota(jnp.int32, (share, share), 1),
        1.0,
        0.0,
    ).astype(BF16)
    rank = dot(earlier, routed.astype(BF16))
    key = jnp.where(routed > 0.5, rank, -1.0).astype(BF16)
    logits = dot(tokens[...], router_ref[...])
    weight = 1.0 / (1.0 + jnp.exp(-logits))
    high = weight.astype(BF16)
    low = (weight - high.astype(F32)).astype(BF16)
    chunk = SLOTS // CHUNKS
    rows = experts * chunk
    spread = jnp.where(
        lax.broadcasted_iota(jnp.int32, (experts, rows), 0)
        == lax.broadcasted_iota(jnp.int32, (experts, rows), 1) // chunk,
        1.0,
        0.0,
    ).astype(BF16)
    wide = dot(jnp.concatenate([key, high, low], axis=0), spread)
    ranks, highs, lows = wide[:share], wide[share : 2 * share], wide[2 * share :]
    slot = (lax.broadcasted_iota(jnp.int32, (share, rows), 1) % chunk).astype(F32)
    for i in range(CHUNKS):
        placed = ranks == slot + float(i * chunk)
        weight_ref[i, :share] = jnp.where(placed, highs, 0.0).astype(BF16)
        weight_ref[i, share:] = jnp.where(placed, lows, 0.0).astype(BF16)
        pick = jnp.where(placed, 1.0, 0.0).T.astype(BF16)
        for j in range(ROW):
            put_cells(stage, j, dot(pick, tokens[:, j * CELL : (j + 1) * CELL]))
        drain_stage(stage, out_refs[i])


def experts_kernel(
    x_ref,
    g0,
    u0,
    d0,
    g1,
    u1,
    d1,
    out_ref,
    stage,
    rows,
    hidden,
    wide,
    deep,
    wide_sem,
    deep_sem,
):
    count, width = rows.shape
    unit = g0.shape[1]
    n_wide, n_deep = wide.shape[0], deep.shape[0]
    wide_step, deep_step = 2 * unit // n_wide, width // n_deep
    halves = [(g0, u0, d0), (g1, u1, d1)]

    def copies(s):
        if s < n_wide:
            half = halves[s * wide_step // unit]
            columns = pl.ds(s * wide_step % unit, wide_step)
            return [
                pltpu.make_async_copy(half[i].at[:, columns], wide.at[s, i], wide_sem.at[s, i])
                for i in range(2)
            ]
        s -= n_wide
        columns = pl.ds(s * deep_step, deep_step)
        return [
            pltpu.make_async_copy(
                halves[i][2].at[:, columns], deep.at[s, pl.ds(i * unit, unit)], deep_sem.at[s, i]
            )
            for i in range(2)
        ]

    total_steps = n_wide + n_deep
    ahead = 3
    for s in range(ahead):
        for copy in copies(s):
            copy.start()
    fill_stage(stage, x_ref)
    for j in range(ROW):
        rows[:, j * CELL : (j + 1) * CELL] = take_cells(stage, j, count)
    for s in range(total_steps):
        if s + ahead < total_steps:
            for copy in copies(s + ahead):
                copy.start()
        for copy in copies(s):
            copy.wait()
        if s < n_wide:
            gated = dot(rows[...], wide[s, 0])
            raised = dot(rows[...], wide[s, 1])
            hidden[:, s * wide_step : (s + 1) * wide_step] = (
                gated / (1.0 + jnp.exp(-gated)) * raised
            ).astype(BF16)
        else:
            d = s - n_wide
            for c in range(deep_step // CELL):
                part = dot(hidden[...], deep[d, :, c * CELL : (c + 1) * CELL])
                put_cells(stage, d * (deep_step // CELL) + c, part)
    drain_stage(stage, out_ref)


def combine_kernel(base_ref, weight_ref, rows_ref, out_ref, stage):
    share = base_ref.shape[0]
    count = weight_ref.shape[1]
    fill_stage(stage, rows_ref)
    for j in range(ROW):
        columns = slice(j * CELL, (j + 1) * CELL)
        part = dot(weight_ref[...], take_cells(stage, j, count))
        out_ref[:, columns] = (base_ref[:, columns] + part[:share] + part[share:]).astype(
            out_ref.dtype
        )


def whole(shape):
    return pl.BlockSpec(shape, lambda s, *_: (0,) * len(shape))


def params(mib=60):
    return pltpu.CompilerParams(
        dimension_semantics=("arbitrary",), vmem_limit_bytes=mib * MIB
    )


def body(
    ssd_input,
    dt_raw,
    dt_bias,
    log_decay,
    input_map,
    output_map,
    head_group,
    d_skip,
    norm_gain,
    w_out,
    residual,
    moe_gain,
    w_router,
    expert_ids,
    w_gate,
    w_up,
    w_down,
):
    length = ssd_input.shape[0]
    heads = dt_raw.shape[1]
    width = w_out.shape[1]
    share = residual.shape[0]
    me = lax.axis_index("exp")
    ring = lax.axis_size("exp")
    seq_count = lax.axis_size("seq")
    nxt = [(i, (i + 1) % ring) for i in range(ring)]
    prv = [(i, (i - 1) % ring) for i in range(ring)]
    partner = [(i, i ^ 1) for i in range(seq_count)]
    steps = heads // (2 * STEP_PAIRS)
    columns = STEP_PAIRS * PAIR

    opposite = [(i, (i + 2) % ring) for i in range(ring)]

    def gather_maps(own):
        far = lax.ppermute(own, "exp", opposite)
        return own, lax.ppermute(own, "exp", prv), far, lax.ppermute(own, "exp", nxt)

    in_maps = gather_maps(input_map.transpose(1, 2, 0))
    out_maps = gather_maps(output_map.transpose(1, 0, 2))
    slot = (lax.rem(head_group // 2 - me + ring, ring) * 2 + head_group % 2).astype(jnp.int32)

    prep = pl.pallas_call(
        prep_kernel,
        out_shape=jax.ShapeDtypeStruct((4, heads, length), F32),
        compiler_params=pltpu.CompilerParams(vmem_limit_bytes=16 * MIB),
        cost_estimate=pl.CostEstimate(
            flops=30_000_000, bytes_accessed=400_000, transcendentals=100_000
        ),
        name="prep",
    )(dt_raw.T, dt_bias[:, None], log_decay.T)
    skip_lanes = jnp.repeat(d_skip, P_SIZE)[None, :]
    gain_lanes = norm_gain[None, :]

    x_spec = pl.BlockSpec((length, columns), lambda s, *_: (0, s))
    prep_spec = pl.BlockSpec((4, 2 * STEP_PAIRS, length), lambda s, *_: (0, s, 0))
    lane_spec = pl.BlockSpec((1, columns), lambda s, *_: (0, s))
    state_spec = pl.BlockSpec((STEP_PAIRS, NST, PAIR), lambda s, *_: (s, 0, 0))
    in_specs = [whole((2, NST, length))] * 4
    out_specs = [whole((2, length, NST))] * 4

    fresh, sending = pl.pallas_call(
        states_kernel,
        grid_spec=pltpu.PrefetchScalarGridSpec(
            num_scalar_prefetch=1,
            grid=(steps,),
            in_specs=[x_spec, prep_spec] + in_specs,
            out_specs=[pl.BlockSpec(memory_space=pltpu.HBM)] * 2,
            scratch_shapes=[
                pltpu.VMEM((G, NST, length), BF16),
                pltpu.VMEM((heads // 2, NST, PAIR), BF16),
                pltpu.VMEM((heads, 72, PAIR), BF16),
                pltpu.SemaphoreType.DMA((steps,)),
                pltpu.SemaphoreType.DMA((steps,)),
            ],
        ),
        out_shape=[
            jax.ShapeDtypeStruct((heads // 2, NST, PAIR), BF16),
            jax.ShapeDtypeStruct((heads, 72, PAIR), BF16),
        ],
        compiler_params=params(16),
        cost_estimate=pl.CostEstimate(
            flops=600_000_000, bytes_accessed=5_000_000, transcendentals=0
        ),
        name="states",
    )(slot, ssd_input, prep, *in_maps)

    sending, own_gate = lax.optimization_barrier((sending, w_gate[0]))
    other_gate = lax.ppermute(own_gate, "seq", partner)
    other_up = lax.ppermute(w_up[0], "seq", partner)
    other_down = lax.ppermute(w_down[0], "seq", partner)

    arrived = lax.all_to_all(sending, "seq", split_axis=0, concat_axis=0, tiled=True)
    prefix = pl.pallas_call(
        scan_kernel,
        out_shape=jax.ShapeDtypeStruct((seq_count, 64, PAIR), BF16),
        compiler_params=pltpu.CompilerParams(vmem_limit_bytes=16 * MIB),
        name="scan",
    )(arrived)
    entering = lax.all_to_all(prefix, "seq", split_axis=0, concat_axis=0, tiled=True)
    entering = entering.reshape(heads // 2, NST, PAIR)

    within = pl.pallas_call(
        within_kernel,
        grid_spec=pltpu.PrefetchScalarGridSpec(
            num_scalar_prefetch=1,
            grid=(steps,),
            in_specs=[x_spec, prep_spec, lane_spec] + in_specs + out_specs,
            out_specs=x_spec,
            scratch_shapes=[pltpu.VMEM((G, 2, BLOCK, BLOCK), F32)],
        ),
        out_shape=jax.ShapeDtypeStruct(ssd_input.shape, BF16),
        compiler_params=params(),
        cost_estimate=pl.CostEstimate(
            flops=12_000_000_000, bytes_accessed=8_000_000, transcendentals=4_000_000
        ),
        name="within",
    )(slot, ssd_input, prep, skip_lanes, *in_maps, *out_maps)

    vmem = pl.BlockSpec(memory_space=pltpu.VMEM)
    hbm = pl.BlockSpec(memory_space=pl.ANY)
    within, other_gate = lax.optimization_barrier((within, other_gate))
    own, up, far, down = pl.pallas_call(
        project_kernel,
        grid_spec=pltpu.PrefetchScalarGridSpec(
            num_scalar_prefetch=2,
            grid=(steps,),
            in_specs=[x_spec, prep_spec, lane_spec, state_spec, state_spec]
            + out_specs
            + [pl.BlockSpec((columns, width), lambda s, *_: (s, 0))],
            out_specs=[whole((share, width))] * 4,
            scratch_shapes=[
                pltpu.VMEM((G, length, NST), BF16),
                pltpu.VMEM((length, columns), BF16),
                pltpu.VMEM((length, width), F32),
            ],
        ),
        out_shape=[jax.ShapeDtypeStruct((share, width), BF16)] * 4,
        compiler_params=params(),
        cost_estimate=pl.CostEstimate(
            flops=6_000_000_000, bytes_accessed=16_000_000, transcendentals=0
        ),
        name="project",
    )(slot, me[None].astype(jnp.int32), within, prep, gain_lanes, entering, fresh, *out_maps, w_out)

    from_prev = lax.ppermute(up, "exp", nxt)
    from_next = lax.ppermute(down, "exp", prv)
    from_far = lax.ppermute(far, "exp", opposite)

    experts = w_router.shape[1]
    per_group = experts // ring
    router = w_router.reshape(-1, ring, per_group).swapaxes(1, 2).reshape(-1, experts)
    chunk = SLOTS // CHUNKS
    count = experts * chunk
    cells = (count * ROW, CELL)
    stage = (2, count * ROW, CELL // 2)
    stream, weights, *outgoing = pl.pallas_call(
        functools.partial(tokens_kernel, ring=ring),
        out_shape=[
            jax.ShapeDtypeStruct((share, width), F32),
            jax.ShapeDtypeStruct((CHUNKS, 2 * share, count), BF16),
        ]
        + [jax.ShapeDtypeStruct(cells, BF16)] * CHUNKS,
        scratch_shapes=[pltpu.VMEM(stage, F32), pltpu.VMEM((share, width), BF16)],
        compiler_params=pltpu.CompilerParams(vmem_limit_bytes=32 * MIB),
        cost_estimate=pl.CostEstimate(
            flops=1_000_000_000, bytes_accessed=8_000_000, transcendentals=0
        ),
        name="tokens",
    )(residual, own, from_prev, from_next, from_far, moe_gain[None, :], router, expert_ids)

    cores = [
        [(c // ring * 2 + h) * ring + c % ring for c in range(experts)] for h in range(2)
    ]

    def swap(rows):
        swapped = lax.all_to_all(
            rows.reshape(count, ROW, CELL),
            ("seq", "exp"),
            split_axis=0,
            concat_axis=0,
            tiled=True,
            axis_index_groups=cores,
        )
        return swapped.reshape(cells)

    unit = w_gate.shape[2]
    run_experts = pl.pallas_call(
        experts_kernel,
        in_specs=[vmem] + [hbm] * 6,
        out_specs=vmem,
        out_shape=jax.ShapeDtypeStruct(cells, BF16),
        scratch_shapes=[
            pltpu.VMEM(stage, F32),
            pltpu.VMEM((count, width), BF16),
            pltpu.VMEM((count, 2 * unit), BF16),
            pltpu.VMEM((8, 2, width, unit // 4), BF16),
            pltpu.VMEM((4, 2 * unit, width // 4), BF16),
            pltpu.SemaphoreType.DMA((8, 2)),
            pltpu.SemaphoreType.DMA((4, 2)),
        ],
        compiler_params=pltpu.CompilerParams(vmem_limit_bytes=60 * MIB),
        cost_estimate=pl.CostEstimate(
            flops=12 * count * width * unit,
            bytes_accessed=28_000_000,
            transcendentals=0,
        ),
        name="experts",
    )

    def combine(base, weight, rows, dtype):
        return pl.pallas_call(
            combine_kernel,
            out_shape=jax.ShapeDtypeStruct((share, width), dtype),
            scratch_shapes=[pltpu.VMEM(stage, F32)],
            compiler_params=pltpu.CompilerParams(vmem_limit_bytes=24 * MIB),
            cost_estimate=pl.CostEstimate(
                flops=500_000_000, bytes_accessed=4_000_000, transcendentals=0
            ),
            name="combine",
        )(base, weight, rows)

    arrivals = [swap(rows) for rows in outgoing]
    returned = [
        swap(
            run_experts(
                rows, w_gate[0], w_up[0], w_down[0], other_gate, other_up, other_down
            )
        )
        for rows in arrivals
    ]
    mixed = stream
    for i in range(CHUNKS):
        mixed = combine(mixed, weights[i], returned[i], BF16 if i == CHUNKS - 1 else F32)
    return mixed


def solution(mesh):
    return jax.shard_map(
        body,
        mesh=mesh,
        in_specs=(
            P("seq", "exp"),
            P("seq", "exp"),
            P("exp"),
            P("seq", "exp"),
            P("seq", "exp", None),
            P("seq", "exp", None),
            P("exp"),
            P("exp"),
            P("exp"),
            P("exp", None),
            P(("seq", "exp"), None),
            P(),
            P(),
            P(("seq", "exp"), None),
            P(("seq", "exp"), None, None),
            P(("seq", "exp"), None, None),
            P(("seq", "exp"), None, None),
        ),
        out_specs=P(("seq", "exp"), None),
        check_vma=False,
    )
```
